32 devices in a mesh: dp: 4 (over x, core), seq: 8 (over z, y).
Axes of the slice: x: 2, y: 2, z: 4, core: 2. Of those that a mesh axis runs over, the one named last changes fastest.
Arguments:
- inputs: bfloat16 [8, 4096, 512], P('dp', 'seq'), may hold values from -6 to 6
- segment_ids: int32 [8, 4096], P('dp', 'seq'), may hold values from 0 to 4095, as said below
- real_block: int32 [8, 128], P('dp', 'seq'), may hold values from 0 to 1, as said below
- gain_attn: bfloat16 [512], replicated, may hold values from 0.25 to 1.75
- w_query: bfloat16 [512, 512], replicated, may hold values from -0.25 to 0.25
- w_key: bfloat16 [512, 512], replicated, may hold values from -0.25 to 0.25
- w_value: bfloat16 [512, 512], replicated, may hold values from -0.25 to 0.25
- w_output: bfloat16 [512, 512], replicated, may hold values from -2 to 2
- w_sort: bfloat16 [512, 512], replicated, may hold values from -0.25 to 0.25
- gain_ffn: bfloat16 [512], replicated, may hold values from 0.25 to 1.75
- w_in: bfloat16 [512, 2048], replicated, may hold values from -0.25 to 0.25
- w_out: bfloat16 [2048, 512], replicated, may hold values from -0.125 to 0.125
- cotangent: bfloat16 [8, 4096, 512], P('dp', 'seq'), may hold values from -6 to 6
Outputs:
- output: bfloat16 [8, 4096, 512], P('dp', 'seq')
- input_grad: bfloat16 [8, 4096, 512], P('dp', 'seq')
- penalty: float32 [], replicated
- grad_gain_attn: float32 [512], replicated
- grad_query: float32 [512, 512], replicated
- grad_key: float32 [512, 512], replicated
- grad_value: float32 [512, 512], replicated
- grad_output: float32 [512, 512], replicated
- grad_sort: float32 [512, 512], replicated
- slope_feedforward_scaler: float32 [512], replicated
- grad_in: float32 [512, 2048], replicated
- grad_out: float32 [2048, 512], replicated
The draws below stay inside these ranges and needn't reach their ends.
Inputs may be any that keep to these rules, and one draw needn't show every extreme that they name: `segment_ids`: Non-decreasing along each sequence; the ids of the pack that begins at position p * 256 lie in p * 256 to p * 256 + 255, so ids of different packs differ; the last position of every sequence holds the top id of its pack. `real_block`: the last block of every sequence is 1.
All inputs are finite; a program needn't handle non-finite values.
Results may differ from the reference program's by a relative error of at most 0.035.
Values may be sent and summed in bfloat16 or wider, within the bound.
No kernel may reach another device: no remote copies, remote signals or barrier semaphores. Data moves between devices by JAX's collectives and lax.ppermute only.
A program may use at most 384 MiB of HBM per device.

```python
import math
import jax
import jax.numpy as jnp
from jax import lax

D = 512
HEADS = 8
FF = 2048
BLOCK = 32
ITERS = 8
PACK = 256
SEQS = 8
LEN = 4096
NBLK = 128


def draw_segment_ids(key, part):
    key = jax.random.fold_in(key, 11)
    position = jnp.arange(LEN, dtype=jnp.int32)
    breaks = (jax.random.randint(key, (SEQS, LEN), 0, 24) == 0).astype(jnp.int32)
    running = jnp.cumsum(breaks, axis=1).astype(jnp.int32)
    pack_start = (position - position % PACK).astype(jnp.int32)
    at_start = jnp.take(running, pack_start, axis=1)
    local_ids = running - at_start
    ids = (position // PACK * PACK)[None, :] + local_ids
    top_id = (LEN - 1) // PACK * PACK + PACK - 1
    ids = jnp.where((position == LEN - 1)[None, :], top_id, ids)
    return ids.astype(jnp.int32)


def draw_real_block(key, part):
    key = jax.random.fold_in(key, 12)
    index = jnp.arange(NBLK, dtype=jnp.int32)
    sequence = jnp.arange(SEQS, dtype=jnp.int32)
    spread_seq = max(SEQS - 1, 1)
    ticket = jax.random.randint(key, (SEQS, NBLK), 0, 4 * NBLK)
    level = (NBLK + 3 * index[None, :]) * (spread_seq + 2 * sequence[:, None]) // (3 * spread_seq)
    chosen = jnp.logical_or(ticket < level, index[None, :] == NBLK - 1)
    return chosen.astype(jnp.int32)


def steps_of(key, dims, cuts, least, largest):
    factor_of = 1.0
    for dim, parts in cuts:
        heights = jax.random.uniform(jax.random.fold_in(jax.random.fold_in(key, 6), dim), (parts,), jnp.float32, least / len(cuts), largest / len(cuts))
        factor_of = factor_of * jnp.repeat(jnp.exp(heights), dims[dim] // parts).reshape((-1,) + (1,) * (len(dims) - 1 - dim))
    return factor_of


def scatter_about(key, dims, deviation, most, pieces=(), held_as=jnp.bfloat16):
    values = jax.random.normal(key, dims, jnp.float32) * deviation
    if len(pieces) > 0:
        values = steps_of(key, dims, pieces, -0.22, 0.18) * values
    return jnp.clip(values, min=-most, max=most).astype(held_as)


def setup_inputs(seed: int = 0) -> dict:
    seeds = jax.random.split(jax.random.key(seed), 14)
    return {
        "inputs": scatter_about(seeds[0], (SEQS, LEN, D), 1.0, 6.0, ((0, 4), (1, 8))),
        "segment_ids": draw_segment_ids(jax.random.fold_in(seeds[13], 71), 0),
        "real_block": draw_real_block(jax.random.fold_in(seeds[13], 71), 0),
        "gain_attn": jnp.clip(1.0 + 0.15 * jax.random.normal(seeds[3], (D,), jnp.float32), 0.25, 1.75).astype(jnp.bfloat16),
        "w_query": scatter_about(seeds[4], (D, D), D ** -0.5, 0.25),
        "w_key": scatter_about(seeds[5], (D, D), D ** -0.5, 0.25),
        "w_value": scatter_about(seeds[6], (D, D), D ** -0.5, 0.25),
        "w_output": scatter_about(seeds[7], (D, D), (D // (2 * BLOCK)) ** -0.5, 2.0),
        "w_sort": scatter_about(seeds[8], (D, D), D ** -0.5, 0.25),
        "gain_ffn": jnp.clip(1.0 + 0.15 * jax.random.normal(seeds[9], (D,), jnp.float32), 0.25, 1.75).astype(jnp.bfloat16),
        "w_in": scatter_about(seeds[10], (D, FF), D ** -0.5, 0.25),
        "w_out": scatter_about(seeds[11], (FF, D), FF ** -0.5, 0.125),
        "cotangent": scatter_about(seeds[12], (SEQS, LEN, D), 1.0, 6.0, ((0, 4), (1, 8))),
    }


EPS = 1e-06
NEG = -1000000000.0
SORT_GAIN = 2.5
HIGH = lax.Precision.HIGHEST

@jax.custom_vjp
def low(v):
    return lax.optimization_barrier(v.astype(jnp.bfloat16)).astype(jnp.float32)

@jax.custom_vjp
def low_back(v):
    return v

def low_keep(v):
    return (low(v), None)

def low_pass(kept, grad):
    return (grad,)

def back_keep(v):
    return (v, None)

def back_low(kept, grad):
    return (low(grad),)
low.defvjp(low_keep, low_pass)
low_back.defvjp(back_keep, back_low)

def rms_norm(payload_vector_entries, gain_vec):
    return payload_vector_entries * lax.rsqrt(lax.optimization_barrier(jnp.mean(payload_vector_entries * payload_vector_entries, axis=-1, keepdims=True)) + EPS) * gain_vec

def matmul(lhs_mat, rhs_mat):
    return jnp.matmul(lhs_mat, rhs_mat, precision=HIGH)

def doubly_stochastic_normalizer(permutation_raw_scores, retained_target_slots):
    keep_mask = retained_target_slots[:, None, :]
    logarithmic_coupling_matrix = jnp.where(keep_mask, permutation_raw_scores, NEG)
    for sweep_index in range(ITERS):
        logarithmic_coupling_matrix = logarithmic_coupling_matrix - jax.nn.logsumexp(logarithmic_coupling_matrix, axis=2, keepdims=True)
        logarithmic_coupling_matrix = logarithmic_coupling_matrix - jnp.where(keep_mask, jax.nn.logsumexp(logarithmic_coupling_matrix, axis=1, keepdims=True), 0.0)
    return logarithmic_coupling_matrix

def forward(inputs_f, gain_attn, w_query, w_key, w_value, w_output, w_sort, gain_ffn, w_in, w_out, segment_ids, real_block, block_grand_total):
    seq_count = inputs_f.shape[0]
    head_dim = D // HEADS
    hidden = low(rms_norm(inputs_f, gain_attn))
    blocks = hidden.reshape(seq_count, NBLK, BLOCK, D)
    summary = low(lax.optimization_barrier(jnp.mean(blocks, axis=2)))
    sort_proj = low(low_back(matmul(summary, w_sort)))
    sort_scale = SORT_GAIN * BLOCK / math.sqrt(D)
    permutation_raw_scores = low_back(sort_scale * jnp.einsum('sid,sjd->sij', sort_proj, summary, precision=HIGH))
    retained_target_slots = real_block == 1
    logarithmic_coupling_matrix = doubly_stochastic_normalizer(permutation_raw_scores, retained_target_slots)
    prob_full = jnp.exp(logarithmic_coupling_matrix)
    penalty = -jnp.sum(jnp.where(retained_target_slots[:, :, None], prob_full * logarithmic_coupling_matrix, 0.0)) / block_grand_total
    prob_low = low(prob_full)
    mixed = low(low_back(jnp.einsum('sij,sjtd->sitd', prob_low, blocks, precision=HIGH)))
    shape_heads = (seq_count, NBLK, BLOCK, HEADS, head_dim)
    queries = low(low_back(matmul(hidden, w_query))).reshape(shape_heads)
    key_local = low(low_back(matmul(hidden, w_key))).reshape(shape_heads)
    value_local = low(low_back(matmul(hidden, w_value))).reshape(shape_heads)
    key_sorted = low(low_back(matmul(mixed, w_key))).reshape(shape_heads)
    value_sorted = low(low_back(matmul(mixed, w_value))).reshape(shape_heads)
    key_all = jnp.concatenate([key_local, key_sorted], axis=2)
    value_all = jnp.concatenate([value_local, value_sorted], axis=2)
    att_scale = 1.0 / math.sqrt(head_dim)
    scores = low_back(jnp.einsum('snthd,snkhd->snhtk', queries, key_all, precision=HIGH) * att_scale)
    segments = segment_ids.reshape(seq_count, NBLK, BLOCK)
    same_seg = segments[:, :, :, None] == segments[:, :, None, :]
    allowed = jnp.concatenate([same_seg, jnp.ones_like(same_seg)], axis=-1)[:, :, None]
    scores = jnp.where(allowed, scores, NEG)
    peak_score = lax.optimization_barrier(jnp.max(scores, axis=-1, keepdims=True))
    exponent = jnp.exp(scores - peak_score)
    weights = low(exponent / lax.optimization_barrier(jnp.sum(exponent, axis=-1, keepdims=True)))
    attended = low(low_back(jnp.einsum('snhtk,snkhd->snthd', weights, value_all, precision=HIGH)))
    attended = attended.reshape(seq_count, LEN, D)
    residual = inputs_f + low_back(matmul(attended, w_output))
    hidden_two = low(rms_norm(residual, gain_ffn))
    pre_act = low_back(matmul(hidden_two, w_in))
    activation = low(jax.nn.gelu(pre_act))
    return (residual + matmul(activation, w_out), penalty)

def reference(inputs, segment_ids, real_block, gain_attn, w_query, w_key, w_value, w_output, w_sort, gain_ffn, w_in, w_out, cotangent):
    block_grand_total = jnp.sum(real_block).astype(jnp.float32)
    params = tuple((array_in.astype(jnp.float32) for array_in in (inputs, gain_attn, w_query, w_key, w_value, w_output, w_sort, gain_ffn, w_in, w_out)))

    def objective(*weights_in):
        return forward(*weights_in, segment_ids, real_block, block_grand_total)
    (output, penalty), pullback = jax.vjp(objective, *params)
    grads = pullback((cotangent.astype(jnp.float32), jnp.ones_like(penalty)))
    return (output.astype(jnp.bfloat16), grads[0].astype(jnp.bfloat16), penalty, grads[1], grads[2], grads[3], grads[4], grads[5], grads[6], grads[7], grads[8], grads[9])
```

```python
import math

import jax
import jax.numpy as jnp
from jax import lax
from jax.sharding import PartitionSpec as P

HEADS = 8
BLOCK = 32
ITERS = 8


EPS = 1e-06
NEG = -1000000000.0
SORT_GAIN = 2.5


def normalize(payload_vector_entries, gain_vec):
    inv_rms = lax.rsqrt(
        jnp.mean(payload_vector_entries * payload_vector_entries, axis=-1, keepdims=True) + EPS
    )
    unit_vals = payload_vector_entries * inv_rms
    return (unit_vals * gain_vec, unit_vals, inv_rms)


def norm_back(upstream, unit_vals, inv_rms, gain_vec):
    d_unit = upstream * gain_vec
    d_values = inv_rms * (d_unit - unit_vals * jnp.mean(d_unit * unit_vals, axis=-1, keepdims=True))
    return (d_values, jnp.sum(upstream * unit_vals, axis=(0, 1)))


def doubly_stochastic_normalizer(permutation_raw_scores, retained_target_slots):
    keep_mask = retained_target_slots[:, None, :]
    logarithmic_coupling_matrix = jnp.where(keep_mask, permutation_raw_scores, NEG)
    for sweep_index in range(ITERS):
        logarithmic_coupling_matrix = logarithmic_coupling_matrix - jax.nn.logsumexp(
            logarithmic_coupling_matrix, axis=2, keepdims=True
        )
        logarithmic_coupling_matrix = logarithmic_coupling_matrix - jnp.where(
            keep_mask, jax.nn.logsumexp(logarithmic_coupling_matrix, axis=1, keepdims=True), 0.0
        )
    return logarithmic_coupling_matrix


def product(left_mat, right_mat):
    return lax.dot_general(
        left_mat,
        right_mat,
        (((left_mat.ndim - 1,), (0,)), ((), ())),
        preferred_element_type=jnp.float32,
    )


def product_back(left_mat, right_mat):
    return lax.dot_general(
        left_mat,
        right_mat,
        (((left_mat.ndim - 1,), (1,)), ((), ())),
        preferred_element_type=jnp.float32,
    )


def weight_grad(left_mat, right_mat):
    flat_left = left_mat.reshape(-1, left_mat.shape[-1])
    flat_right = right_mat.reshape(-1, right_mat.shape[-1])
    return lax.dot_general(
        flat_left, flat_right, (((0,), (0,)), ((), ())), preferred_element_type=jnp.float32
    )


def attend_scores(queries, key_all, segments, att_scale):
    scores = (
        jnp.einsum("snthd,snkhd->snhtk", queries, key_all, preferred_element_type=jnp.float32)
        * att_scale
    )
    same_seg = segments[:, :, :, None] == segments[:, :, None, :]
    allowed = jnp.concatenate([same_seg, jnp.ones_like(same_seg)], axis=-1)[:, :, None]
    return jnp.where(allowed, scores, NEG)


def bits(size):
    return [1 << k for k in range(size.bit_length() - 1)]


def swap(array, axis, bit):
    return lax.ppermute(array, axis, [(i, i ^ bit) for i in range(lax.axis_size(axis))])


def reduce_all(rows, order):
    for axis, bit in order:
        halves = rows.reshape(2, rows.shape[0] // 2, rows.shape[1])
        mine = (lax.axis_index(axis) // bit) % 2
        keep = lax.dynamic_index_in_dim(halves, mine, 0, False)
        give = lax.dynamic_index_in_dim(halves, 1 - mine, 0, False)
        got = swap(give, axis, bit)
        rows = (keep.astype(jnp.float32) + got.astype(jnp.float32)).astype(jnp.bfloat16)
    for axis, bit in reversed(order):
        mine = (lax.axis_index(axis) // bit) % 2
        got = swap(rows, axis, bit)
        both = jnp.where(mine == 0, jnp.stack([rows, got]), jnp.stack([got, rows]))
        rows = both.reshape(2 * rows.shape[0], rows.shape[1])
    return rows


def sum_seq(part):
    parts = lax.axis_size("seq")
    if parts * part.size > 1 << 20:
        return lax.psum(part.astype(jnp.float32), "seq")
    heard = lax.all_to_all(
        jnp.broadcast_to(part[None], (parts,) + part.shape), "seq", 0, 0, tiled=True
    )
    return jnp.sum(heard.astype(jnp.float32), axis=0)


def to_chunks(blocks, parts):
    seqs, count, rows, width = blocks.shape
    row_parts = min(parts, rows)
    col_parts = parts // row_parts
    cut = blocks.reshape(
        seqs, count, row_parts, rows // row_parts, col_parts, width // col_parts
    ).transpose(2, 4, 0, 3, 1, 5)
    return cut.reshape(parts, seqs, rows // row_parts, count, width // col_parts)


def from_chunks(chunks):
    parts, seqs, rows, count, width = chunks.shape
    row_parts = min(parts, BLOCK)
    col_parts = parts // row_parts
    cut = chunks.reshape(row_parts, col_parts, seqs, rows, count, width).transpose(2, 4, 0, 3, 1, 5)
    return cut.reshape(seqs, count, row_parts * rows, col_parts * width)


def gathered(chunks):
    parts, seqs, rows, count, width = chunks.shape
    return chunks.transpose(1, 2, 0, 3, 4).reshape(seqs, rows, parts * count, width)


def scattered(spread, parts):
    seqs, rows, count, width = spread.shape
    return spread.reshape(seqs, rows, parts, count // parts, width).transpose(2, 0, 1, 3, 4)


def body(
    inputs,
    segment_ids,
    real_block,
    gain_attn,
    w_query,
    w_key,
    w_value,
    w_output,
    w_sort,
    gain_ffn,
    w_in,
    w_out,
    cotangent,
):
    seq_count, span_len, model_width = inputs.shape
    local_blocks = span_len // BLOCK
    head_dim = model_width // HEADS
    flat_width = BLOCK * model_width
    att_scale = 1.0 / math.sqrt(head_dim)
    sort_scale = SORT_GAIN * BLOCK / math.sqrt(model_width)
    seq_size = lax.axis_size("seq")
    seq_index = lax.axis_index("seq")
    first_block = seq_index * local_blocks
    inputs_f = inputs.astype(jnp.float32)
    gain_one = gain_attn.astype(jnp.float32)
    gain_two = gain_ffn.astype(jnp.float32)
    normed, leading_identity_scalar, scale_one = normalize(inputs_f, gain_one)
    hidden = normed.astype(jnp.bfloat16)
    blocks = hidden.reshape(seq_count, local_blocks, BLOCK, model_width)
    blocks_flat = blocks.reshape(seq_count, local_blocks, flat_width)
    summary = jnp.mean(blocks, axis=2, dtype=jnp.float32).astype(jnp.bfloat16)
    flag_rows = jnp.broadcast_to(
        real_block.astype(jnp.bfloat16)[:, :, None], (seq_count, local_blocks, 128)
    )
    told = jnp.concatenate([summary, flag_rows], axis=-1)
    told_all = lax.all_to_all(
        jnp.broadcast_to(told[None], (seq_size,) + told.shape), "seq", 0, 0, tiled=True
    )
    told_all = told_all.transpose(1, 0, 2, 3).reshape(seq_count, seq_size * local_blocks, -1)
    summary_all = told_all[:, :, :model_width]
    real_all = told_all[:, :, model_width]
    retained_target_slots = real_all == 1
    block_grand_total = jnp.sum(real_all.astype(jnp.float32)).reshape(1, 1)
    for bit in bits(lax.axis_size("dp")):
        block_grand_total = block_grand_total + swap(block_grand_total, "dp", bit)
    block_grand_total = block_grand_total[0, 0]
    spread = lax.all_to_all(to_chunks(blocks, seq_size), "seq", 0, 0, tiled=True)
    spread = gathered(spread)
    sort_proj = product(summary_all, w_sort).astype(jnp.bfloat16)
    permutation_raw_scores = sort_scale * jnp.einsum(
        "sid,sjd->sij", sort_proj, summary_all, preferred_element_type=jnp.float32
    )

    def plan_of(payload_vector_entries):
        return doubly_stochastic_normalizer(payload_vector_entries, retained_target_slots)

    logarithmic_coupling_matrix, plan_back = jax.vjp(plan_of, permutation_raw_scores)
    prob_full = jnp.exp(logarithmic_coupling_matrix)
    plan_rows = lax.dynamic_slice_in_dim(logarithmic_coupling_matrix, first_block, local_blocks, 1)
    entropy_mine = jnp.sum(
        jnp.where((real_block == 1)[:, :, None], jnp.exp(plan_rows) * plan_rows, 0.0)
    )
    prob_low = prob_full.astype(jnp.bfloat16)
    mixed_spread = jnp.einsum(
        "sim,stmf->stif", prob_low, spread, preferred_element_type=jnp.float32
    ).astype(jnp.bfloat16)
    mixed = from_chunks(
        lax.all_to_all(scattered(mixed_spread, seq_size), "seq", 0, 0, tiled=True)
    )
    shape_heads = (seq_count, local_blocks, BLOCK, HEADS, head_dim)
    queries = product(hidden, w_query).astype(jnp.bfloat16).reshape(shape_heads)
    key_local = product(hidden, w_key).astype(jnp.bfloat16).reshape(shape_heads)
    value_local = product(hidden, w_value).astype(jnp.bfloat16).reshape(shape_heads)
    key_sorted = product(mixed, w_key).astype(jnp.bfloat16).reshape(shape_heads)
    value_sorted = product(mixed, w_value).astype(jnp.bfloat16).reshape(shape_heads)
    key_all = jnp.concatenate([key_local, key_sorted], axis=2)
    value_all = jnp.concatenate([value_local, value_sorted], axis=2)
    segments = segment_ids.reshape(seq_count, local_blocks, BLOCK)
    scores = attend_scores(queries, key_all, segments, att_scale)
    peak_score = jnp.max(scores, axis=-1, keepdims=True)
    exponent = jnp.exp(scores - peak_score)
    denominator = jnp.sum(exponent, axis=-1, keepdims=True)
    log_total = peak_score + jnp.log(denominator)
    weights_low = (exponent / denominator).astype(jnp.bfloat16)
    attended = jnp.einsum(
        "snhtk,snkhd->snthd", weights_low, value_all, preferred_element_type=jnp.float32
    )
    attended = attended.astype(jnp.bfloat16).reshape(seq_count, span_len, model_width)
    residual = inputs_f + product(attended, w_output)
    normed_two, unit_two, scale_two = normalize(residual, gain_two)
    hidden_two = normed_two.astype(jnp.bfloat16)
    pre_act = product(hidden_two, w_in)
    activation, gelu_back = jax.vjp(jax.nn.gelu, pre_act)
    activation_low = activation.astype(jnp.bfloat16)
    output = (residual + product(activation_low, w_out)).astype(jnp.bfloat16)
    grad_out = weight_grad(activation_low, cotangent)
    (d_pre,) = gelu_back(product_back(cotangent, w_out))
    d_pre_low = d_pre.astype(jnp.bfloat16)
    grad_in = jnp.concatenate(
        [
            weight_grad(hidden_two, d_pre_low[..., c : c + model_width])
            for c in range(0, d_pre_low.shape[-1], model_width)
        ],
        axis=0,
    )
    d_resid, grad_gain_two = norm_back(product_back(d_pre_low, w_in), unit_two, scale_two, gain_two)
    d_resid = d_resid + cotangent.astype(jnp.float32)
    d_branch = d_resid.astype(jnp.bfloat16)
    grad_output = weight_grad(attended, d_branch)
    d_att = product_back(d_branch, w_output).astype(jnp.bfloat16).reshape(shape_heads)
    weights_full = jnp.exp(attend_scores(queries, key_all, segments, att_scale) - log_total)
    d_weights = jnp.einsum(
        "snthd,snkhd->snhtk", d_att, value_all, preferred_element_type=jnp.float32
    )
    d_scores = weights_full * (
        d_weights - jnp.sum(weights_full * d_weights, axis=-1, keepdims=True)
    )
    d_scores = d_scores.astype(jnp.bfloat16)
    d_query = (
        att_scale
        * jnp.einsum("snhtk,snkhd->snthd", d_scores, key_all, preferred_element_type=jnp.float32)
    ).astype(jnp.bfloat16)
    cotangent_lookup_vectors = (
        att_scale
        * jnp.einsum("snhtk,snthd->snkhd", d_scores, queries, preferred_element_type=jnp.float32)
    ).astype(jnp.bfloat16)
    d_vals = jnp.einsum(
        "snhtk,snthd->snkhd", weights_low, d_att, preferred_element_type=jnp.float32
    ).astype(jnp.bfloat16)
    d_query = d_query.reshape(seq_count, span_len, model_width)
    d_key_local = cotangent_lookup_vectors[:, :, :BLOCK].reshape(seq_count, span_len, model_width)
    d_key_sorted = cotangent_lookup_vectors[:, :, BLOCK:].reshape(
        seq_count, local_blocks, BLOCK, model_width
    )
    d_value_local = d_vals[:, :, :BLOCK].reshape(seq_count, span_len, model_width)
    d_value_sorted = d_vals[:, :, BLOCK:].reshape(seq_count, local_blocks, BLOCK, model_width)
    grad_query = weight_grad(hidden, d_query)
    grad_key = weight_grad(hidden, d_key_local) + weight_grad(mixed, d_key_sorted)
    grad_value = weight_grad(hidden, d_value_local) + weight_grad(mixed, d_value_sorted)
    d_hidden = (
        product_back(d_query, w_query)
        + product_back(d_key_local, w_key)
        + product_back(d_value_local, w_value)
    )
    mixed_gradient = (
        product_back(d_key_sorted, w_key) + product_back(d_value_sorted, w_value)
    ).astype(jnp.bfloat16)
    dmixed_spread = gathered(
        lax.all_to_all(to_chunks(mixed_gradient, seq_size), "seq", 0, 0, tiled=True)
    )
    d_prob = jnp.einsum(
        "stmf,stjf->smj", dmixed_spread, spread, preferred_element_type=jnp.float32
    ).astype(jnp.bfloat16)
    d_prob = sum_seq(d_prob)
    block_sum = jnp.einsum(
        "smj,stmf->stjf", prob_low, dmixed_spread, preferred_element_type=jnp.float32
    ).astype(jnp.bfloat16)
    block_sum = from_chunks(
        lax.all_to_all(scattered(block_sum, seq_size), "seq", 0, 0, tiled=True)
    ).astype(jnp.float32)
    entropy_grad = jnp.where(
        retained_target_slots[:, :, None], prob_full * logarithmic_coupling_matrix + prob_full, 0.0
    )
    d_plan = prob_full * d_prob - entropy_grad / block_grand_total
    (d_logits,) = plan_back(d_plan)
    d_logits = d_logits.astype(jnp.bfloat16)
    rows_grad = lax.dynamic_slice_in_dim(d_logits, first_block, local_blocks, 1)
    cols_grad = lax.dynamic_slice_in_dim(d_logits, first_block, local_blocks, 2)
    d_proj = (
        sort_scale
        * jnp.einsum("sij,sjd->sid", rows_grad, summary_all, preferred_element_type=jnp.float32)
    ).astype(jnp.bfloat16)
    grad_sort = weight_grad(summary, d_proj)
    d_summary = sort_scale * jnp.einsum(
        "sij,sid->sjd", cols_grad, sort_proj, preferred_element_type=jnp.float32
    ) + product_back(d_proj, w_sort)
    d_hidden = (
        d_hidden.reshape(seq_count, local_blocks, BLOCK, model_width)
        + block_sum
        + d_summary[:, :, None, :] / BLOCK
    )
    d_input, grad_gain_one = norm_back(
        d_hidden.reshape(seq_count, span_len, model_width),
        leading_identity_scalar,
        scale_one,
        gain_one,
    )
    input_grad = (d_input + d_resid).astype(jnp.bfloat16)
    dp_size = lax.axis_size("dp")
    dp_bits, seq_bits = bits(dp_size), bits(seq_size)
    one = [("dp", bit) for bit in dp_bits] + [("seq", bit) for bit in seq_bits]
    two = one[:1] + [one[len(dp_bits)]] + one[1 : len(dp_bits)] + one[len(dp_bits) + 1 :]
    grad_out = reduce_all(grad_out.astype(jnp.bfloat16), one).astype(jnp.float32)
    grad_in = reduce_all(grad_in.astype(jnp.bfloat16), two)
    grad_in = jnp.concatenate(
        [grad_in[c : c + model_width] for c in range(0, grad_in.shape[0], model_width)], axis=1
    ).astype(jnp.float32)
    late = jnp.concatenate([grad_query, grad_key, grad_value, grad_output], axis=0)
    late = reduce_all(late.astype(jnp.bfloat16), one).astype(jnp.float32)
    grad_query, grad_key, grad_value, grad_output = jnp.split(late, 4, axis=0)
    grad_sort = reduce_all(grad_sort.astype(jnp.bfloat16), two).astype(jnp.float32)
    small = jnp.stack(
        [grad_gain_one, grad_gain_two, jnp.full_like(grad_gain_one, entropy_mine)]
        + [jnp.zeros_like(grad_gain_one)] * 5
    )
    small = lax.all_to_all(
        jnp.broadcast_to(small[None], (dp_size * seq_size,) + small.shape),
        ("dp", "seq"),
        0,
        0,
        tiled=True,
    )
    small = jnp.sum(small, axis=0)
    penalty = -small[2, 0] / block_grand_total
    return (
        output,
        input_grad,
        penalty,
        small[0],
        grad_query,
        grad_key,
        grad_value,
        grad_output,
        grad_sort,
        small[1],
        grad_in,
        grad_out,
    )


def solution(mesh):
    placed = (
        P("dp", "seq", None),
        P("dp", "seq"),
        P("dp", "seq"),
        P(),
        P(),
        P(),
        P(),
        P(),
        P(),
        P(),
        P(),
        P(),
        P("dp", "seq", None),
    )
    return jax.shard_map(
        body,
        mesh=mesh,
        in_specs=placed,
        out_specs=(
            P("dp", "seq", None),
            P("dp", "seq", None),
            P(),
            P(),
            P(),
            P(),
            P(),
            P(),
            P(),
            P(),
            P(),
            P(),
        ),
        check_vma=False,
    )
```

```python
import math

import jax
import jax.numpy as jnp
from jax import lax
from jax.experimental import pallas as pl
from jax.experimental.pallas import tpu as pltpu
from jax.sharding import PartitionSpec as P

HEADS = 8
BLOCK = 32
ITERS = 8
GROUP = 128

EPS = 1e-06
NEG = -1000000000.0
SORT_GAIN = 2.5
F32 = jnp.float32
BF16 = jnp.bfloat16
VMEM_BYTES = 56 * 2**20


def bits(size):
    return [1 << k for k in range(size.bit_length() - 1)]


def swap(array, axis, bit):
    return lax.ppermute(array, axis, [(i, i ^ bit) for i in range(lax.axis_size(axis))])


def reduce_all(rows, order):
    for axis, bit in order:
        halves = rows.reshape(2, rows.shape[0] // 2, rows.shape[1])
        mine = (lax.axis_index(axis) // bit) % 2
        keep = lax.dynamic_index_in_dim(halves, mine, 0, False)
        give = lax.dynamic_index_in_dim(halves, 1 - mine, 0, False)
        got = swap(give, axis, bit)
        rows = (keep.astype(F32) + got.astype(F32)).astype(BF16)
    for axis, bit in reversed(order):
        mine = (lax.axis_index(axis) // bit) % 2
        got = swap(rows, axis, bit)
        both = jnp.where(mine == 0, jnp.stack([rows, got]), jnp.stack([got, rows]))
        rows = both.reshape(2 * rows.shape[0], rows.shape[1])
    return rows


def exchange(chunks):
    return lax.all_to_all(chunks, "seq", 0, 0, tiled=True)


def tell_all(part):
    return exchange(jnp.broadcast_to(part[None], (lax.axis_size("seq"),) + part.shape))


def sum_seq(part):
    if lax.axis_size("seq") * part.size > 1 << 20:
        return lax.psum(part.astype(F32), "seq")[None]
    return tell_all(part)


def to_chunks(rows, parts):
    count, blocks, width = rows.shape
    row_parts = min(parts, count)
    col_parts = parts // row_parts
    cut = rows.reshape(
        row_parts, count // row_parts, blocks, col_parts, width // col_parts
    ).transpose(0, 3, 1, 2, 4)
    return cut.reshape(parts, count // row_parts, blocks, width // col_parts)


def from_chunks(chunks):
    parts, count, blocks, width = chunks.shape
    row_parts = min(parts, BLOCK)
    col_parts = parts // row_parts
    cut = chunks.reshape(row_parts, col_parts, count, blocks, width).transpose(0, 2, 3, 1, 4)
    return cut.reshape(row_parts * count, blocks, col_parts * width)


def dot(left, right, left_dim=1, right_dim=0):
    return lax.dot_general(
        left, right, (((left_dim,), (right_dim,)), ((), ())), preferred_element_type=F32
    )


def whole(array):
    return pl.BlockSpec(array.shape, lambda *_: (0,) * array.ndim)


def nth(array, index):
    return pl.BlockSpec((1,) + array.shape[1:], lambda *_: (index,) + (0,) * (array.ndim - 1))


def call(kernel, outs, args, specs=None, scratch=(), flops=0):
    specs = specs or [whole(a) for a in args]
    moved = sum(math.prod(o.shape) * o.dtype.itemsize for o in outs) + sum(
        math.prod(s.block_shape) * a.dtype.itemsize for s, a in zip(specs, args)
    )
    return pl.pallas_call(
        kernel,
        out_shape=outs,
        grid=(1,),
        in_specs=specs,
        out_specs=[whole(o) for o in outs],
        scratch_shapes=list(scratch),
        compiler_params=pltpu.CompilerParams(vmem_limit_bytes=VMEM_BYTES),
        cost_estimate=pl.CostEstimate(flops=flops, bytes_accessed=moved, transcendentals=0),
    )(*args)


def like(shape, dtype):
    return jax.ShapeDtypeStruct(shape, dtype)


def lay(buffer, value):
    for c in range(buffer.shape[0]):
        buffer[c] = value[:, c * 128 : (c + 1) * 128]


def lift(buffer):
    return jnp.concatenate([buffer[c] for c in range(buffer.shape[0])], axis=1)


def pick(buffer, t, count):
    return jnp.concatenate(
        [buffer[c, pl.ds(t, count, stride=BLOCK), :] for c in range(buffer.shape[0])], axis=1
    )


def strew(buffer, t, rows):
    for c in range(buffer.shape[0]):
        buffer[c, pl.ds(t, rows.shape[0], stride=BLOCK), :] = rows[:, c * 128 : (c + 1) * 128]


def row_buffer(span, width):
    return pltpu.VMEM((width // 128, span, 128), F32)


def enter_kernel(x_ref, gain_ref, hidden_ref, rows_ref, summary_ref, buffer):
    x = x_ref[0].astype(F32)
    scale = lax.rsqrt(jnp.mean(x * x, axis=-1, keepdims=True) + EPS)
    hidden = (x * scale * gain_ref[...]).astype(BF16)
    hidden_ref[...] = hidden
    lay(buffer, hidden.astype(F32))
    total = None
    for t in range(BLOCK):
        rows = pick(buffer, t, rows_ref.shape[1])
        rows_ref[t] = rows.astype(BF16)
        total = rows if total is None else total + rows
    summary_ref[...] = (total * (1.0 / BLOCK)).astype(BF16)


def enter(inputs, gain, index):
    _, span, width = inputs.shape
    blocks = span // BLOCK
    return call(
        enter_kernel,
        [
            like((span, width), BF16),
            like((BLOCK, blocks, width), BF16),
            like((blocks, width), BF16),
        ],
        [inputs, gain],
        [nth(inputs, index), whole(gain)],
        [row_buffer(span, width)],
    )


def plan_kernel(sort_scale, told_ref, w_ref, proj_ref, steps_ref, plan_ref, low_ref, entropy_ref):
    seqs = told_ref.shape[1]
    width = w_ref.shape[0]
    count = low_ref.shape[1]
    plans, reals = [], []
    entropy = jnp.zeros((), F32)
    for s in range(seqs):
        summary = told_ref[:, s, :, :width].reshape(count, width)
        flags = told_ref[:, s, :, width:].reshape(count, -1).astype(F32)
        real = flags[:, :128].T > 0.5
        proj = dot(summary, w_ref[...]).astype(BF16)
        proj_ref[s] = proj
        plans.append(jnp.where(real, sort_scale * dot(proj, summary, 1, 1), NEG))
        reals.append(real)
    for step in range(2 * ITERS):
        axis = 1 - step % 2
        for s in range(seqs):
            peak = jnp.max(plans[s], axis=axis, keepdims=True)
            share = jnp.exp(plans[s] - peak)
            total = jnp.sum(share, axis=axis, keepdims=True)
            fall = peak + jnp.log(total)
            share = share * (1.0 / total)
            if axis == 0:
                fall = jnp.where(reals[s][:1], fall, 0.0)
                share = jnp.where(reals[s], share, 0.0)
            plans[s] = plans[s] - fall
            steps_ref[step, s] = share
    for s in range(seqs):
        flags = told_ref[:, s, :, width:].reshape(count, -1).astype(F32)[:, :1]
        prob = jnp.exp(plans[s])
        plan_ref[s] = plans[s]
        low_ref[s] = prob.astype(BF16)
        entropy = entropy + jnp.sum(jnp.where(flags > 0.5, prob * plans[s], 0.0))
    entropy_ref[...] = jnp.full(entropy_ref.shape, entropy, F32)


def plan_back_kernel(
    sort_scale,
    count_ref,
    first_ref,
    heard_ref,
    told_ref,
    w_ref,
    proj_ref,
    steps_ref,
    plan_ref,
    d_summary_ref,
    grad_ref,
    buffer,
):
    seqs = told_ref.shape[1]
    blocks = told_ref.shape[2]
    width = w_ref.shape[0]
    count = plan_ref.shape[1]
    part = 1.0 / count_ref[0, 0]
    grads = []
    for s in range(seqs):
        flags = told_ref[:, s, :, width:].reshape(count, -1).astype(F32)[:, :1]
        plan = plan_ref[s]
        prob = jnp.exp(plan)
        d_prob = heard_ref[0, s].astype(F32)
        for k in range(1, heard_ref.shape[0]):
            d_prob = d_prob + heard_ref[k, s].astype(F32)
        grads.append(prob * d_prob - jnp.where(flags > 0.5, prob * plan + prob, 0.0) * part)
    for step in reversed(range(2 * ITERS)):
        for s in range(seqs):
            total = jnp.sum(grads[s], axis=1 - step % 2, keepdims=True)
            grads[s] = grads[s] - steps_ref[step, s] * total
    grad_sort = None
    for s in range(seqs):
        summary = told_ref[:, s, :, :width].reshape(count, width)
        flags = told_ref[:, s, :, width:].reshape(count, -1).astype(F32)
        real = flags[:, :128].T > 0.5
        d_logits = jnp.where(real, grads[s], 0.0)
        low = d_logits.astype(BF16)
        d_proj = (sort_scale * dot(low, summary)).astype(BF16)
        turned = low.astype(F32).T.astype(BF16)
        buffer[...] = sort_scale * dot(turned, proj_ref[s]) + dot(d_proj, w_ref[...], 1, 1)
        first = pl.multiple_of(first_ref[0, 0], blocks)
        d_summary_ref[s] = buffer[pl.ds(first, blocks), :]
        here = dot(summary, d_proj, 0, 0)
        grad_sort = here if grad_sort is None else grad_sort + here
    grad_ref[...] = grad_sort


def mix_kernel(plan_index, low_ref, spread_ref, mixed_ref):
    low = low_ref[0]
    parts, rows, blocks, width = spread_ref.shape
    for t in range(rows):
        mixed = dot(low, spread_ref[:, t].reshape(parts * blocks, width)).astype(BF16)
        mixed_ref[:, t] = mixed.reshape(parts, blocks, width)


def mix(low, spread, index):
    return call(
        lambda *refs: mix_kernel(index, *refs),
        [like(spread.shape, BF16)],
        [low, spread],
        [nth(low, index), whole(spread)],
    )[0]


def unmix_kernel(low_ref, spread_ref, d_mixed_ref, d_spread_ref, d_prob_ref):
    turned = low_ref[0].astype(F32).T.astype(BF16)
    parts, rows, blocks, width = spread_ref.shape
    d_prob = None
    for t in range(rows):
        grad = d_mixed_ref[:, t].reshape(parts * blocks, width)
        here = dot(grad, spread_ref[:, t].reshape(parts * blocks, width), 1, 1)
        d_prob = here if d_prob is None else d_prob + here
        back = dot(turned, grad).astype(BF16)
        d_spread_ref[:, t] = back.reshape(parts, blocks, width)
    d_prob_ref[...] = d_prob.astype(BF16)


def unmix(low, spread, d_mixed, index):
    return call(
        unmix_kernel,
        [like(spread.shape, BF16), like(low.shape[1:], BF16)],
        [low, spread, d_mixed],
        [nth(low, index), whole(spread), whole(d_mixed)],
    )


def block_masks():
    lane = lax.broadcasted_iota(jnp.int32, (BLOCK, 2 * GROUP), 1)
    owner = (lane % GROUP) // BLOCK
    return [owner == b for b in range(GROUP // BLOCK)]


def narrow(full, masks, start):
    out = full[start : start + BLOCK]
    for b in range(1, len(masks)):
        out = jnp.where(masks[b], full[start + b * BLOCK : start + (b + 1) * BLOCK], out)
    return out


def widen(first, second, masks):
    zero = jnp.zeros_like(first)
    return jnp.concatenate(
        [jnp.where(m, first, zero) for m in masks] + [jnp.where(m, second, zero) for m in masks],
        axis=0,
    ).astype(BF16)


def two_heads_lanes(rows):
    lane = lax.broadcasted_iota(jnp.int32, rows.shape, 1)
    low = lane < rows.shape[1] // 2
    zero = jnp.zeros_like(rows)
    return jnp.concatenate([jnp.where(low, rows, zero), jnp.where(low, zero, rows)], axis=0)


def two_heads_rows(columns):
    row = lax.broadcasted_iota(jnp.int32, columns.shape, 0)
    low = row < columns.shape[0] // 2
    zero = jnp.zeros_like(columns)
    return jnp.concatenate([jnp.where(low, columns, zero), jnp.where(low, zero, columns)], axis=1)


def own_heads(full):
    half = full.shape[1] // 2
    row = lax.broadcasted_iota(jnp.int32, (full.shape[0], half), 0)
    return jnp.where(row < full.shape[0] // 2, full[:, :half], full[:, half:])


def turn(array):
    return array.astype(F32).T.astype(BF16)


def attend_kernel(
    att_scale,
    hidden_ref,
    rows_ref,
    allowed_ref,
    wq_ref,
    wk_ref,
    wv_ref,
    att_ref,
    mixed_ref,
    q_ref,
    v_ref,
    vs_ref,
    kt_ref,
    kst_ref,
    weights_ref,
    buffer,
    qt,
    k,
    ks,
    vt,
    vst,
):
    span, width = hidden_ref.shape
    for t in range(BLOCK):
        strew(buffer, t, rows_ref[t].astype(F32))
    mixed_ref[...] = lift(buffer).astype(BF16)
    hidden = hidden_ref[...]
    mixed = mixed_ref[...]
    q_ref[...] = dot(hidden, wq_ref[...]).astype(BF16)
    k[...] = dot(hidden, wk_ref[...]).astype(BF16)
    v_ref[...] = dot(hidden, wv_ref[...]).astype(BF16)
    ks[...] = dot(mixed, wk_ref[...]).astype(BF16)
    vs_ref[...] = dot(mixed, wv_ref[...]).astype(BF16)
    qt[...] = turn(q_ref[...])
    kt_ref[...] = turn(k[...])
    kst_ref[...] = turn(ks[...])
    vt[...] = turn(v_ref[...])
    vst[...] = turn(vs_ref[...])
    masks = block_masks()
    pairs = HEADS // 2

    def group(g, carry):
        rows = pl.ds(pl.multiple_of(g * GROUP, GROUP), GROUP)
        allowed = allowed_ref[0, :, rows]
        allowed = jnp.concatenate([allowed, allowed], axis=1) > 0.5
        for p in range(pairs):
            lanes = pl.ds(p * GROUP, GROUP)
            keys = jnp.concatenate([k[rows, lanes], ks[rows, lanes]], axis=0)
            scores = dot(keys, two_heads_rows(qt[lanes, rows]))
            near = jnp.where(allowed, narrow(scores, masks, 0) * att_scale, NEG)
            far = narrow(scores, masks, GROUP) * att_scale
            peak = jnp.maximum(
                jnp.max(near, axis=0, keepdims=True), jnp.max(far, axis=0, keepdims=True)
            )
            near = jnp.exp(near - peak)
            far = jnp.exp(far - peak)
            total = jnp.sum(near, axis=0, keepdims=True) + jnp.sum(far, axis=0, keepdims=True)
            part = 1.0 / total
            near = near * part
            far = far * part
            weights_ref[g * pairs + p, :BLOCK] = near
            weights_ref[g * pairs + p, BLOCK:] = far
            values = jnp.concatenate([vt[lanes, rows], vst[lanes, rows]], axis=1)
            out = own_heads(dot(values, widen(near, far, masks)))
            att_ref[rows, lanes] = out.T.astype(BF16)
        return carry

    lax.fori_loop(0, span // GROUP, group, 0)


def attend(hidden, rows, allowed, wq, wk, wv, index):
    span, width = hidden.shape
    units = span // GROUP * (HEADS // 2)
    flat = like((span, width), BF16)
    turned = like((width, span), BF16)
    return call(
        lambda *refs: attend_kernel(1.0 / math.sqrt(width // HEADS), *refs),
        [flat, flat, flat, flat, flat, turned, turned]
        + [like((units, 2 * BLOCK, 2 * GROUP), F32)],
        [hidden, rows, allowed, wq, wk, wv],
        [whole(hidden), whole(rows), nth(allowed, index), whole(wq), whole(wk), whole(wv)],
        [row_buffer(span, width)]
        + [pltpu.VMEM(s, BF16) for s in ((width, span), (span, width), (span, width))]
        + [pltpu.VMEM((width, span), BF16)] * 2,
        flops=5 * 2 * span * width * width * 2,
    )


def attend_back_kernel(
    att_scale,
    d_att_ref,
    hidden_ref,
    mixed_ref,
    q_ref,
    v_ref,
    vs_ref,
    kt_ref,
    kst_ref,
    weights_ref,
    wq_ref,
    wk_ref,
    wv_ref,
    d_rows_ref,
    d_hidden_ref,
    gq_ref,
    gk_ref,
    gv_ref,
    buffer,
    datt_t,
    dq,
    dk,
    dv,
    dks,
    dvs,
):
    span, width = hidden_ref.shape
    datt_t[...] = turn(d_att_ref[0])
    masks = block_masks()
    pairs = HEADS // 2

    def group(g, carry):
        rows = pl.ds(pl.multiple_of(g * GROUP, GROUP), GROUP)
        for p in range(pairs):
            lanes = pl.ds(p * GROUP, GROUP)
            values = jnp.concatenate([v_ref[rows, lanes], vs_ref[rows, lanes]], axis=0)
            d_weights = dot(values, two_heads_rows(datt_t[lanes, rows]))
            near = weights_ref[g * pairs + p, :BLOCK]
            far = weights_ref[g * pairs + p, BLOCK:]
            d_near = near * narrow(d_weights, masks, 0)
            d_far = far * narrow(d_weights, masks, GROUP)
            total = jnp.sum(d_near, axis=0, keepdims=True) + jnp.sum(d_far, axis=0, keepdims=True)
            d_near = d_near - near * total
            d_far = d_far - far * total
            d_scores = widen(d_near, d_far, masks)
            keys = jnp.concatenate([kt_ref[lanes, rows], kst_ref[lanes, rows]], axis=1)
            dq[rows, lanes] = (own_heads(dot(keys, d_scores)).T * att_scale).astype(BF16)
            d_keys = (dot(d_scores, two_heads_lanes(q_ref[rows, lanes])) * att_scale).astype(BF16)
            dk[rows, lanes] = d_keys[:GROUP]
            dks[rows, lanes] = d_keys[GROUP:]
            d_values = dot(
                widen(near, far, masks), two_heads_lanes(d_att_ref[0, rows, lanes])
            ).astype(BF16)
            dv[rows, lanes] = d_values[:GROUP]
            dvs[rows, lanes] = d_values[GROUP:]
        return carry

    lax.fori_loop(0, span // GROUP, group, 0)
    lay(buffer, dot(dks[...], wk_ref[...], 1, 1) + dot(dvs[...], wv_ref[...], 1, 1))
    for t in range(BLOCK):
        d_rows_ref[t] = pick(buffer, t, d_rows_ref.shape[1]).astype(BF16)
    d_hidden_ref[...] = (
        dot(dq[...], wq_ref[...], 1, 1)
        + dot(dk[...], wk_ref[...], 1, 1)
        + dot(dv[...], wv_ref[...], 1, 1)
    )
    hidden_t = turn(hidden_ref[...])
    mixed_t = turn(mixed_ref[...])
    gq_ref[...] = dot(hidden_t, dq[...])
    gk_ref[...] = dot(hidden_t, dk[...]) + dot(mixed_t, dks[...])
    gv_ref[...] = dot(hidden_t, dv[...]) + dot(mixed_t, dvs[...])


def attend_back(d_att, hidden, kept, wq, wk, wv, index):
    span, width = hidden.shape
    args = [d_att, hidden, *kept, wq, wk, wv]
    square = like((width, width), F32)
    return call(
        lambda *refs: attend_back_kernel(1.0 / math.sqrt(width // HEADS), *refs),
        [like((BLOCK, span // BLOCK, width), BF16), like((span, width), F32)] + [square] * 3,
        args,
        [nth(d_att, index)] + [whole(a) for a in args[1:]],
        [row_buffer(span, width), pltpu.VMEM((width, span), BF16)]
        + [pltpu.VMEM((span, width), BF16)] * 5,
        flops=10 * 2 * span * width * width * 2,
    )


def feed_kernel(
    x_ref,
    att_ref,
    cot_ref,
    gain_ref,
    wo_ref,
    win_ref,
    wout_ref,
    out_ref,
    gout_ref,
    gin_ref,
    gwo_ref,
    d_resid_ref,
    d_att_ref,
    slope_ref,
    y1,
    unit,
    h2,
    h2t,
    d_h2,
    f_all,
    du_all,
    scales,
):
    step = pl.program_id(0)
    span = x_ref.shape[0]
    tile = 256
    tiles = [pl.ds(r, tile) for r in range(0, span, tile)]

    @pl.when(step == 0)
    def _():
        for rows in tiles:
            y = x_ref[rows].astype(F32) + dot(att_ref[rows], wo_ref[...])
            y1[rows] = y
            scale = lax.rsqrt(jnp.mean(y * y, axis=-1, keepdims=True) + EPS)
            n = y * scale
            unit[rows] = n
            scales[rows] = jnp.broadcast_to(scale, (tile, scales.shape[1]))
            low = (n * gain_ref[...]).astype(BF16)
            h2[rows] = low
            h2t[:, rows] = turn(low)
            d_h2[rows] = jnp.zeros((tile, d_h2.shape[1]), F32)

    root = math.sqrt(2.0 / math.pi)
    for rows in tiles:
        u = dot(h2[rows], win_ref[...])
        square = u * u
        bend = jnp.tanh(root * u * (1.0 + 0.044715 * square))
        half = 0.5 + 0.5 * bend
        f = (u * half).astype(BF16)
        slope = half + (0.5 * root) * u * (1.0 - bend * bend) * (1.0 + 0.134145 * square)
        du = (dot(cot_ref[rows], wout_ref[...], 1, 1) * slope).astype(BF16)
        y1[rows] = y1[rows] + dot(f, wout_ref[...])
        d_h2[rows] = d_h2[rows] + dot(du, win_ref[...], 1, 1)
        f_all[:, rows] = turn(f)
        du_all[rows] = du
    gout_ref[0] = dot(f_all[...], cot_ref[...]).astype(BF16)
    gin_ref[0] = dot(h2t[...], du_all[...]).astype(BF16)

    @pl.when(step == pl.num_programs(0) - 1)
    def _():
        total = None
        grad = None
        for rows in tiles:
            out_ref[rows] = y1[rows].astype(BF16)
            up, n = d_h2[rows], unit[rows]
            here = jnp.sum(up * n, axis=0, keepdims=True)
            total = here if total is None else total + here
            d_n = up * gain_ref[...]
            d_y = scales[rows][:, :1] * (d_n - n * jnp.mean(d_n * n, axis=-1, keepdims=True))
            d_y = d_y + cot_ref[rows].astype(F32)
            d_resid_ref[rows] = d_y
            low = d_y.astype(BF16)
            d_att_ref[rows] = dot(low, wo_ref[...], 1, 1).astype(BF16)
            du_all[rows] = low
            f_all[:, rows] = turn(att_ref[rows])
        gwo_ref[...] = dot(f_all[...], du_all[...]).astype(BF16)
        slope_ref[...] = jnp.broadcast_to(total, slope_ref.shape)


def feed(x, att, cot, gain, wo, win, wout):
    span, width = x.shape
    hidden = win.shape[1]
    steps = hidden // width
    flat = lambda dtype: like((span, width), dtype)
    parts = like((steps, width, width), BF16)
    outs = [
        flat(BF16),
        parts,
        parts,
        like((width, width), BF16),
        flat(F32),
        flat(BF16),
        like((8, width), F32),
    ]
    part_spec = pl.BlockSpec((1, width, width), lambda c: (c, 0, 0))
    return pl.pallas_call(
        feed_kernel,
        grid=(steps,),
        out_shape=outs,
        in_specs=[whole(a) for a in (x, att, cot, gain, wo)]
        + [
            pl.BlockSpec((width, width), lambda c: (0, c)),
            pl.BlockSpec((width, width), lambda c: (c, 0)),
        ],
        out_specs=[whole(outs[0]), part_spec, part_spec] + [whole(o) for o in outs[3:]],
        scratch_shapes=[
            pltpu.VMEM((span, width), F32),
            pltpu.VMEM((span, width), F32),
            pltpu.VMEM((span, width), BF16),
            pltpu.VMEM((width, span), BF16),
            pltpu.VMEM((span, width), F32),
            pltpu.VMEM((width, span), BF16),
            pltpu.VMEM((span, width), BF16),
            pltpu.VMEM((span, 128), F32),
        ],
        compiler_params=pltpu.CompilerParams(vmem_limit_bytes=VMEM_BYTES),
        cost_estimate=pl.CostEstimate(
            flops=6 * 2 * span * width * hidden, bytes_accessed=24 << 20, transcendentals=0
        ),
    )(x, att, cot, gain, wo, win, wout)


def leave_kernel(
    x_ref, gain_ref, d_hidden_ref, rows_ref, d_summary_ref, d_resid_ref, out_ref, total_ref, buffer
):
    d_summary = d_summary_ref[0] * (1.0 / BLOCK)
    for t in range(BLOCK):
        strew(buffer, t, rows_ref[t].astype(F32) + d_summary)
    x = x_ref[0].astype(F32)
    scale = lax.rsqrt(jnp.mean(x * x, axis=-1, keepdims=True) + EPS)
    n = x * scale
    up = d_hidden_ref[...] + lift(buffer)
    total_ref[...] = jnp.broadcast_to(jnp.sum(up * n, axis=0, keepdims=True), total_ref.shape)
    d_n = up * gain_ref[...]
    d_x = scale * (d_n - n * jnp.mean(d_n * n, axis=-1, keepdims=True))
    out_ref[...] = (d_x + d_resid_ref[0]).astype(BF16)


def leave(inputs, gain, d_hidden, rows, d_summary, d_resid, index):
    _, span, width = inputs.shape
    args = [inputs, gain, d_hidden, rows, d_summary, d_resid]
    return call(
        leave_kernel,
        [like((span, width), BF16), like((8, width), F32)],
        args,
        [
            nth(inputs, index),
            whole(gain),
            whole(d_hidden),
            whole(rows),
            nth(d_summary, index),
            nth(d_resid, index),
        ],
        [row_buffer(span, width)],
    )


def plan_plain(sort_scale, summary_all, real, w_sort):
    def plan_of(logits):
        plan = jnp.where(real, logits, NEG)
        for _ in range(ITERS):
            plan = plan - jax.nn.logsumexp(plan, axis=2, keepdims=True)
            fall = jax.nn.logsumexp(plan, axis=1, keepdims=True)
            plan = plan - jnp.where(real, fall, 0.0)
        return plan

    proj = lax.dot_general(
        summary_all, w_sort, (((2,), (0,)), ((), ())), preferred_element_type=F32
    ).astype(BF16)
    logits = sort_scale * jnp.einsum("sid,sjd->sij", proj, summary_all, preferred_element_type=F32)
    plan, back = jax.vjp(plan_of, logits)
    return proj, plan, back


def body(
    inputs,
    segment_ids,
    real_block,
    gain_attn,
    w_query,
    w_key,
    w_value,
    w_output,
    w_sort,
    gain_ffn,
    w_in,
    w_out,
    cotangent,
):
    seqs, span, width = inputs.shape
    blocks = span // BLOCK
    seq_size, dp_size = lax.axis_size("seq"), lax.axis_size("dp")
    count = blocks * seq_size
    small_plan = count == 128
    sort_scale = SORT_GAIN * BLOCK / math.sqrt(width)
    gain_one = gain_attn.astype(F32).reshape(1, width)
    gain_two = gain_ffn.astype(F32).reshape(1, width)
    first_block = lax.axis_index("seq") * blocks

    hidden, rows, summary = zip(*[enter(inputs, gain_one, s) for s in range(seqs)])
    flag_rows = jnp.broadcast_to(real_block.astype(BF16)[:, :, None], (seqs, blocks, 128))
    told = tell_all(jnp.concatenate([jnp.stack(summary), flag_rows], axis=-1))
    spread = [exchange(to_chunks(r, seq_size)) for r in rows]

    reals = told[:, :, :, width].transpose(1, 0, 2).reshape(seqs, count)
    total_blocks = jnp.sum(reals.astype(F32)).reshape(1, 1)
    for bit in bits(dp_size):
        total_blocks = total_blocks + swap(total_blocks, "dp", bit)

    if small_plan:
        proj, steps, plan, low, entropy = call(
            lambda *refs: plan_kernel(sort_scale, *refs),
            [
                like((seqs, count, width), BF16),
                like((2 * ITERS, seqs, count, count), F32),
                like((seqs, count, count), F32),
                like((seqs, count, count), BF16),
                like((8, 128), F32),
            ],
            [told, w_sort],
        )
        entropy = entropy[0, 0]
    else:
        summary_all = told[..., :width].transpose(1, 0, 2, 3).reshape(seqs, count, width)
        real = reals[:, None, :] == 1
        proj, plan, plan_back = plan_plain(sort_scale, summary_all, real, w_sort)
        prob = jnp.exp(plan)
        low = prob.astype(BF16)
        entropy = jnp.sum(jnp.where(reals[:, :, None] == 1, prob * plan, 0.0))

    segments = segment_ids.reshape(seqs, blocks, BLOCK)
    allowed = (segments.transpose(0, 2, 1)[:, :, :, None] == segments[:, None]).astype(F32)
    allowed = allowed.reshape(seqs, BLOCK, span)

    att, kept = [], []
    for s in range(seqs):
        mixed = from_chunks(exchange(mix(low, spread[s], s)))
        here, *rest = attend(hidden[s], mixed, allowed, w_query, w_key, w_value, s)
        att.append(here)
        kept.append(rest)

    flat = (seqs * span, width)
    output, grad_out, grad_in, grad_output, d_resid, d_att, slope = feed(
        inputs.reshape(flat),
        jnp.concatenate(att, axis=0),
        cotangent.reshape(flat),
        gain_two,
        w_output,
        w_in,
        w_out,
    )
    d_resid = d_resid.reshape(inputs.shape)
    d_att = d_att.reshape(inputs.shape)

    dp_bits, seq_bits = bits(dp_size), bits(seq_size)
    one = [("dp", bit) for bit in dp_bits] + [("seq", bit) for bit in seq_bits]
    two = one[:1] + [one[len(dp_bits)]] + one[1 : len(dp_bits)] + one[len(dp_bits) + 1 :]
    grad_out = reduce_all(grad_out.reshape(-1, width), one).astype(F32)
    grad_in = reduce_all(grad_in.reshape(-1, width), two)
    grad_in = jnp.concatenate(
        [grad_in[c : c + width] for c in range(0, grad_in.shape[0], width)], axis=1
    ).astype(F32)

    d_hidden, d_rows, d_prob, late = [], [], [], None
    for s in range(seqs):
        sent, here, *grads = attend_back(
            d_att, hidden[s], kept[s], w_query, w_key, w_value, s
        )
        d_hidden.append(here)
        late = grads if late is None else [a + b for a, b in zip(late, grads)]
        d_mixed = exchange(to_chunks(sent, seq_size))
        back, part = unmix(low, spread[s], d_mixed, s)
        d_rows.append(back)
        d_prob.append(part)
    heard = sum_seq(jnp.stack(d_prob))
    d_rows = [from_chunks(exchange(r)) for r in d_rows]

    late = jnp.concatenate([g.astype(BF16) for g in late] + [grad_output], axis=0)
    late = reduce_all(late, one).astype(F32)
    grad_query, grad_key, grad_value, grad_output = jnp.split(late, 4, axis=0)

    if small_plan:
        scalar = pl.BlockSpec(memory_space=pltpu.SMEM)
        args = [
            total_blocks,
            jnp.full((1, 1), first_block, jnp.int32),
            heard,
            told,
            w_sort,
            proj,
            steps,
            plan,
        ]
        outs = [like((seqs, blocks, width), F32), like((width, width), F32)]
        d_summary, grad_sort = pl.pallas_call(
            lambda *refs: plan_back_kernel(sort_scale, *refs),
            out_shape=outs,
            grid=(1,),
            in_specs=[scalar, scalar] + [whole(a) for a in args[2:]],
            out_specs=[whole(o) for o in outs],
            scratch_shapes=[pltpu.VMEM((count, width), F32)],
            compiler_params=pltpu.CompilerParams(vmem_limit_bytes=VMEM_BYTES),
        )(*args)
    else:
        d_prob = jnp.sum(heard.astype(F32), axis=0)
        d_plan = prob * d_prob - (
            jnp.where(reals[:, :, None] == 1, prob * plan + prob, 0.0) / total_blocks[0, 0]
        )
        (d_logits,) = plan_back(d_plan)
        d_logits = d_logits.astype(BF16)
        d_proj = sort_scale * jnp.einsum(
            "sij,sjd->sid", d_logits, summary_all, preferred_element_type=F32
        )
        d_proj = d_proj.astype(BF16)
        grad_sort = jnp.einsum("sid,sie->de", summary_all, d_proj, preferred_element_type=F32)
        d_summary = sort_scale * jnp.einsum(
            "sij,sid->sjd", d_logits, proj, preferred_element_type=F32
        ) + jnp.einsum("sie,de->sid", d_proj, w_sort, preferred_element_type=F32)
        d_summary = lax.dynamic_slice_in_dim(d_summary, first_block, blocks, 1)

    grad_sort = grad_sort.astype(BF16)
    for bit in bits(dp_size):
        got = swap(grad_sort, "dp", bit)
        grad_sort = (grad_sort.astype(F32) + got.astype(F32)).astype(BF16)

    input_grad, gains = zip(
        *[
            leave(inputs, gain_one, d_hidden[s], d_rows[s], d_summary, d_resid, s)
            for s in range(seqs)
        ]
    )
    small = jnp.concatenate(
        [
            sum(g[:1] for g in gains),
            slope[:1],
            jnp.full((1, width), entropy / seq_size),
            jnp.zeros((5, width), F32),
        ]
    )
    small = lax.all_to_all(
        jnp.broadcast_to(small[None], (dp_size * seq_size,) + small.shape),
        ("dp", "seq"),
        0,
        0,
        tiled=True,
    )
    small = jnp.sum(small, axis=0)
    penalty = -small[2, 0] / total_blocks[0, 0]
    return (
        output.reshape(inputs.shape),
        jnp.stack(input_grad),
        penalty,
        small[0],
        grad_query,
        grad_key,
        grad_value,
        grad_output,
        grad_sort.astype(F32),
        small[1],
        grad_in,
        grad_out,
    )


def solution(mesh):
    placed = (
        P("dp", "seq", None),
        P("dp", "seq"),
        P("dp", "seq"),
        P(),
        P(),
        P(),
        P(),
        P(),
        P(),
        P(),
        P(),
        P(),
        P("dp", "seq", None),
    )
    return jax.shard_map(
        body,
        mesh=mesh,
        in_specs=placed,
        out_specs=(
            P("dp", "seq", None),
            P("dp", "seq", None),
            P(),
            P(),
            P(),
            P(),
            P(),
            P(),
            P(),
            P(),
            P(),
            P(),
        ),
        check_vma=False,
    )
```

```python
import math

import jax
import jax.numpy as jnp
from jax import lax
from jax.experimental import pallas as pl
from jax.experimental.pallas import tpu as pltpu
from jax.sharding import PartitionSpec as P

HEADS = 8
BLOCK = 32
ITERS = 8
GROUP = 128

EPS = 1e-06
NEG = -1000000000.0
SORT_GAIN = 2.5
F32 = jnp.float32
BF16 = jnp.bfloat16
VMEM_BYTES = 56 * 2**20
COST = 3.0


def bits(size):
    return [1 << k for k in range(size.bit_length() - 1)]


def swap(array, axis, bit):
    return lax.ppermute(array, axis, [(i, i ^ bit) for i in range(lax.axis_size(axis))])


def send(array, dp_bits, seq_bits):
    seq = lax.axis_size("seq")
    mask = dp_bits * seq + seq_bits
    count = lax.axis_size("dp") * seq
    return lax.ppermute(array, ("dp", "seq"), [(i, i ^ mask) for i in range(count)])


CORE = (1, 0)
PLANE = ((0, 1), (2, 0), (2, 1))
LINE = ((0, 4), (0, 2), (0, 6))


def add_kernel(count, *refs):
    outs = refs[count:]
    each = outs[0].shape[0]
    for n, out_ref in enumerate(outs):
        part = pl.ds(n * each, each)
        total = refs[0][part].astype(F32)
        for ref in refs[1:count]:
            total = total + ref[part].astype(F32)
        out_ref[...] = total.astype(BF16)


def add_split(arrays, pieces, after=()):
    shape = arrays[0].shape
    out = like((shape[0] // pieces,) + shape[1:], BF16)
    kernel = lambda *refs: add_kernel(len(arrays), *refs)
    return list(call(kernel, [out] * pieces, arrays, after=after))


def sum_stages(keep, give):
    got = send(give, *CORE)
    own = add_split([keep, got], 4)
    yield own
    got = [send(g, *to) for g, to in zip(own[1:], PLANE)]
    own = add_split([own[0]] + got, 4)
    yield own
    got = [send(g, *to) for g, to in zip(own[1:], LINE)]
    own = add_split([own[0]] + got, 1)
    for bit in bits(lax.axis_size("seq"))[3:]:
        own = add_split([own[0], send(own[0], 0, bit)], 1)
    yield own
    got = [send(own[0], *to) for to in LINE]
    quarter = jnp.concatenate(own + got, axis=0)
    yield [quarter]
    got = [send(quarter, *to) for to in PLANE]
    quarters = [quarter] + got
    yield quarters
    yield quarters + [send(q, *CORE) for q in quarters]


def exchange(chunks):
    return lax.all_to_all(chunks, "seq", 0, 0, tiled=True)


def add(left, right):
    return (left.astype(F32) + right.astype(F32)).astype(BF16)


def sum_seq(part):
    for bit in bits(lax.axis_size("seq")):
        part = add(part, swap(part, "seq", bit))
    return part


def dot(left, right, left_dim=1, right_dim=0):
    return lax.dot_general(
        left, right, (((left_dim,), (right_dim,)), ((), ())), preferred_element_type=F32
    )


def whole(array):
    return pl.BlockSpec(array.shape, lambda *_: (0,) * array.ndim)


def nth(array, index):
    return pl.BlockSpec((1,) + array.shape[1:], lambda *_: (index,) + (0,) * (array.ndim - 1))


def call(
    kernel, outs, args, specs=None, scratch=(), flops=0, out_specs=None, grid=(1,), after=(), **more
):
    specs = specs or [whole(a) for a in args]
    moved = sum(math.prod(o.shape) * o.dtype.itemsize for o in outs)
    moved += sum(math.prod(a.shape) * a.dtype.itemsize for a in args)
    count, skip = len(args), len(after)
    return pl.pallas_call(
        lambda *refs: kernel(*refs[:count], *refs[count + skip :]),
        out_shape=outs,
        grid=grid,
        in_specs=list(specs) + [pl.BlockSpec(memory_space=pl.ANY)] * skip,
        out_specs=out_specs or [whole(o) for o in outs],
        scratch_shapes=list(scratch),
        compiler_params=pltpu.CompilerParams(vmem_limit_bytes=VMEM_BYTES),
        cost_estimate=pl.CostEstimate(
            flops=int(flops * COST), bytes_accessed=int(moved * COST), transcendentals=0
        ),
        **more,
    )(*args, *after)


SCALAR = pl.BlockSpec(memory_space=pltpu.SMEM)


def like(shape, dtype):
    return jax.ShapeDtypeStruct(shape, dtype)


def lay(buffer, value):
    for c in range(buffer.shape[0]):
        buffer[c] = value[:, c * 128 : (c + 1) * 128]


def lift(buffer):
    return jnp.concatenate([buffer[c] for c in range(buffer.shape[0])], axis=1)


def pick(buffer, t, count):
    return jnp.concatenate(
        [buffer[c, pl.ds(t, count, stride=BLOCK), :] for c in range(buffer.shape[0])], axis=1
    )


def strew(buffer, t, rows):
    for c in range(buffer.shape[0]):
        buffer[c, pl.ds(t, rows.shape[0], stride=BLOCK), :] = rows[:, c * 128 : (c + 1) * 128]


def chunk_shape(parts, blocks, width):
    row_parts = min(parts, BLOCK)
    return (parts, BLOCK // row_parts, blocks, width * row_parts // parts)


def chunk_places(shape, t):
    per = BLOCK // shape[1]
    cols = shape[0] // per
    return [(t // shape[1]) * cols + f for f in range(cols)], t % shape[1]


def store_row(ref, t, rows, shape=None):
    parts, place = chunk_places(shape or ref.shape, t)
    for f, part in enumerate(parts):
        ref[part, place] = rows[:, f * ref.shape[3] : (f + 1) * ref.shape[3]]


def load_row(ref, t):
    parts, place = chunk_places(ref.shape, t)
    return jnp.concatenate([ref[part, place] for part in parts], axis=1)


def row_buffer(span, width):
    return pltpu.VMEM((width // 128, span, 128), F32)


def enter_kernel(x_ref, gain_ref, flag_ref, hidden_ref, *refs):
    rows_refs, buffer = refs[:-1], refs[-1]
    seqs = len(rows_refs)
    parts, _, blocks, cols = rows_refs[0].shape
    width = hidden_ref.shape[2]
    each = width // cols
    shape = chunk_shape(parts, blocks, width)
    for s in range(seqs):
        x = x_ref[s].astype(F32)
        scale = lax.rsqrt(jnp.mean(x * x, axis=-1, keepdims=True) + EPS)
        hidden = (x * scale * gain_ref[...]).astype(BF16)
        hidden_ref[s] = hidden
        lay(buffer, hidden.astype(F32))
        total = None
        for t in range(BLOCK):
            rows = pick(buffer, t, blocks)
            store_row(rows_refs[s], t, rows.astype(BF16), shape)
            total = rows if total is None else total + rows
        low = (total * (1.0 / BLOCK)).astype(BF16)
        for part in range(parts):
            for f in range(each):
                rows_refs[0][part, shape[1] + s * each + f] = low[:, f * cols : (f + 1) * cols]
    for part in range(parts):
        rows_refs[0][part, shape[1] + seqs * each] = flag_ref[...]


def enter(inputs, gain, real, parts):
    seqs, span, width = inputs.shape
    blocks = span // BLOCK
    p, r, n, w = chunk_shape(parts, blocks, width)
    flags = jnp.repeat(real.astype(BF16).T, w // seqs, axis=1)
    more = seqs * (width // w) + 1
    return call(
        enter_kernel,
        [like(inputs.shape, BF16)]
        + [like((p, r + (more if s == 0 else 0), n, w), BF16) for s in range(seqs)],
        [inputs, gain, flags],
        scratch=[row_buffer(span, width)],
    )


def told_of(first, seqs, width):
    parts, _, blocks, cols = first.shape
    shape = chunk_shape(parts, blocks, width)
    each = width // cols
    told = first[:, shape[1] :]
    told = told.transpose(1, 0, 2, 3).reshape(told.shape[1], parts * blocks, cols)
    flags = told[-1][:, :: cols // seqs].T
    told = told[:-1].reshape(seqs, each, parts * blocks, cols).transpose(0, 2, 1, 3)
    return told.reshape(seqs, parts * blocks, width), flags


def told_summary(first_ref, s):
    parts, rows, blocks, width = first_ref.shape
    row = chunk_shape(parts, blocks, width)[1] + s
    return first_ref[:, row].reshape(parts * blocks, width)


def told_flags(first_ref, seqs, s):
    parts, rows, blocks, width = first_ref.shape
    flags = first_ref[:, rows - 1, :, s * (width // seqs) : s * (width // seqs) + 128]
    return flags.reshape(parts * blocks, 128).astype(F32)


def plan_kernel(sort_scale, told_ref, w_ref, proj_ref, steps_ref, plan_ref, low_ref, entropy_ref, count_ref):
    seqs = plan_ref.shape[0]
    plans, reals = [], []
    entropy = jnp.zeros((), F32)
    for s in range(seqs):
        summary = told_summary(told_ref, s)
        flags = told_flags(told_ref, seqs, s)
        real = flags.T > 0.5
        proj = dot(summary, w_ref[...]).astype(BF16)
        proj_ref[s] = proj
        plans.append(jnp.where(real, sort_scale * dot(proj, summary, 1, 1), NEG))
        reals.append(real)
    for step in range(2 * ITERS):
        axis = 1 - step % 2
        for s in range(seqs):
            peak = jnp.max(plans[s], axis=axis, keepdims=True)
            share = jnp.exp(plans[s] - peak)
            total = jnp.sum(share, axis=axis, keepdims=True)
            fall = peak + jnp.log(total)
            share = share * (1.0 / total)
            if axis == 0:
                fall = jnp.where(reals[s][:1], fall, 0.0)
                share = jnp.where(reals[s], share, 0.0)
            plans[s] = plans[s] - fall
            steps_ref[step, s] = share
    for s in range(seqs):
        flags = told_flags(told_ref, seqs, s)[:, :1]
        prob = jnp.exp(plans[s])
        plan_ref[s] = plans[s]
        low_ref[s] = prob.astype(BF16)
        entropy = entropy + jnp.sum(jnp.where(flags > 0.5, prob * plans[s], 0.0))
    entropy_ref[...] = jnp.full(entropy_ref.shape, entropy, F32)
    blocks = [jnp.sum(told_flags(told_ref, seqs, s), axis=0, keepdims=True) for s in range(seqs)]
    count_ref[...] = jnp.broadcast_to(sum(blocks), count_ref.shape)


def plan_back_kernel(
    sort_scale,
    count_ref,
    place_ref,
    heard_ref,
    told_ref,
    w_ref,
    proj_ref,
    steps_ref,
    plan_ref,
    d_summary_ref,
    grad_ref,
    buffer,
):
    place = place_ref[0, 0]
    seqs = plan_ref.shape[0]
    blocks = told_ref.shape[2]
    part = 1.0 / count_ref[:1]
    grads = []
    for s in range(seqs):
        flags = told_flags(told_ref, seqs, s)[:, :1]
        plan = plan_ref[s]
        prob = jnp.exp(plan)
        d_prob = heard_ref[s].astype(F32)
        grads.append(prob * d_prob - jnp.where(flags > 0.5, prob * plan + prob, 0.0) * part)
    for step in reversed(range(2 * ITERS)):
        for s in range(seqs):
            total = jnp.sum(grads[s], axis=1 - step % 2, keepdims=True)
            grads[s] = grads[s] - steps_ref[step, s] * total
    grad_sort = None
    for s in range(seqs):
        summary = told_summary(told_ref, s)
        flags = told_flags(told_ref, seqs, s)
        real = flags.T > 0.5
        d_logits = jnp.where(real, grads[s], 0.0)
        low = d_logits.astype(BF16)
        d_proj = (sort_scale * dot(low, summary)).astype(BF16)
        turned = low.astype(F32).T.astype(BF16)
        buffer[...] = sort_scale * dot(turned, proj_ref[s]) + dot(d_proj, w_ref[...], 1, 1)
        first = pl.multiple_of(place * blocks, blocks)
        d_summary_ref[s] = buffer[pl.ds(first, blocks), :]
        here = dot(summary, d_proj, 0, 0)
        grad_sort = here if grad_sort is None else grad_sort + here
    grad_ref[...] = grad_sort.astype(grad_ref.dtype)


def spread_row(ref, t):
    parts, rows, blocks, width = ref.shape
    return ref[:, t].reshape(parts * blocks, width)


def mix_kernel(low_ref, spread_ref, mixed_ref):
    parts, rows, blocks, width = mixed_ref.shape
    for t in range(rows):
        mixed = dot(low_ref[0], spread_row(spread_ref, t)).astype(BF16)
        mixed_ref[:, t] = mixed.reshape(parts, blocks, width)


def mix(low, spread, index, width):
    shape = chunk_shape(spread.shape[0], spread.shape[2], width)
    return call(mix_kernel, [like(shape, BF16)], [low, spread], [nth(low, index), whole(spread)])[0]


def unmix_kernel(low_ref, *refs):
    seqs = low_ref.shape[0]
    spread_refs, d_mixed_refs = refs[:seqs], refs[seqs : 2 * seqs]
    d_spread_ref, d_prob_ref = refs[2 * seqs :]
    parts, rows, blocks, width = d_mixed_refs[0].shape
    for s in range(seqs):
        turned = low_ref[s].astype(F32).T.astype(BF16)
        d_prob = None
        for t in range(rows):
            grad = spread_row(d_mixed_refs[s], t)
            here = dot(grad, spread_row(spread_refs[s], t), 1, 1)
            d_prob = here if d_prob is None else d_prob + here
            back = dot(turned, grad).astype(BF16)
            d_spread_ref[:, s * rows + t] = back.reshape(parts, blocks, width)
        d_prob_ref[s] = d_prob.astype(BF16)


def unmix(low, spread, d_mixed, after=()):
    p, r, n, w = d_mixed[0].shape
    seqs = low.shape[0]
    return call(
        unmix_kernel,
        [like((p, seqs * r, n, w), BF16), like(low.shape, BF16)],
        [low, *spread, *d_mixed],
        after=after,
    )


def block_masks():
    lane = lax.broadcasted_iota(jnp.int32, (BLOCK, 2 * GROUP), 1)
    owner = (lane % GROUP) // BLOCK
    return [owner == b for b in range(GROUP // BLOCK)]


def narrow(full, masks, start):
    out = full[start : start + BLOCK]
    for b in range(1, len(masks)):
        out = jnp.where(masks[b], full[start + b * BLOCK : start + (b + 1) * BLOCK], out)
    return out


def widen(first, second, masks):
    zero = jnp.zeros_like(first)
    return jnp.concatenate(
        [jnp.where(m, first, zero) for m in masks] + [jnp.where(m, second, zero) for m in masks],
        axis=0,
    ).astype(BF16)


def two_heads_lanes(rows):
    lane = lax.broadcasted_iota(jnp.int32, rows.shape, 1)
    low = lane < rows.shape[1] // 2
    zero = jnp.zeros_like(rows)
    return jnp.concatenate([jnp.where(low, rows, zero), jnp.where(low, zero, rows)], axis=0)


def two_heads_rows(columns):
    row = lax.broadcasted_iota(jnp.int32, columns.shape, 0)
    low = row < columns.shape[0] // 2
    zero = jnp.zeros_like(columns)
    return jnp.concatenate([jnp.where(low, columns, zero), jnp.where(low, zero, columns)], axis=1)


def own_heads(full):
    half = full.shape[1] // 2
    row = lax.broadcasted_iota(jnp.int32, (full.shape[0], half), 0)
    return jnp.where(row < full.shape[0] // 2, full[:, :half], full[:, half:])


def turn(array):
    return array.astype(F32).T.astype(BF16)


def project_kernel(hidden_ref, wq_ref, wk_ref, wv_ref, q_ref, k_ref, v_ref, qt_ref, kt_ref, vt_ref):
    hidden = hidden_ref[0]
    for w_ref, flat_ref, turned_ref in (
        (wq_ref, q_ref, qt_ref),
        (wk_ref, k_ref, kt_ref),
        (wv_ref, v_ref, vt_ref),
    ):
        full = dot(hidden, w_ref[...])
        flat_ref[0] = full.astype(BF16)
        turned_ref[0] = full.T.astype(BF16)


def project(hidden, wq, wk, wv):
    seqs, span, width = hidden.shape
    flat = pl.BlockSpec((1, span, width), lambda s: (s, 0, 0))
    turned = pl.BlockSpec((1, width, span), lambda s: (s, 0, 0))
    return call(
        project_kernel,
        [like((seqs, span, width), BF16)] * 3 + [like((seqs, width, span), BF16)] * 3,
        [hidden, wq, wk, wv],
        [flat] + [whole(wq)] * 3,
        flops=6 * seqs * span * width * width,
        grid=(seqs,),
        out_specs=[flat] * 3 + [turned] * 3,
    )


def attend_kernel(
    att_scale,
    rows_ref,
    allowed_ref,
    wk_ref,
    wv_ref,
    k_ref,
    qt_ref,
    vt_ref,
    att_ref,
    mixed_ref,
    vs_ref,
    kst_ref,
    weights_ref,
    buffer,
    ks,
    vst,
):
    span, width = mixed_ref.shape
    for t in range(BLOCK):
        strew(buffer, t, load_row(rows_ref, t).astype(F32))
    mixed_ref[...] = lift(buffer).astype(BF16)
    mixed = mixed_ref[...]
    full = dot(mixed, wk_ref[...])
    ks[...] = full.astype(BF16)
    kst_ref[...] = full.T.astype(BF16)
    full = dot(mixed, wv_ref[...])
    vs_ref[...] = full.astype(BF16)
    vst[...] = full.T.astype(BF16)
    masks = block_masks()
    pairs = HEADS // 2

    def group(g, carry):
        rows = pl.ds(pl.multiple_of(g * GROUP, GROUP), GROUP)
        allowed = allowed_ref[0, :, rows]
        allowed = jnp.concatenate([allowed, allowed], axis=1) > 0.5
        for p in range(pairs):
            lanes = pl.ds(p * GROUP, GROUP)
            keys = jnp.concatenate([k_ref[0, rows, lanes], ks[rows, lanes]], axis=0)
            scores = dot(keys, two_heads_rows(qt_ref[0, lanes, rows]))
            near = jnp.where(allowed, narrow(scores, masks, 0) * att_scale, NEG)
            far = narrow(scores, masks, GROUP) * att_scale
            peak = jnp.maximum(
                jnp.max(near, axis=0, keepdims=True), jnp.max(far, axis=0, keepdims=True)
            )
            near = jnp.exp(near - peak)
            far = jnp.exp(far - peak)
            total = jnp.sum(near, axis=0, keepdims=True) + jnp.sum(far, axis=0, keepdims=True)
            part = 1.0 / total
            near = near * part
            far = far * part
            weights_ref[g * pairs + p, :BLOCK] = near
            weights_ref[g * pairs + p, BLOCK:] = far
            values = jnp.concatenate([vt_ref[0, lanes, rows], vst[lanes, rows]], axis=1)
            out = own_heads(dot(values, widen(near, far, masks)))
            att_ref[rows, lanes] = out.T.astype(BF16)
        return carry

    lax.fori_loop(0, span // GROUP, group, 0)


def attend(rows, allowed, wk, wv, k, qt, vt, index):
    seqs, span, width = k.shape
    units = span // GROUP * (HEADS // 2)
    flat = like((span, width), BF16)
    args = [rows, allowed, wk, wv, k, qt, vt]
    return call(
        lambda *refs: attend_kernel(1.0 / math.sqrt(width // HEADS), *refs),
        [flat] * 3 + [like((width, span), BF16), like((units, 2 * BLOCK, 2 * GROUP), F32)],
        args,
        [whole(rows), nth(allowed, index), whole(wk), whole(wv)]
        + [nth(a, index) for a in (k, qt, vt)],
        [row_buffer(span, width), pltpu.VMEM((span, width), BF16), pltpu.VMEM((width, span), BF16)],
        flops=8 * span * width * width,
    )


def attend_back_kernel(
    att_scale,
    d_att_ref,
    q_ref,
    v_ref,
    kt_ref,
    vs_ref,
    kst_ref,
    weights_ref,
    wk_ref,
    wv_ref,
    d_rows_ref,
    dq,
    dk,
    dv,
    dks,
    dvs,
    buffer,
    datt_t,
):
    span, width = vs_ref.shape
    datt_t[...] = turn(d_att_ref[0])
    masks = block_masks()
    pairs = HEADS // 2

    def group(g, carry):
        rows = pl.ds(pl.multiple_of(g * GROUP, GROUP), GROUP)
        for p in range(pairs):
            lanes = pl.ds(p * GROUP, GROUP)
            values = jnp.concatenate([v_ref[0, rows, lanes], vs_ref[rows, lanes]], axis=0)
            d_weights = dot(values, two_heads_rows(datt_t[lanes, rows]))
            near = weights_ref[g * pairs + p, :BLOCK]
            far = weights_ref[g * pairs + p, BLOCK:]
            d_near = near * narrow(d_weights, masks, 0)
            d_far = far * narrow(d_weights, masks, GROUP)
            total = jnp.sum(d_near, axis=0, keepdims=True) + jnp.sum(d_far, axis=0, keepdims=True)
            d_near = d_near - near * total
            d_far = d_far - far * total
            d_scores = widen(d_near, d_far, masks)
            keys = jnp.concatenate([kt_ref[0, lanes, rows], kst_ref[lanes, rows]], axis=1)
            dq[rows, lanes] = (own_heads(dot(keys, d_scores)).T * att_scale).astype(BF16)
            d_keys = (dot(d_scores, two_heads_lanes(q_ref[0, rows, lanes])) * att_scale).astype(BF16)
            dk[rows, lanes] = d_keys[:GROUP]
            dks[rows, lanes] = d_keys[GROUP:]
            d_values = dot(
                widen(near, far, masks), two_heads_lanes(d_att_ref[0, rows, lanes])
            ).astype(BF16)
            dv[rows, lanes] = d_values[:GROUP]
            dvs[rows, lanes] = d_values[GROUP:]
        return carry

    lax.fori_loop(0, span // GROUP, group, 0)
    lay(buffer, dot(dks[...], wk_ref[...], 1, 1) + dot(dvs[...], wv_ref[...], 1, 1))
    for t in range(BLOCK):
        store_row(d_rows_ref, t, pick(buffer, t, d_rows_ref.shape[2]).astype(BF16))


def attend_back(d_att, q, v, kt, kept, wk, wv, shape, index, after=()):
    seqs, span, width = q.shape
    args = [d_att, q, v, kt, *kept, wk, wv]
    flat = like((span, width), BF16)
    return call(
        lambda *refs: attend_back_kernel(1.0 / math.sqrt(width // HEADS), *refs),
        [like(shape, BF16)] + [flat] * 5,
        args,
        [nth(a, index) for a in args[:4]]
        + [whole(a) for a in args[4:]],
        [row_buffer(span, width), pltpu.VMEM((width, span), BF16)],
        flops=12 * span * width * width,
        after=after,
    )


def late_kernel(split_ref, hidden_ref, gwo_ref, *refs):
    keep_ref, give_ref, buffer = refs[-3:]
    seqs, span, width = hidden_ref.shape
    core, place = split_ref[0], split_ref[1]
    per = len(refs[:-3]) // seqs
    totals = [None, None, None]
    for s in range(seqs):
        mixed_ref, dq, dk, dv, dks, dvs = refs[s * per : (s + 1) * per]
        hidden_t = turn(hidden_ref[s])
        mixed_t = turn(mixed_ref[...])
        here = (
            dot(hidden_t, dq[...]),
            dot(hidden_t, dk[...]) + dot(mixed_t, dks[...]),
            dot(hidden_t, dv[...]) + dot(mixed_t, dvs[...]),
        )
        totals = [h if t is None else t + h for t, h in zip(totals, here)]
    for n in range(3):
        buffer[n] = totals[n]
    buffer[3] = gwo_ref[...].astype(F32)
    blocks, rows = keep_ref.shape[0], keep_ref.shape[1] // 4
    for side, ref in ((core, keep_ref), (1 - core, give_ref)):
        for j in range(blocks):
            part = pl.ds(pl.multiple_of((side * blocks + j) * rows, rows), rows)
            at = j ^ (place % blocks)
            for n in range(4):
                ref[at, n * rows : (n + 1) * rows] = buffer[n, part].astype(BF16)


def late(split, hidden, gwo, parts, after=()):
    seqs, span, width = hidden.shape
    args = [split, hidden, gwo, *[a for part in parts for a in part]]
    shape = like((16, 4 * width // 32, width), BF16)
    return call(
        late_kernel,
        [shape, shape],
        args,
        [SCALAR] + [whole(a) for a in args[1:]],
        [pltpu.VMEM((4, width, width), F32)],
        flops=10 * seqs * span * width * width,
        after=after,
    )


def end_blocks(split_ref, refs):
    each = refs[0].shape[0]
    for n, ref in enumerate(refs):
        for r in range(each):
            yield ref[r], (n * each + r) ^ split_ref[1]


def late_end_kernel(split_ref, *refs):
    outs = refs[-4:]
    rows = refs[0].shape[1] // 4
    for block, index in end_blocks(split_ref, refs[:-4]):
        part = pl.ds(pl.multiple_of(index * rows, rows), rows)
        for n, out_ref in enumerate(outs):
            out_ref[part] = block[n * rows : (n + 1) * rows].astype(F32)


def late_end(split, parts):
    width = parts[0].shape[2]
    return call(
        late_end_kernel,
        [like((width, width), F32)] * 4,
        [split, *parts],
        [SCALAR] + [whole(p) for p in parts],
    )


def d_hidden_kernel(wq_ref, wk_ref, wv_ref, *refs):
    out_ref = refs[-1]
    for s in range(out_ref.shape[0]):
        dq, dk, dv = refs[3 * s : 3 * s + 3]
        out_ref[s] = (
            dot(dq[...], wq_ref[...], 1, 1)
            + dot(dk[...], wk_ref[...], 1, 1)
            + dot(dv[...], wv_ref[...], 1, 1)
        )


def d_hidden_of(wq, wk, wv, parts, after=()):
    args = [wq, wk, wv] + [a for part in parts for a in part]
    shape = (len(parts),) + parts[0][0].shape
    flops = 6 * shape[0] * shape[1] * shape[2] ** 2
    return call(d_hidden_kernel, [like(shape, F32)], args, flops=flops, after=after)[0]


def feed_kernel(
    seqs,
    split_ref,
    x_ref,
    cot_ref,
    gain_ref,
    wo_ref,
    win_ref,
    wout_ref,
    *refs,
):
    att_refs = refs[:seqs]
    (
        out_ref,
        keep_ref,
        give_ref,
        gwo_ref,
        d_resid_ref,
        d_att_ref,
        slope_ref,
        y1,
        unit,
        h2,
        h2t,
        d_h2,
        f_all,
        du_all,
        scales,
    ) = refs[seqs:]
    step = pl.program_id(0)
    span = x_ref.shape[0]
    tile = 512
    tiles = [pl.ds(r, tile) for r in range(0, span, tile)]

    def att_tile(rows):
        each = att_refs[0].shape[0]
        return att_refs[rows.start // each][pl.ds(rows.start % each, tile)]

    @pl.when(step == 0)
    def _():
        for rows in tiles:
            y = x_ref[rows].astype(F32) + dot(att_tile(rows), wo_ref[...])
            y1[rows] = y
            scale = lax.rsqrt(jnp.mean(y * y, axis=-1, keepdims=True) + EPS)
            n = y * scale
            unit[rows] = n
            scales[rows] = jnp.broadcast_to(scale, (tile, scales.shape[1]))
            low = (n * gain_ref[...]).astype(BF16)
            h2[rows] = low
            h2t[:, rows] = turn(low)
            d_h2[rows] = jnp.zeros((tile, d_h2.shape[1]), F32)

    root = math.sqrt(2.0 / math.pi)
    for rows in tiles:
        u = dot(h2[rows], win_ref[...])
        square = u * u
        bend = jnp.tanh(root * u * (1.0 + 0.044715 * square))
        half = 0.5 + 0.5 * bend
        f = (u * half).astype(BF16)
        slope = half + (0.5 * root) * u * (1.0 - bend * bend) * (1.0 + 0.134145 * square)
        du = (dot(cot_ref[rows], wout_ref[...], 1, 1) * slope).astype(BF16)
        y1[rows] = y1[rows] + dot(f, wout_ref[...])
        d_h2[rows] = d_h2[rows] + dot(du, win_ref[...], 1, 1)
        f_all[:, rows] = turn(f)
        du_all[rows] = du
    grads = (
        dot(f_all[...], cot_ref[...]).astype(BF16),
        dot(h2t[...], du_all[...]).astype(BF16),
    )
    blocks, block = keep_ref.shape[0], keep_ref.shape[1] // 2
    count = grads[0].shape[0] // block
    for first, ref in ((0, give_ref), (2, keep_ref)):

        @pl.when(step // 2 * 2 == first)
        def _():
            for j in range(count):
                at = ((step % 2) * count + j) ^ (split_ref[1] % blocks)
                for n in range(2):
                    ref[at, n * block : (n + 1) * block] = grads[n][j * block : (j + 1) * block]


    @pl.when(step == pl.num_programs(0) - 1)
    def _():
        total = None
        grad = None
        for rows in tiles:
            out_ref[rows] = y1[rows].astype(BF16)
            up, n = d_h2[rows], unit[rows]
            here = jnp.sum(up * n, axis=0, keepdims=True)
            total = here if total is None else total + here
            d_n = up * gain_ref[...]
            d_y = scales[rows][:, :1] * (d_n - n * jnp.mean(d_n * n, axis=-1, keepdims=True))
            d_y = d_y + cot_ref[rows].astype(F32)
            low = d_y.astype(BF16)
            d_resid_ref[rows] = low
            d_att_ref[rows] = dot(low, wo_ref[...], 1, 1).astype(BF16)
            du_all[rows] = low
            f_all[:, rows] = turn(att_tile(rows))
        gwo_ref[...] = dot(f_all[...], du_all[...]).astype(BF16)
        slope_ref[...] = jnp.broadcast_to(total, slope_ref.shape)


def feed(split, x, att, cot, gain, wo, win, wout):
    span, width = x.shape
    hidden = win.shape[1]
    steps = hidden // width
    flat = lambda dtype: like((span, width), dtype)
    parts = like((16, 2 * hidden // 32, width), BF16)
    outs = [
        flat(BF16),
        parts,
        parts,
        like((width, width), BF16),
        flat(BF16),
        flat(BF16),
        like((8, width), F32),
    ]

    def chunk(c, split_ref):
        return ((1 - c // 2) ^ split_ref[0]) * 2 + c % 2

    return pl.pallas_call(
        lambda *refs: feed_kernel(len(att), *refs),
        grid_spec=pltpu.PrefetchScalarGridSpec(
            num_scalar_prefetch=1,
            grid=(steps,),
            in_specs=[whole(a) for a in (x, cot, gain, wo)]
            + [
                pl.BlockSpec((width, width), lambda c, r: (0, chunk(c, r))),
                pl.BlockSpec((width, width), lambda c, r: (chunk(c, r), 0)),
            ]
            + [whole(a) for a in att],
            out_specs=[whole(o) for o in outs],
            scratch_shapes=[
                pltpu.VMEM((span, width), F32),
                pltpu.VMEM((span, width), F32),
                pltpu.VMEM((span, width), BF16),
                pltpu.VMEM((width, span), BF16),
                pltpu.VMEM((span, width), F32),
                pltpu.VMEM((width, span), BF16),
                pltpu.VMEM((span, width), BF16),
                pltpu.VMEM((span, 128), F32),
            ],
        ),
        out_shape=outs,
        compiler_params=pltpu.CompilerParams(vmem_limit_bytes=VMEM_BYTES),
        cost_estimate=pl.CostEstimate(
            flops=int(COST * 12 * span * width * hidden),
            bytes_accessed=int(COST * (24 << 20)),
            transcendentals=0,
        ),
    )(split, x, cot, gain, wo, win, wout, *att)


def feed_end_kernel(split_ref, *refs):
    gout_ref, gin_ref = refs[-2:]
    width = gout_ref.shape[1]
    rows = refs[0].shape[1] // 2
    per = width // rows
    for block, index in end_blocks(split_ref, refs[:-2]):
        gout_ref[pl.ds(pl.multiple_of(index * rows, rows), rows)] = block[:rows].astype(F32)
        part = pl.ds(pl.multiple_of(index % per * rows, rows), rows)
        lanes = pl.ds(pl.multiple_of(index // per * width, width), width)
        gin_ref[part, lanes] = block[rows:].astype(F32)


def feed_end(split, parts):
    width = parts[0].shape[2]
    hidden = 16 * parts[0].shape[1]
    return call(
        feed_end_kernel,
        [like((hidden, width), F32), like((width, hidden), F32)],
        [split, *parts],
        [SCALAR] + [whole(p) for p in parts],
    )


def leave_kernel(
    x_ref, gain_ref, d_hidden_ref, rows_ref, d_summary_ref, d_resid_ref, out_ref, total_ref, buffer
):
    d_summary = d_summary_ref[0] * (1.0 / BLOCK)
    for t in range(BLOCK):
        strew(buffer, t, load_row(rows_ref, t).astype(F32) + d_summary)
    x = x_ref[0].astype(F32)
    scale = lax.rsqrt(jnp.mean(x * x, axis=-1, keepdims=True) + EPS)
    n = x * scale
    up = d_hidden_ref[0] + lift(buffer)
    total_ref[0] = jnp.broadcast_to(jnp.sum(up * n, axis=0, keepdims=True), total_ref.shape[1:])
    d_n = up * gain_ref[...]
    d_x = scale * (d_n - n * jnp.mean(d_n * n, axis=-1, keepdims=True))
    out_ref[0] = (d_x + d_resid_ref[0].astype(F32)).astype(BF16)


def leave(inputs, gain, d_hidden, rows, d_summary, d_resid, after=()):
    seqs, span, width = inputs.shape
    p, r, n, w = rows.shape
    args = [inputs, gain, d_hidden, rows, d_summary, d_resid]
    each = lambda a: pl.BlockSpec((1,) + a.shape[1:], lambda s: (s, 0, 0))
    outs = [like(inputs.shape, BF16), like((seqs, 8, width), F32)]
    return call(
        leave_kernel,
        outs,
        args,
        [
            each(inputs),
            whole(gain),
            each(d_hidden),
            pl.BlockSpec((p, r // seqs, n, w), lambda s: (0, s, 0, 0)),
            each(d_summary),
            each(d_resid),
        ],
        [row_buffer(span, width)],
        grid=(seqs,),
        out_specs=[each(o) for o in outs],
        after=after,
    )


def plan_plain(sort_scale, summary_all, real, w_sort):
    def plan_of(logits):
        plan = jnp.where(real, logits, NEG)
        for _ in range(ITERS):
            plan = plan - jax.nn.logsumexp(plan, axis=2, keepdims=True)
            fall = jax.nn.logsumexp(plan, axis=1, keepdims=True)
            plan = plan - jnp.where(real, fall, 0.0)
        return plan

    proj = lax.dot_general(
        summary_all, w_sort, (((2,), (0,)), ((), ())), preferred_element_type=F32
    ).astype(BF16)
    logits = sort_scale * jnp.einsum("sid,sjd->sij", proj, summary_all, preferred_element_type=F32)
    plan, back = jax.vjp(plan_of, logits)
    return proj, plan, back


def places():
    dp, seq = lax.axis_index("dp"), lax.axis_index("seq")
    core, x, y = dp % 2, (dp // 2) % 2, seq % 2
    line = (seq // 2) % 2 * 2 + (seq // 4) % 2
    return jnp.stack([core, core * 16 + x * 8 + y * 4 + line]).astype(jnp.int32)


def body(
    inputs,
    segment_ids,
    real_block,
    gain_attn,
    w_query,
    w_key,
    w_value,
    w_output,
    w_sort,
    gain_ffn,
    w_in,
    w_out,
    cotangent,
):
    seqs, span, width = inputs.shape
    blocks = span // BLOCK
    seq_size, dp_size = lax.axis_size("seq"), lax.axis_size("dp")
    count = blocks * seq_size
    small_plan = count == 128
    sort_scale = SORT_GAIN * BLOCK / math.sqrt(width)
    gain_one = gain_attn.astype(F32).reshape(1, width)
    gain_two = gain_ffn.astype(F32).reshape(1, width)
    place = lax.axis_index("seq")
    first_block = place * blocks
    place = place.astype(jnp.int32).reshape(1, 1)
    split = places()

    hidden, *rows = enter(inputs, gain_one, real_block, seq_size)
    spread = [exchange(r) for r in rows]
    q, k, v, qt, kt, vt = project(hidden, w_query, w_key, w_value)

    if small_plan:
        proj, steps, plan, low, entropy, total_blocks = call(
            lambda *refs: plan_kernel(sort_scale, *refs),
            [
                like((seqs, count, width), BF16),
                like((2 * ITERS, seqs, count, count), F32),
                like((seqs, count, count), F32),
                like((seqs, count, count), BF16),
                like((8, 128), F32),
                like((8, 128), F32),
            ],
            [spread[0], w_sort],
            after=(q,),
        )
        entropy = entropy[0, 0]
    else:
        summary_all, reals = told_of(spread[0], seqs, width)
        real = reals[:, None, :] == 1
        proj, plan, plan_back = plan_plain(sort_scale, summary_all, real, w_sort)
        prob = jnp.exp(plan)
        low = prob.astype(BF16)
        entropy = jnp.sum(jnp.where(reals[:, :, None] == 1, prob * plan, 0.0))
        total_blocks = jnp.full((8, 128), jnp.sum(reals.astype(F32)))
    for bit in bits(dp_size):
        total_blocks = total_blocks + swap(total_blocks, "dp", bit)

    segments = segment_ids.reshape(seqs, blocks, BLOCK)
    allowed = (segments.transpose(0, 2, 1)[:, :, :, None] == segments[:, None]).astype(F32)
    allowed = allowed.reshape(seqs, BLOCK, span)

    att, kept = [], []
    for s in range(seqs):
        part = mix(low, spread[s], s, width)
        here, *rest = attend(exchange(part), allowed, w_key, w_value, k, qt, vt, s)
        att.append(here)
        kept.append(rest)

    flat = (seqs * span, width)
    output, keep, give, grad_output, d_resid, d_att, slope = feed(
        split,
        inputs.reshape(flat),
        att,
        cotangent.reshape(flat),
        gain_two,
        w_output,
        w_in,
        w_out,
    )
    d_resid = d_resid.reshape(inputs.shape)
    d_att = d_att.reshape(inputs.shape)
    stages = sum_stages(keep, give)
    next(stages)
    grads, d_mixed = [], []
    chunks = chunk_shape(seq_size, blocks, width)
    for s in range(seqs):
        sent, *here = attend_back(d_att, q, v, kt, kept[s][1:], w_key, w_value, chunks, s)
        grads.append(here)
        if s == 0:
            next(stages)
        d_mixed.append(exchange(sent))
    parts = late(
        split, hidden, grad_output, [[kept[s][0], *grads[s]] for s in range(seqs)]
    )
    next(stages)
    d_hidden = d_hidden_of(w_query, w_key, w_value, [g[:3] for g in grads])
    late_stages = sum_stages(*parts)
    d_rows, d_prob = unmix(low, spread, d_mixed)
    heard = sum_seq(d_prob)
    d_rows = exchange(d_rows)
    *_, last = stages
    grad_out, grad_in = feed_end(split, last)
    *_, last = late_stages
    grad_query, grad_key, grad_value, grad_output = late_end(split, last)

    if small_plan:
        args = [
            total_blocks,
            place,
            heard,
            spread[0],
            w_sort,
            proj,
            steps,
            plan,
        ]
        outs = [like((seqs, blocks, width), F32), like((width, width), BF16)]
        d_summary, grad_sort = pl.pallas_call(
            lambda *refs: plan_back_kernel(sort_scale, *refs),
            out_shape=outs,
            grid=(1,),
            in_specs=[whole(total_blocks), SCALAR] + [whole(a) for a in args[2:]],
            out_specs=[whole(o) for o in outs],
            scratch_shapes=[pltpu.VMEM((count, width), F32)],
            compiler_params=pltpu.CompilerParams(vmem_limit_bytes=VMEM_BYTES),
        )(*args)
    else:
        d_prob = heard.astype(F32)
        d_plan = prob * d_prob - (
            jnp.where(reals[:, :, None] == 1, prob * plan + prob, 0.0) / total_blocks[0, 0]
        )
        (d_logits,) = plan_back(d_plan)
        d_logits = d_logits.astype(BF16)
        d_proj = sort_scale * jnp.einsum(
            "sij,sjd->sid", d_logits, summary_all, preferred_element_type=F32
        )
        d_proj = d_proj.astype(BF16)
        grad_sort = jnp.einsum("sid,sie->de", summary_all, d_proj, preferred_element_type=F32)
        d_summary = sort_scale * jnp.einsum(
            "sij,sid->sjd", d_logits, proj, preferred_element_type=F32
        ) + jnp.einsum("sie,de->sid", d_proj, w_sort, preferred_element_type=F32)
        d_summary = lax.dynamic_slice_in_dim(d_summary, first_block, blocks, 1)

    grad_sort = grad_sort.astype(BF16)
    grad_sort = add(grad_sort, send(grad_sort, *CORE))
    input_grad, gains = leave(
        inputs, gain_one, d_hidden, d_rows, d_summary, d_resid, (grad_sort,)
    )
    grad_sort = grad_sort.astype(F32) + send(grad_sort, 2, 0).astype(F32)
    small = jnp.concatenate(
        [
            jnp.sum(gains[:, :1], axis=0),
            slope[:1],
            jnp.full((1, width), entropy / seq_size),
            jnp.zeros((5, width), F32),
        ]
    )
    small = lax.all_to_all(
        jnp.broadcast_to(small[None], (dp_size * seq_size,) + small.shape),
        ("dp", "seq"),
        0,
        0,
        tiled=True,
    )
    small = jnp.sum(small, axis=0)
    penalty = -small[2, 0] / total_blocks[0, 0]
    return (
        output.reshape(inputs.shape),
        input_grad,
        penalty,
        small[0],
        grad_query,
        grad_key,
        grad_value,
        grad_output,
        grad_sort,
        small[1],
        grad_in,
        grad_out,
    )


def solution(mesh):
    placed = (
        P("dp", "seq", None),
        P("dp", "seq"),
        P("dp", "seq"),
        P(),
        P(),
        P(),
        P(),
        P(),
        P(),
        P(),
        P(),
        P(),
        P("dp", "seq", None),
    )
    return jax.shard_map(
        body,
        mesh=mesh,
        in_specs=placed,
        out_specs=(
            P("dp", "seq", None),
            P("dp", "seq", None),
            P(),
            P(),
            P(),
            P(),
            P(),
            P(),
            P(),
            P(),
            P(),
            P(),
        ),
        check_vma=False,
    )
```

```python
import math

import jax
import jax.numpy as jnp
from jax import lax
from jax.experimental import pallas as pl
from jax.experimental.pallas import tpu as pltpu
from jax.sharding import PartitionSpec as P

HEADS = 8
BLOCK = 32
ITERS = 8
GROUP = 128

EPS = 1e-06
NEG = -1000000000.0
SORT_GAIN = 2.5
F32 = jnp.float32
BF16 = jnp.bfloat16
VMEM_BYTES = 56 * 2**20
COST = 3.0


def bits(size):
    return [1 << k for k in range(size.bit_length() - 1)]


def swap(array, axis, bit):
    return lax.ppermute(array, axis, [(i, i ^ bit) for i in range(lax.axis_size(axis))])


def send(array, *to):
    seq = lax.axis_size("seq")
    pairs = []
    for i in range(lax.axis_size("dp") * seq):
        dp_bits, seq_bits = to[-(i // seq % 2)]
        pairs.append((i, i ^ (dp_bits * seq + seq_bits)))
    return lax.ppermute(array, ("dp", "seq"), pairs)


CORE = (1, 0)
X, Y = (2, 0), (0, 1)
LINE = ((0, 4), (0, 2), (0, 6))


def spot(index, place, core):
    at = (index ^ place) % 16
    turned = at % 4 + at // 4 % 2 * 8 + at // 8 * 4
    return jnp.where(core == 0, at, turned)


def add_kernel(count, *refs):
    outs = refs[count:]
    each = outs[0].shape[0]
    for n, out_ref in enumerate(outs):
        part = pl.ds(n * each, each)
        total = refs[0][part].astype(F32)
        for ref in refs[1:count]:
            total = total + ref[part].astype(F32)
        out_ref[...] = total.astype(out_ref.dtype)


def add_split(arrays, pieces, dtype=BF16, **more):
    shape = arrays[0].shape
    out = like((shape[0] // pieces,) + shape[1:], dtype)
    kernel = lambda *refs: add_kernel(len(arrays), *refs)
    return list(call(kernel, [out] * pieces, arrays, **more))


def join_kernel(*refs):
    each = refs[0].shape[0]
    for n, ref in enumerate(refs[:-1]):
        refs[-1][n * each : (n + 1) * each] = ref[...]


def join(arrays, **more):
    shape = arrays[0].shape
    out = like((len(arrays) * shape[0],) + shape[1:], BF16)
    return list(call(join_kernel, [out], arrays, **more))


def sum_stages(keep, give, more):
    own = add_split([keep, send(give, CORE)], 2)
    yield own
    own = add_split([own[0], send(own[1], X, Y)], 2)
    yield own
    own = add_split([own[0], send(own[1], Y, X)], 4, **more.get("second", {}))
    yield own
    got = [send(g, to) for g, to in zip(own[1:], LINE)]
    own = add_split([own[0]] + got, 1, **more.get("line", {}))
    for bit in bits(lax.axis_size("seq"))[3:]:
        own = add_split([own[0], send(own[0], (0, bit))], 1) + own[1:]
    yield own
    got = [send(own[0], to) for to in LINE]
    quarter, *passed = join(own[:1] + got, **more.get("join", {}))
    yield [quarter, *passed]
    (half,) = join([quarter, send(quarter, Y, X)], **more.get("half", {}))
    yield [half]
    halves = [half, send(half, X, Y)]
    yield halves
    yield halves + [send(h, CORE) for h in halves]


def exchange(chunks):
    return lax.all_to_all(chunks, "seq", 0, 0, tiled=True)


def add(left, right):
    return (left.astype(F32) + right.astype(F32)).astype(BF16)


def sum_seq(part):
    for bit in bits(lax.axis_size("seq")):
        part = add(part, swap(part, "seq", bit))
    return part


def dot(left, right, left_dim=1, right_dim=0):
    return lax.dot_general(
        left, right, (((left_dim,), (right_dim,)), ((), ())), preferred_element_type=F32
    )


def whole(array):
    return pl.BlockSpec(array.shape, lambda *_: (0,) * array.ndim)


def nth(array, index):
    return pl.BlockSpec((1,) + array.shape[1:], lambda *_: (index,) + (0,) * (array.ndim - 1))


def call(
    kernel,
    outs,
    args,
    specs=None,
    scratch=(),
    flops=0,
    out_specs=None,
    grid=(1,),
    after=(),
    passing=(),
):
    specs = specs or [whole(a) for a in args]
    moved = sum(math.prod(o.shape) * o.dtype.itemsize for o in outs)
    moved += sum(math.prod(a.shape) * a.dtype.itemsize for a in args)
    count, made = len(args), len(outs)
    extra = [*passing, *after]
    skip, pas = len(extra), len(passing)
    anywhere = pl.BlockSpec(memory_space=pl.ANY)
    return pl.pallas_call(
        lambda *refs: kernel(
            *refs[:count],
            *refs[count + skip : count + skip + made],
            *refs[count + skip + made + pas :],
        ),
        out_shape=list(outs) + [like(p.shape, p.dtype) for p in passing],
        grid=grid,
        in_specs=list(specs) + [anywhere] * skip,
        out_specs=list(out_specs or [whole(o) for o in outs]) + [anywhere] * pas,
        scratch_shapes=list(scratch),
        input_output_aliases={count + k: made + k for k in range(pas)},
        compiler_params=pltpu.CompilerParams(vmem_limit_bytes=VMEM_BYTES),
        cost_estimate=pl.CostEstimate(
            flops=int(flops * COST), bytes_accessed=int(moved * COST), transcendentals=0
        ),
    )(*args, *extra)


SCALAR = pl.BlockSpec(memory_space=pltpu.SMEM)


def like(shape, dtype):
    return jax.ShapeDtypeStruct(shape, dtype)


def lay(buffer, value):
    for c in range(buffer.shape[0]):
        buffer[c] = value[:, c * 128 : (c + 1) * 128]


def lift(buffer):
    return jnp.concatenate([buffer[c] for c in range(buffer.shape[0])], axis=1)


def pick(buffer, t, count):
    return jnp.concatenate(
        [buffer[c, pl.ds(t, count, stride=BLOCK), :] for c in range(buffer.shape[0])], axis=1
    )


def strew(buffer, t, rows):
    for c in range(buffer.shape[0]):
        buffer[c, pl.ds(t, rows.shape[0], stride=BLOCK), :] = rows[:, c * 128 : (c + 1) * 128]


def chunk_shape(parts, blocks, width):
    row_parts = min(parts, BLOCK)
    return (parts, BLOCK // row_parts, blocks, width * row_parts // parts)


def chunk_places(shape, t):
    per = BLOCK // shape[1]
    cols = shape[0] // per
    return [(t // shape[1]) * cols + f for f in range(cols)], t % shape[1]


def store_row(ref, t, rows, shape=None):
    parts, place = chunk_places(shape or ref.shape, t)
    for f, part in enumerate(parts):
        ref[part, place] = rows[:, f * ref.shape[3] : (f + 1) * ref.shape[3]]


def load_row(ref, t):
    parts, place = chunk_places(ref.shape, t)
    return jnp.concatenate([ref[part, place] for part in parts], axis=1)


def row_buffer(span, width):
    return pltpu.VMEM((width // 128, span, 128), F32)


def enter_kernel(x_ref, gain_ref, flag_ref, hidden_ref, *refs):
    rows_refs, buffer = refs[:-1], refs[-1]
    seqs = len(rows_refs)
    parts, _, blocks, cols = rows_refs[0].shape
    width = hidden_ref.shape[2]
    each = width // cols
    shape = chunk_shape(parts, blocks, width)
    for s in range(seqs):
        x = x_ref[s].astype(F32)
        scale = lax.rsqrt(jnp.mean(x * x, axis=-1, keepdims=True) + EPS)
        hidden = (x * scale * gain_ref[...]).astype(BF16)
        hidden_ref[s] = hidden
        lay(buffer, hidden.astype(F32))
        total = None
        for t in range(BLOCK):
            rows = pick(buffer, t, blocks)
            store_row(rows_refs[s], t, rows.astype(BF16), shape)
            total = rows if total is None else total + rows
        low = (total * (1.0 / BLOCK)).astype(BF16)
        for part in range(parts):
            for f in range(each):
                rows_refs[0][part, shape[1] + s * each + f] = low[:, f * cols : (f + 1) * cols]
    for part in range(parts):
        rows_refs[0][part, shape[1] + seqs * each] = flag_ref[...]


def enter(inputs, gain, real, parts):
    seqs, span, width = inputs.shape
    blocks = span // BLOCK
    p, r, n, w = chunk_shape(parts, blocks, width)
    flags = jnp.repeat(real.astype(BF16).T, w // seqs, axis=1)
    more = seqs * (width // w) + 1
    return call(
        enter_kernel,
        [like(inputs.shape, BF16)]
        + [like((p, r + (more if s == 0 else 0), n, w), BF16) for s in range(seqs)],
        [inputs, gain, flags],
        scratch=[row_buffer(span, width)],
    )


def told_of(first, seqs, width):
    parts, _, blocks, cols = first.shape
    shape = chunk_shape(parts, blocks, width)
    each = width // cols
    told = first[:, shape[1] :]
    told = told.transpose(1, 0, 2, 3).reshape(told.shape[1], parts * blocks, cols)
    flags = told[-1][:, :: cols // seqs].T
    told = told[:-1].reshape(seqs, each, parts * blocks, cols).transpose(0, 2, 1, 3)
    return told.reshape(seqs, parts * blocks, width), flags


def told_summary(first_ref, s):
    parts, rows, blocks, width = first_ref.shape
    row = chunk_shape(parts, blocks, width)[1] + s
    return first_ref[:, row].reshape(parts * blocks, width)


def told_flags(first_ref, seqs, s):
    parts, rows, blocks, width = first_ref.shape
    flags = first_ref[:, rows - 1, :, s * (width // seqs) : s * (width // seqs) + 128]
    return flags.reshape(parts * blocks, 128).astype(F32)


def plan_kernel(sort_scale, told_ref, w_ref, proj_ref, steps_ref, plan_ref, low_ref, entropy_ref, count_ref):
    seqs = plan_ref.shape[0]
    plans, reals = [], []
    entropy = jnp.zeros((), F32)
    for s in range(seqs):
        summary = told_summary(told_ref, s)
        flags = told_flags(told_ref, seqs, s)
        real = flags.T > 0.5
        proj = dot(summary, w_ref[...]).astype(BF16)
        proj_ref[s] = proj
        plans.append(jnp.where(real, sort_scale * dot(proj, summary, 1, 1), NEG))
        reals.append(real)
    for step in range(2 * ITERS):
        axis = 1 - step % 2
        for s in range(seqs):
            peak = jnp.max(plans[s], axis=axis, keepdims=True)
            share = jnp.exp(plans[s] - peak)
            total = jnp.sum(share, axis=axis, keepdims=True)
            fall = peak + jnp.log(total)
            share = share * (1.0 / total)
            if axis == 0:
                fall = jnp.where(reals[s][:1], fall, 0.0)
                share = jnp.where(reals[s], share, 0.0)
            plans[s] = plans[s] - fall
            steps_ref[step, s] = share
    for s in range(seqs):
        flags = told_flags(told_ref, seqs, s)[:, :1]
        prob = jnp.exp(plans[s])
        plan_ref[s] = plans[s]
        low_ref[s] = prob.astype(BF16)
        entropy = entropy + jnp.sum(jnp.where(flags > 0.5, prob * plans[s], 0.0))
    entropy_ref[...] = jnp.full(entropy_ref.shape, entropy, F32)
    blocks = [jnp.sum(told_flags(told_ref, seqs, s), axis=0, keepdims=True) for s in range(seqs)]
    count_ref[...] = jnp.broadcast_to(sum(blocks), count_ref.shape)


def plan_back_kernel(
    sort_scale,
    count_ref,
    place_ref,
    heard_ref,
    told_ref,
    w_ref,
    proj_ref,
    steps_ref,
    plan_ref,
    split_ref,
    d_summary_ref,
    keep_ref,
    give_ref,
    buffer,
    whole_grad,
):
    place = place_ref[0, 0]
    seqs = plan_ref.shape[0]
    blocks = told_ref.shape[2]
    part = 1.0 / count_ref[:1]
    grads = []
    for s in range(seqs):
        flags = told_flags(told_ref, seqs, s)[:, :1]
        plan = plan_ref[s]
        prob = jnp.exp(plan)
        d_prob = heard_ref[s].astype(F32)
        grads.append(prob * d_prob - jnp.where(flags > 0.5, prob * plan + prob, 0.0) * part)
    for step in reversed(range(2 * ITERS)):
        for s in range(seqs):
            total = jnp.sum(grads[s], axis=1 - step % 2, keepdims=True)
            grads[s] = grads[s] - steps_ref[step, s] * total
    grad_sort = None
    for s in range(seqs):
        summary = told_summary(told_ref, s)
        flags = told_flags(told_ref, seqs, s)
        real = flags.T > 0.5
        d_logits = jnp.where(real, grads[s], 0.0)
        low = d_logits.astype(BF16)
        d_proj = (sort_scale * dot(low, summary)).astype(BF16)
        turned = low.astype(F32).T.astype(BF16)
        buffer[...] = sort_scale * dot(turned, proj_ref[s]) + dot(d_proj, w_ref[...], 1, 1)
        first = pl.multiple_of(place * blocks, blocks)
        d_summary_ref[s] = buffer[pl.ds(first, blocks), :]
        here = dot(summary, d_proj, 0, 0)
        grad_sort = here if grad_sort is None else grad_sort + here
    half = keep_ref.shape[0]
    whole_grad[...] = grad_sort
    keep_ref[...] = whole_grad[pl.ds(pl.multiple_of(split_ref[0] * half, half), half)].astype(BF16)
    give_ref[...] = whole_grad[
        pl.ds(pl.multiple_of((1 - split_ref[0]) * half, half), half)
    ].astype(BF16)


def spread_row(ref, t):
    parts, rows, blocks, width = ref.shape
    return ref[:, t].reshape(parts * blocks, width)


def mix_kernel(low_ref, spread_ref, mixed_ref):
    parts, rows, blocks, width = mixed_ref.shape
    for t in range(rows):
        mixed = dot(low_ref[0], spread_row(spread_ref, t)).astype(BF16)
        mixed_ref[:, t] = mixed.reshape(parts, blocks, width)


def mix(low, spread, index, width, after=()):
    shape = chunk_shape(spread.shape[0], spread.shape[2], width)
    specs = [nth(low, index), whole(spread)]
    return call(mix_kernel, [like(shape, BF16)], [low, spread], specs, after=after)[0]


def unmix_kernel(low_ref, *refs):
    seqs = low_ref.shape[0]
    spread_refs, d_mixed_refs = refs[:seqs], refs[seqs : 2 * seqs]
    d_spread_ref, d_prob_ref = refs[2 * seqs :]
    parts, rows, blocks, width = d_mixed_refs[0].shape
    for s in range(seqs):
        turned = low_ref[s].astype(F32).T.astype(BF16)
        d_prob = None
        for t in range(rows):
            grad = spread_row(d_mixed_refs[s], t)
            here = dot(grad, spread_row(spread_refs[s], t), 1, 1)
            d_prob = here if d_prob is None else d_prob + here
            back = dot(turned, grad).astype(BF16)
            d_spread_ref[:, s * rows + t] = back.reshape(parts, blocks, width)
        d_prob_ref[s] = d_prob.astype(BF16)


def unmix(low, spread, d_mixed, after=()):
    p, r, n, w = d_mixed[0].shape
    seqs = low.shape[0]
    return call(
        unmix_kernel,
        [like((p, seqs * r, n, w), BF16), like(low.shape, BF16)],
        [low, *spread, *d_mixed],
        after=after,
    )


def block_masks():
    lane = lax.broadcasted_iota(jnp.int32, (BLOCK, 2 * GROUP), 1)
    owner = (lane % GROUP) // BLOCK
    return [owner == b for b in range(GROUP // BLOCK)]


def narrow(full, masks, start):
    out = full[start : start + BLOCK]
    for b in range(1, len(masks)):
        out = jnp.where(masks[b], full[start + b * BLOCK : start + (b + 1) * BLOCK], out)
    return out


def widen(first, second, masks):
    zero = jnp.zeros_like(first)
    return jnp.concatenate(
        [jnp.where(m, first, zero) for m in masks] + [jnp.where(m, second, zero) for m in masks],
        axis=0,
    ).astype(BF16)


def two_heads_lanes(rows):
    lane = lax.broadcasted_iota(jnp.int32, rows.shape, 1)
    low = lane < rows.shape[1] // 2
    zero = jnp.zeros_like(rows)
    return jnp.concatenate([jnp.where(low, rows, zero), jnp.where(low, zero, rows)], axis=0)


def two_heads_rows(columns):
    row = lax.broadcasted_iota(jnp.int32, columns.shape, 0)
    low = row < columns.shape[0] // 2
    zero = jnp.zeros_like(columns)
    return jnp.concatenate([jnp.where(low, columns, zero), jnp.where(low, zero, columns)], axis=1)


def own_heads(full):
    half = full.shape[1] // 2
    row = lax.broadcasted_iota(jnp.int32, (full.shape[0], half), 0)
    return jnp.where(row < full.shape[0] // 2, full[:, :half], full[:, half:])


def turn(array):
    return array.astype(F32).T.astype(BF16)


def project_kernel(hidden_ref, wq_ref, wk_ref, wv_ref, q_ref, k_ref, v_ref, qt_ref, kt_ref, vt_ref):
    hidden = hidden_ref[0]
    for w_ref, flat_ref, turned_ref in (
        (wq_ref, q_ref, qt_ref),
        (wk_ref, k_ref, kt_ref),
        (wv_ref, v_ref, vt_ref),
    ):
        full = dot(hidden, w_ref[...])
        flat_ref[0] = full.astype(BF16)
        turned_ref[0] = full.T.astype(BF16)


def project(hidden, wq, wk, wv):
    seqs, span, width = hidden.shape
    flat = pl.BlockSpec((1, span, width), lambda s: (s, 0, 0))
    turned = pl.BlockSpec((1, width, span), lambda s: (s, 0, 0))
    return call(
        project_kernel,
        [like((seqs, span, width), BF16)] * 3 + [like((seqs, width, span), BF16)] * 3,
        [hidden, wq, wk, wv],
        [flat] + [whole(wq)] * 3,
        flops=6 * seqs * span * width * width,
        grid=(seqs,),
        out_specs=[flat] * 3 + [turned] * 3,
    )


def attend_kernel(
    att_scale,
    rows_ref,
    allowed_ref,
    wk_ref,
    wv_ref,
    k_ref,
    qt_ref,
    vt_ref,
    att_ref,
    mixed_ref,
    vs_ref,
    kst_ref,
    weights_ref,
    buffer,
    ks,
    vst,
):
    span, width = mixed_ref.shape
    for t in range(BLOCK):
        strew(buffer, t, load_row(rows_ref, t).astype(F32))
    mixed_ref[...] = lift(buffer).astype(BF16)
    mixed = mixed_ref[...]
    full = dot(mixed, wk_ref[...])
    ks[...] = full.astype(BF16)
    kst_ref[...] = full.T.astype(BF16)
    full = dot(mixed, wv_ref[...])
    vs_ref[...] = full.astype(BF16)
    vst[...] = full.T.astype(BF16)
    masks = block_masks()
    pairs = HEADS // 2

    def group(g, carry):
        rows = pl.ds(pl.multiple_of(g * GROUP, GROUP), GROUP)
        allowed = allowed_ref[0, :, rows]
        allowed = jnp.concatenate([allowed, allowed], axis=1) > 0.5
        for p in range(pairs):
            lanes = pl.ds(p * GROUP, GROUP)
            keys = jnp.concatenate([k_ref[0, rows, lanes], ks[rows, lanes]], axis=0)
            scores = dot(keys, two_heads_rows(qt_ref[0, lanes, rows]))
            near = jnp.where(allowed, narrow(scores, masks, 0) * att_scale, NEG)
            far = narrow(scores, masks, GROUP) * att_scale
            peak = jnp.maximum(
                jnp.max(near, axis=0, keepdims=True), jnp.max(far, axis=0, keepdims=True)
            )
            near = jnp.exp(near - peak)
            far = jnp.exp(far - peak)
            total = jnp.sum(near, axis=0, keepdims=True) + jnp.sum(far, axis=0, keepdims=True)
            part = 1.0 / total
            near = near * part
            far = far * part
            weights_ref[g * pairs + p, :BLOCK] = near
            weights_ref[g * pairs + p, BLOCK:] = far
            values = jnp.concatenate([vt_ref[0, lanes, rows], vst[lanes, rows]], axis=1)
            out = own_heads(dot(values, widen(near, far, masks)))
            att_ref[rows, lanes] = out.T.astype(BF16)
        return carry

    lax.fori_loop(0, span // GROUP, group, 0)


def attend(rows, allowed, wk, wv, k, qt, vt, index):
    seqs, span, width = k.shape
    units = span // GROUP * (HEADS // 2)
    flat = like((span, width), BF16)
    args = [rows, allowed, wk, wv, k, qt, vt]
    return call(
        lambda *refs: attend_kernel(1.0 / math.sqrt(width // HEADS), *refs),
        [flat] * 3 + [like((width, span), BF16), like((units, 2 * BLOCK, 2 * GROUP), F32)],
        args,
        [whole(rows), nth(allowed, index), whole(wk), whole(wv)]
        + [nth(a, index) for a in (k, qt, vt)],
        [row_buffer(span, width), pltpu.VMEM((span, width), BF16), pltpu.VMEM((width, span), BF16)],
        flops=8 * span * width * width,
    )


def attend_back_kernel(
    att_scale,
    d_att_ref,
    q_ref,
    v_ref,
    kt_ref,
    vs_ref,
    kst_ref,
    weights_ref,
    wk_ref,
    wv_ref,
    d_rows_ref,
    dq,
    dk,
    dv,
    dks,
    dvs,
    buffer,
    datt_t,
):
    span, width = vs_ref.shape
    datt_t[...] = turn(d_att_ref[0])
    masks = block_masks()
    pairs = HEADS // 2

    def group(g, carry):
        rows = pl.ds(pl.multiple_of(g * GROUP, GROUP), GROUP)
        for p in range(pairs):
            lanes = pl.ds(p * GROUP, GROUP)
            values = jnp.concatenate([v_ref[0, rows, lanes], vs_ref[rows, lanes]], axis=0)
            d_weights = dot(values, two_heads_rows(datt_t[lanes, rows]))
            near = weights_ref[g * pairs + p, :BLOCK]
            far = weights_ref[g * pairs + p, BLOCK:]
            d_near = near * narrow(d_weights, masks, 0)
            d_far = far * narrow(d_weights, masks, GROUP)
            total = jnp.sum(d_near, axis=0, keepdims=True) + jnp.sum(d_far, axis=0, keepdims=True)
            d_near = d_near - near * total
            d_far = d_far - far * total
            d_scores = widen(d_near, d_far, masks)
            keys = jnp.concatenate([kt_ref[0, lanes, rows], kst_ref[lanes, rows]], axis=1)
            dq[rows, lanes] = (own_heads(dot(keys, d_scores)).T * att_scale).astype(BF16)
            d_keys = (dot(d_scores, two_heads_lanes(q_ref[0, rows, lanes])) * att_scale).astype(BF16)
            dk[rows, lanes] = d_keys[:GROUP]
            dks[rows, lanes] = d_keys[GROUP:]
            d_values = dot(
                widen(near, far, masks), two_heads_lanes(d_att_ref[0, rows, lanes])
            ).astype(BF16)
            dv[rows, lanes] = d_values[:GROUP]
            dvs[rows, lanes] = d_values[GROUP:]
        return carry

    lax.fori_loop(0, span // GROUP, group, 0)
    lay(buffer, dot(dks[...], wk_ref[...], 1, 1) + dot(dvs[...], wv_ref[...], 1, 1))
    for t in range(BLOCK):
        store_row(d_rows_ref, t, pick(buffer, t, d_rows_ref.shape[2]).astype(BF16))


def attend_back(d_att, q, v, kt, kept, wk, wv, shape, index, after=()):
    seqs, span, width = q.shape
    args = [d_att, q, v, kt, *kept, wk, wv]
    flat = like((span, width), BF16)
    return call(
        lambda *refs: attend_back_kernel(1.0 / math.sqrt(width // HEADS), *refs),
        [like(shape, BF16)] + [flat] * 5,
        args,
        [nth(a, index) for a in args[:4]]
        + [whole(a) for a in args[4:]],
        [row_buffer(span, width), pltpu.VMEM((width, span), BF16)],
        flops=12 * span * width * width,
        after=after,
    )


def late_kernel(split_ref, hidden_ref, gwo_ref, *refs):
    keep_ref, give_ref, buffer = refs[-3:]
    seqs, span, width = hidden_ref.shape
    core, place = split_ref[0], split_ref[1]
    per = len(refs[:-3]) // seqs
    totals = [None, None, None]
    for s in range(seqs):
        mixed_ref, dq, dk, dv, dks, dvs = refs[s * per : (s + 1) * per]
        hidden_t = turn(hidden_ref[s])
        mixed_t = turn(mixed_ref[...])
        here = (
            dot(hidden_t, dq[...]),
            dot(hidden_t, dk[...]) + dot(mixed_t, dks[...]),
            dot(hidden_t, dv[...]) + dot(mixed_t, dvs[...]),
        )
        totals = [h if t is None else t + h for t, h in zip(totals, here)]
    for n in range(3):
        buffer[n] = totals[n]
    buffer[3] = gwo_ref[...].astype(F32)
    blocks, rows = keep_ref.shape[0], keep_ref.shape[1] // 4
    for side, ref in ((core, keep_ref), (1 - core, give_ref)):
        for j in range(blocks):
            part = pl.ds(pl.multiple_of((side * blocks + j) * rows, rows), rows)
            at = spot(j, place, side)
            for n in range(4):
                ref[at, n * rows : (n + 1) * rows] = buffer[n, part].astype(BF16)


def late(split, hidden, gwo, parts, after=()):
    seqs, span, width = hidden.shape
    args = [split, hidden, gwo, *[a for part in parts for a in part]]
    shape = like((16, 4 * width // 32, width), BF16)
    return call(
        late_kernel,
        [shape, shape],
        args,
        [SCALAR] + [whole(a) for a in args[1:]],
        [pltpu.VMEM((4, width, width), F32)],
        flops=10 * seqs * span * width * width,
        after=after,
    )


def end_blocks(split_ref, refs):
    each = refs[0].shape[0]
    for n, ref in enumerate(refs):
        core = split_ref[0] if n < 2 else 1 - split_ref[0]
        for r in range(each):
            index = core * 16 + spot(0, n % 2 * each + r, core)
            yield ref[r], index ^ (split_ref[1] % 16)


def late_end_kernel(split_ref, *refs):
    outs = refs[-4:]
    rows = refs[0].shape[1] // 4
    for block, index in end_blocks(split_ref, refs[:-4]):
        part = pl.ds(pl.multiple_of(index * rows, rows), rows)
        for n, out_ref in enumerate(outs):
            out_ref[part] = block[n * rows : (n + 1) * rows].astype(F32)


def late_end(split, parts, after=()):
    width = parts[0].shape[2]
    return call(
        late_end_kernel,
        [like((width, width), F32)] * 4,
        [split, *parts],
        [SCALAR] + [whole(p) for p in parts],
        after=after,
    )


def d_hidden_kernel(wq_ref, wk_ref, wv_ref, *refs):
    out_ref = refs[-1]
    for s in range(out_ref.shape[0]):
        dq, dk, dv = refs[3 * s : 3 * s + 3]
        out_ref[s] = (
            dot(dq[...], wq_ref[...], 1, 1)
            + dot(dk[...], wk_ref[...], 1, 1)
            + dot(dv[...], wv_ref[...], 1, 1)
        )


def d_hidden_of(wq, wk, wv, parts, after=()):
    args = [wq, wk, wv] + [a for part in parts for a in part]
    shape = (len(parts),) + parts[0][0].shape
    flops = 6 * shape[0] * shape[1] * shape[2] ** 2
    return call(d_hidden_kernel, [like(shape, F32)], args, flops=flops, after=after)[0]


def feed_kernel(
    seqs,
    split_ref,
    x_ref,
    cot_ref,
    gain_ref,
    wo_ref,
    win_ref,
    wout_ref,
    *refs,
):
    att_refs = refs[:seqs]
    (
        out_ref,
        keep_ref,
        give_ref,
        gwo_ref,
        d_resid_ref,
        d_att_ref,
        slope_ref,
        y1,
        unit,
        h2,
        h2t,
        d_h2,
        f_all,
        du_all,
        scales,
    ) = refs[seqs:]
    step = pl.program_id(0)
    span = x_ref.shape[0]
    tile = 512
    tiles = [pl.ds(r, tile) for r in range(0, span, tile)]

    def att_tile(rows):
        each = att_refs[0].shape[0]
        return att_refs[rows.start // each][pl.ds(rows.start % each, tile)]

    @pl.when(step == 0)
    def _():
        for rows in tiles:
            y = x_ref[rows].astype(F32) + dot(att_tile(rows), wo_ref[...])
            y1[rows] = y
            scale = lax.rsqrt(jnp.mean(y * y, axis=-1, keepdims=True) + EPS)
            n = y * scale
            unit[rows] = n
            scales[rows] = jnp.broadcast_to(scale, (tile, scales.shape[1]))
            low = (n * gain_ref[...]).astype(BF16)
            h2[rows] = low
            h2t[:, rows] = turn(low)
            d_h2[rows] = jnp.zeros((tile, d_h2.shape[1]), F32)

    root = math.sqrt(2.0 / math.pi)
    for rows in tiles:
        u = dot(h2[rows], win_ref[...])
        square = u * u
        bend = jnp.tanh(root * u * (1.0 + 0.044715 * square))
        half = 0.5 + 0.5 * bend
        f = (u * half).astype(BF16)
        slope = half + (0.5 * root) * u * (1.0 - bend * bend) * (1.0 + 0.134145 * square)
        du = (dot(cot_ref[rows], wout_ref[...], 1, 1) * slope).astype(BF16)
        y1[rows] = y1[rows] + dot(f, wout_ref[...])
        d_h2[rows] = d_h2[rows] + dot(du, win_ref[...], 1, 1)
        f_all[:, rows] = turn(f)
        du_all[rows] = du
    grads = (
        dot(f_all[...], cot_ref[...]).astype(BF16),
        dot(h2t[...], du_all[...]).astype(BF16),
    )
    blocks, block = keep_ref.shape[0], keep_ref.shape[1] // 2
    count = grads[0].shape[0] // block
    for first, ref in ((0, give_ref), (2, keep_ref)):

        @pl.when(step // 2 * 2 == first)
        def _():
            for j in range(count):
                core = split_ref[0] if first else 1 - split_ref[0]
                at = spot((step % 2) * count + j, split_ref[1], core)
                for n in range(2):
                    ref[at, n * block : (n + 1) * block] = grads[n][j * block : (j + 1) * block]


    @pl.when(step == pl.num_programs(0) - 1)
    def _():
        total = None
        grad = None
        for rows in tiles:
            out_ref[rows] = y1[rows].astype(BF16)
            up, n = d_h2[rows], unit[rows]
            here = jnp.sum(up * n, axis=0, keepdims=True)
            total = here if total is None else total + here
            d_n = up * gain_ref[...]
            d_y = scales[rows][:, :1] * (d_n - n * jnp.mean(d_n * n, axis=-1, keepdims=True))
            d_y = d_y + cot_ref[rows].astype(F32)
            low = d_y.astype(BF16)
            d_resid_ref[rows] = low
            d_att_ref[rows] = dot(low, wo_ref[...], 1, 1).astype(BF16)
            du_all[rows] = low
            f_all[:, rows] = turn(att_tile(rows))
        gwo_ref[...] = dot(f_all[...], du_all[...]).astype(BF16)
        slope_ref[...] = jnp.broadcast_to(total, slope_ref.shape)


def feed(split, x, att, cot, gain, wo, win, wout):
    span, width = x.shape
    hidden = win.shape[1]
    steps = hidden // width
    flat = lambda dtype: like((span, width), dtype)
    parts = like((16, 2 * hidden // 32, width), BF16)
    outs = [
        flat(BF16),
        parts,
        parts,
        like((width, width), BF16),
        flat(BF16),
        flat(BF16),
        like((8, width), F32),
    ]

    def chunk(c, split_ref):
        return ((1 - c // 2) ^ split_ref[0]) * 2 + c % 2

    return pl.pallas_call(
        lambda *refs: feed_kernel(len(att), *refs),
        grid_spec=pltpu.PrefetchScalarGridSpec(
            num_scalar_prefetch=1,
            grid=(steps,),
            in_specs=[whole(a) for a in (x, cot, gain, wo)]
            + [
                pl.BlockSpec((width, width), lambda c, r: (0, chunk(c, r))),
                pl.BlockSpec((width, width), lambda c, r: (chunk(c, r), 0)),
            ]
            + [whole(a) for a in att],
            out_specs=[whole(o) for o in outs],
            scratch_shapes=[
                pltpu.VMEM((span, width), F32),
                pltpu.VMEM((span, width), F32),
                pltpu.VMEM((span, width), BF16),
                pltpu.VMEM((width, span), BF16),
                pltpu.VMEM((span, width), F32),
                pltpu.VMEM((width, span), BF16),
                pltpu.VMEM((span, width), BF16),
                pltpu.VMEM((span, 128), F32),
            ],
        ),
        out_shape=outs,
        compiler_params=pltpu.CompilerParams(vmem_limit_bytes=VMEM_BYTES),
        cost_estimate=pl.CostEstimate(
            flops=int(COST * 12 * span * width * hidden),
            bytes_accessed=int(COST * (24 << 20)),
            transcendentals=0,
        ),
    )(split, x, cot, gain, wo, win, wout, *att)


def feed_end_kernel(split_ref, *refs):
    gout_ref, gin_ref = refs[-2:]
    width = gout_ref.shape[1]
    rows = refs[0].shape[1] // 2
    per = width // rows
    for block, index in end_blocks(split_ref, refs[:-2]):
        gout_ref[pl.ds(pl.multiple_of(index * rows, rows), rows)] = block[:rows].astype(F32)
        part = pl.ds(pl.multiple_of(index % per * rows, rows), rows)
        lanes = pl.ds(pl.multiple_of(index // per * width, width), width)
        gin_ref[part, lanes] = block[rows:].astype(F32)


def feed_end(split, parts):
    width = parts[0].shape[2]
    hidden = 16 * parts[0].shape[1]
    return call(
        feed_end_kernel,
        [like((hidden, width), F32), like((width, hidden), F32)],
        [split, *parts],
        [SCALAR] + [whole(p) for p in parts],
    )


def leave_kernel(
    x_ref, gain_ref, d_hidden_ref, rows_ref, d_summary_ref, d_resid_ref, out_ref, total_ref, buffer
):
    d_summary = d_summary_ref[0] * (1.0 / BLOCK)
    for t in range(BLOCK):
        strew(buffer, t, load_row(rows_ref, t).astype(F32) + d_summary)
    x = x_ref[0].astype(F32)
    scale = lax.rsqrt(jnp.mean(x * x, axis=-1, keepdims=True) + EPS)
    n = x * scale
    up = d_hidden_ref[0] + lift(buffer)
    total_ref[0] = jnp.broadcast_to(jnp.sum(up * n, axis=0, keepdims=True), total_ref.shape[1:])
    d_n = up * gain_ref[...]
    d_x = scale * (d_n - n * jnp.mean(d_n * n, axis=-1, keepdims=True))
    out_ref[0] = (d_x + d_resid_ref[0].astype(F32)).astype(BF16)


def leave(inputs, gain, d_hidden, rows, d_summary, d_resid, after=()):
    seqs, span, width = inputs.shape
    p, r, n, w = rows.shape
    args = [inputs, gain, d_hidden, rows, d_summary, d_resid]
    each = lambda a: pl.BlockSpec((1,) + a.shape[1:], lambda s: (s, 0, 0))
    outs = [like(inputs.shape, BF16), like((seqs, 8, width), F32)]
    return call(
        leave_kernel,
        outs,
        args,
        [
            each(inputs),
            whole(gain),
            each(d_hidden),
            pl.BlockSpec((p, r // seqs, n, w), lambda s: (0, s, 0, 0)),
            each(d_summary),
            each(d_resid),
        ],
        [row_buffer(span, width)],
        grid=(seqs,),
        out_specs=[each(o) for o in outs],
        after=after,
    )


def sort_end_kernel(split_ref, half_ref, other_ref, out_ref):
    half = half_ref.shape[0]
    for core, ref in ((split_ref[0], half_ref), (1 - split_ref[0], other_ref)):
        out_ref[pl.ds(pl.multiple_of(core * half, half), half)] = ref[...].astype(F32)


def plan_plain(sort_scale, summary_all, real, w_sort):
    def plan_of(logits):
        plan = jnp.where(real, logits, NEG)
        for _ in range(ITERS):
            plan = plan - jax.nn.logsumexp(plan, axis=2, keepdims=True)
            fall = jax.nn.logsumexp(plan, axis=1, keepdims=True)
            plan = plan - jnp.where(real, fall, 0.0)
        return plan

    proj = lax.dot_general(
        summary_all, w_sort, (((2,), (0,)), ((), ())), preferred_element_type=F32
    ).astype(BF16)
    logits = sort_scale * jnp.einsum("sid,sjd->sij", proj, summary_all, preferred_element_type=F32)
    plan, back = jax.vjp(plan_of, logits)
    return proj, plan, back


def places():
    dp, seq = lax.axis_index("dp"), lax.axis_index("seq")
    core, x, y = dp % 2, (dp // 2) % 2, seq % 2
    line = (seq // 2) % 2 * 2 + (seq // 4) % 2
    return jnp.stack([core, core * 16 + x * 8 + y * 4 + line]).astype(jnp.int32)


def body(
    inputs,
    segment_ids,
    real_block,
    gain_attn,
    w_query,
    w_key,
    w_value,
    w_output,
    w_sort,
    gain_ffn,
    w_in,
    w_out,
    cotangent,
):
    seqs, span, width = inputs.shape
    blocks = span // BLOCK
    seq_size, dp_size = lax.axis_size("seq"), lax.axis_size("dp")
    count = blocks * seq_size
    small_plan = count == 128
    sort_scale = SORT_GAIN * BLOCK / math.sqrt(width)
    gain_one = gain_attn.astype(F32).reshape(1, width)
    gain_two = gain_ffn.astype(F32).reshape(1, width)
    place = lax.axis_index("seq")
    first_block = place * blocks
    place = place.astype(jnp.int32).reshape(1, 1)
    split = places()

    segments = segment_ids.reshape(seqs, blocks, BLOCK)
    allowed = (segments.transpose(0, 2, 1)[:, :, :, None] == segments[:, None]).astype(F32)
    allowed = allowed.reshape(seqs, BLOCK, span)


    hidden, *rows = enter(inputs, gain_one, real_block, seq_size)
    spread = [exchange(r) for r in rows]
    q, k, v, qt, kt, vt = project(hidden, w_query, w_key, w_value)

    if small_plan:
        proj, steps, plan, low, entropy, total_blocks = call(
            lambda *refs: plan_kernel(sort_scale, *refs),
            [
                like((seqs, count, width), BF16),
                like((2 * ITERS, seqs, count, count), F32),
                like((seqs, count, count), F32),
                like((seqs, count, count), BF16),
                like((8, 128), F32),
                like((8, 128), F32),
            ],
            [spread[0], w_sort],
            after=(q,),
        )
        entropy = entropy[0, 0]
    else:
        summary_all, reals = told_of(spread[0], seqs, width)
        real = reals[:, None, :] == 1
        proj, plan, plan_back = plan_plain(sort_scale, summary_all, real, w_sort)
        prob = jnp.exp(plan)
        low = prob.astype(BF16)
        entropy = jnp.sum(jnp.where(reals[:, :, None] == 1, prob * plan, 0.0))
        total_blocks = jnp.full((8, 128), jnp.sum(reals.astype(F32)))
    for bit in bits(dp_size):
        total_blocks = total_blocks + swap(total_blocks, "dp", bit)

    att, kept = [], []
    for s in range(seqs):
        part = mix(low, spread[s], s, width, [allowed, split, gain_two, total_blocks] if s else ())
        here, *rest = attend(exchange(part), allowed, w_key, w_value, k, qt, vt, s)
        att.append(here)
        kept.append(rest)

    flat = (seqs * span, width)
    output, keep, give, grad_output, d_resid, d_att, slope = feed(
        split,
        inputs.reshape(flat),
        att,
        cotangent.reshape(flat),
        gain_two,
        w_output,
        w_in,
        w_out,
    )
    d_resid = d_resid.reshape(inputs.shape)
    d_att = d_att.reshape(inputs.shape)
    more = {}
    stages = sum_stages(keep, give, more)
    summed = next(stages)
    grads, d_mixed = [], []
    chunks = chunk_shape(seq_size, blocks, width)
    for s in range(seqs):
        after = summed[:1] if s else ()
        sent, *here = attend_back(d_att, q, v, kt, kept[s][1:], w_key, w_value, chunks, s, after)
        grads.append(here)
        d_mixed.append(exchange(sent))
    parts = late(
        split, hidden, grad_output, [[kept[s][0], *grads[s]] for s in range(seqs)]
    )
    plane = next(stages)
    d_hidden = d_hidden_of(w_query, w_key, w_value, [g[:3] for g in grads])
    late_more = {}
    late_stages = sum_stages(*parts, late_more)
    d_rows, d_prob = unmix(low, spread, d_mixed, plane[:1])
    heard = sum_seq(d_prob)
    more["line"] = dict(passing=[d_rows])
    next(stages)
    _, d_rows = next(stages)
    d_rows = exchange(d_rows)
    *_, last = stages
    grad_out, grad_in = feed_end(split, last)
    next(late_stages)
    late2 = next(late_stages)

    if small_plan:
        args = [
            total_blocks,
            place,
            heard,
            spread[0],
            w_sort,
            proj,
            steps,
            plan,
        ]
        half = like((width // 2, width), BF16)
        outs = [like((seqs, blocks, width), F32), half, half]
        d_summary, sort_keep, sort_give = call(
            lambda *refs: plan_back_kernel(sort_scale, *refs),
            outs,
            args + [split],
            [whole(total_blocks), SCALAR] + [whole(a) for a in args[2:]] + [SCALAR],
            [pltpu.VMEM((count, width), F32), pltpu.VMEM((width, width), F32)],
            after=[late2[0], d_hidden],
        )
    else:
        d_prob = heard.astype(F32)
        d_plan = prob * d_prob - (
            jnp.where(reals[:, :, None] == 1, prob * plan + prob, 0.0) / total_blocks[0, 0]
        )
        (d_logits,) = plan_back(d_plan)
        d_logits = d_logits.astype(BF16)
        d_proj = sort_scale * jnp.einsum(
            "sij,sjd->sid", d_logits, summary_all, preferred_element_type=F32
        )
        d_proj = d_proj.astype(BF16)
        grad_sort = jnp.einsum("sid,sie->de", summary_all, d_proj, preferred_element_type=F32)
        d_summary = sort_scale * jnp.einsum(
            "sij,sid->sjd", d_logits, proj, preferred_element_type=F32
        ) + jnp.einsum("sie,de->sid", d_proj, w_sort, preferred_element_type=F32)
        d_summary = lax.dynamic_slice_in_dim(d_summary, first_block, blocks, 1)
        sides = grad_sort.astype(BF16).reshape(2, width // 2, width)
        sort_keep = lax.dynamic_index_in_dim(sides, split[0], 0, False)
        sort_give = lax.dynamic_index_in_dim(sides, 1 - split[0], 0, False)

    (sort_half,) = add_split([sort_keep, send(sort_give, CORE)], 1)
    late_more["second"] = dict(after=[sort_half])
    next(late_stages)
    (sort_half,) = add_split([sort_half, send(sort_half, X)], 1)
    late_more["line"] = dict(after=[sort_half])
    sort_other = send(sort_half, CORE)
    input_grad, gains = leave(
        inputs, gain_one, d_hidden, d_rows, d_summary, d_resid, ()
    )
    *_, last = late_stages
    grad_query, grad_key, grad_value, grad_output = late_end(split, last)
    (grad_sort,) = call(
        sort_end_kernel,
        [like((width, width), F32)],
        [split, sort_half, sort_other],
        [SCALAR, whole(sort_half), whole(sort_other)],
    )
    small = jnp.concatenate(
        [
            jnp.sum(gains[:, :1], axis=0),
            slope[:1],
            jnp.full((1, width), entropy / seq_size),
            jnp.zeros((5, width), F32),
        ]
    )
    small = lax.all_to_all(
        jnp.broadcast_to(small[None], (dp_size * seq_size,) + small.shape),
        ("dp", "seq"),
        0,
        0,
        tiled=True,
    )
    small = jnp.sum(small, axis=0)
    penalty = -small[2, 0] / total_blocks[0, 0]
    return (
        output.reshape(inputs.shape),
        input_grad,
        penalty,
        small[0],
        grad_query,
        grad_key,
        grad_value,
        grad_output,
        grad_sort,
        small[1],
        grad_in,
        grad_out,
    )


def solution(mesh):
    placed = (
        P("dp", "seq", None),
        P("dp", "seq"),
        P("dp", "seq"),
        P(),
        P(),
        P(),
        P(),
        P(),
        P(),
        P(),
        P(),
        P(),
        P("dp", "seq", None),
    )
    return jax.shard_map(
        body,
        mesh=mesh,
        in_specs=placed,
        out_specs=(
            P("dp", "seq", None),
            P("dp", "seq", None),
            P(),
            P(),
            P(),
            P(),
            P(),
            P(),
            P(),
            P(),
            P(),
            P(),
        ),
        check_vma=False,
    )
```

```python
import math

import jax
import jax.numpy as jnp
from jax import lax
from jax.experimental import pallas as pl
from jax.experimental.pallas import tpu as pltpu
from jax.sharding import PartitionSpec as P

HEADS = 8
BLOCK = 32
ITERS = 8
GROUP = 128

EPS = 1e-06
NEG = -1000000000.0
SORT_GAIN = 2.5
F32 = jnp.float32
BF16 = jnp.bfloat16
VMEM_BYTES = 56 * 2**20
COST = 3.0


def bits(size):
    return [1 << k for k in range(size.bit_length() - 1)]


def swap(array, axis, bit):
    return lax.ppermute(array, axis, [(i, i ^ bit) for i in range(lax.axis_size(axis))])


def send(array, *to):
    seq = lax.axis_size("seq")
    pairs = []
    for i in range(lax.axis_size("dp") * seq):
        dp_bits, seq_bits = to[-(i // seq % 2)]
        pairs.append((i, i ^ (dp_bits * seq + seq_bits)))
    return lax.ppermute(array, ("dp", "seq"), pairs)


CORE = (1, 0)
X, Y = (2, 0), (0, 1)
LINE = ((0, 4), (0, 2), (0, 6))


def spot(index, place, core):
    at = (index ^ place) % 16
    turned = at % 4 + at // 4 % 2 * 8 + at // 8 * 4
    return jnp.where(core == 0, at, turned)


def add_kernel(count, *refs):
    outs = refs[count:]
    each = outs[0].shape[0]
    for n, out_ref in enumerate(outs):
        part = pl.ds(n * each, each)
        total = refs[0][part].astype(F32)
        for ref in refs[1:count]:
            total = total + ref[part].astype(F32)
        out_ref[...] = total.astype(out_ref.dtype)


def add_split(arrays, pieces, dtype=BF16, **more):
    shape = arrays[0].shape
    out = like((shape[0] // pieces,) + shape[1:], dtype)
    kernel = lambda *refs: add_kernel(len(arrays), *refs)
    return list(call(kernel, [out] * pieces, arrays, **more))


def join_kernel(*refs):
    each = refs[0].shape[0]
    for n, ref in enumerate(refs[:-1]):
        refs[-1][n * each : (n + 1) * each] = ref[...]


def join(arrays, **more):
    shape = arrays[0].shape
    out = like((len(arrays) * shape[0],) + shape[1:], BF16)
    return list(call(join_kernel, [out], arrays, **more))


def sum_stages(keep, give, more):
    own = add_split([keep, send(give, CORE)], 2)
    yield own
    own = add_split([own[0], send(own[1], X, Y)], 2)
    yield own
    own = add_split([own[0], send(own[1], Y, X)], 4, **more.get("second", {}))
    yield own
    got = [send(g, to) for g, to in zip(own[1:], LINE)]
    own = add_split([own[0]] + got, 1, **more.get("line", {}))
    for bit in bits(lax.axis_size("seq"))[3:]:
        own = add_split([own[0], send(own[0], (0, bit))], 1) + own[1:]
    yield own
    got = [send(own[0], to) for to in LINE]
    quarter, *passed = join(own[:1] + got, **more.get("join", {}))
    yield [quarter, *passed]
    (half,) = join([quarter, send(quarter, Y, X)], **more.get("half", {}))
    yield [half]
    halves = [half, send(half, X, Y)]
    yield halves
    yield halves + [send(h, CORE) for h in halves]


def exchange(chunks):
    return lax.all_to_all(chunks, "seq", 0, 0, tiled=True)


def add(left, right):
    return (left.astype(F32) + right.astype(F32)).astype(BF16)


def sum_seq(part):
    for bit in bits(lax.axis_size("seq")):
        part = add(part, swap(part, "seq", bit))
    return part


def dot(left, right, left_dim=1, right_dim=0):
    return lax.dot_general(
        left, right, (((left_dim,), (right_dim,)), ((), ())), preferred_element_type=F32
    )


def whole(array):
    return pl.BlockSpec(array.shape, lambda *_: (0,) * array.ndim)


def nth(array, index):
    return pl.BlockSpec((1,) + array.shape[1:], lambda *_: (index,) + (0,) * (array.ndim - 1))


def call(
    kernel,
    outs,
    args,
    specs=None,
    scratch=(),
    flops=0,
    out_specs=None,
    grid=(1,),
    after=(),
    passing=(),
):
    specs = specs or [whole(a) for a in args]
    moved = sum(math.prod(o.shape) * o.dtype.itemsize for o in outs)
    moved += sum(math.prod(a.shape) * a.dtype.itemsize for a in args)
    count, made = len(args), len(outs)
    extra = [*passing, *after]
    skip, pas = len(extra), len(passing)
    anywhere = pl.BlockSpec(memory_space=pl.ANY)
    return pl.pallas_call(
        lambda *refs: kernel(
            *refs[:count],
            *refs[count + skip : count + skip + made],
            *refs[count + skip + made + pas :],
        ),
        out_shape=list(outs) + [like(p.shape, p.dtype) for p in passing],
        grid=grid,
        in_specs=list(specs) + [anywhere] * skip,
        out_specs=list(out_specs or [whole(o) for o in outs]) + [anywhere] * pas,
        scratch_shapes=list(scratch),
        input_output_aliases={count + k: made + k for k in range(pas)},
        compiler_params=pltpu.CompilerParams(vmem_limit_bytes=VMEM_BYTES),
        cost_estimate=pl.CostEstimate(
            flops=int(flops * COST), bytes_accessed=int(moved * COST), transcendentals=0
        ),
    )(*args, *extra)


SCALAR = pl.BlockSpec(memory_space=pltpu.SMEM)


def like(shape, dtype):
    return jax.ShapeDtypeStruct(shape, dtype)


def lay(buffer, value):
    for c in range(buffer.shape[0]):
        buffer[c] = value[:, c * 128 : (c + 1) * 128]


def lift(buffer):
    return jnp.concatenate([buffer[c] for c in range(buffer.shape[0])], axis=1)


def pick(buffer, t, count):
    return jnp.concatenate(
        [buffer[c, pl.ds(t, count, stride=BLOCK), :] for c in range(buffer.shape[0])], axis=1
    )


def strew(buffer, t, rows):
    for c in range(buffer.shape[0]):
        buffer[c, pl.ds(t, rows.shape[0], stride=BLOCK), :] = rows[:, c * 128 : (c + 1) * 128]


def chunk_shape(parts, blocks, width):
    row_parts = min(parts, BLOCK)
    return (parts, BLOCK // row_parts, blocks, width * row_parts // parts)


def chunk_places(shape, t):
    per = BLOCK // shape[1]
    cols = shape[0] // per
    return [(t // shape[1]) * cols + f for f in range(cols)], t % shape[1]


def store_row(ref, t, rows, shape=None):
    parts, place = chunk_places(shape or ref.shape, t)
    for f, part in enumerate(parts):
        ref[part, place] = rows[:, f * ref.shape[3] : (f + 1) * ref.shape[3]]


def load_row(ref, t):
    parts, place = chunk_places(ref.shape, t)
    return jnp.concatenate([ref[part, place] for part in parts], axis=1)


def row_buffer(span, width):
    return pltpu.VMEM((width // 128, span, 128), F32)


def enter_kernel(x_ref, gain_ref, flag_ref, hidden_ref, *refs):
    rows_refs, buffer = refs[:-1], refs[-1]
    seqs = len(rows_refs)
    parts, _, blocks, cols = rows_refs[0].shape
    width = hidden_ref.shape[2]
    each = width // cols
    shape = chunk_shape(parts, blocks, width)
    for s in range(seqs):
        x = x_ref[s].astype(F32)
        scale = lax.rsqrt(jnp.mean(x * x, axis=-1, keepdims=True) + EPS)
        hidden = (x * scale * gain_ref[...]).astype(BF16)
        hidden_ref[s] = hidden
        lay(buffer, hidden.astype(F32))
        total = None
        for t in range(BLOCK):
            rows = pick(buffer, t, blocks)
            store_row(rows_refs[s], t, rows.astype(BF16), shape)
            total = rows if total is None else total + rows
        low = (total * (1.0 / BLOCK)).astype(BF16)
        for part in range(parts):
            for f in range(each):
                rows_refs[0][part, shape[1] + s * each + f] = low[:, f * cols : (f + 1) * cols]
    for part in range(parts):
        rows_refs[0][part, shape[1] + seqs * each] = flag_ref[...]


def enter(inputs, gain, real, parts):
    seqs, span, width = inputs.shape
    blocks = span // BLOCK
    p, r, n, w = chunk_shape(parts, blocks, width)
    lane = jnp.arange(w)[None] * seqs // w
    flags = jnp.zeros((blocks, w), BF16)
    for s in range(seqs):
        flags = jnp.where(lane == s, real[s].astype(BF16)[:, None], flags)
    more = seqs * (width // w) + 1
    return call(
        enter_kernel,
        [like(inputs.shape, BF16)]
        + [like((p, r + (more if s == 0 else 0), n, w), BF16) for s in range(seqs)],
        [inputs, gain, flags],
        scratch=[row_buffer(span, width)],
    )


def told_of(first, seqs, width):
    parts, _, blocks, cols = first.shape
    shape = chunk_shape(parts, blocks, width)
    each = width // cols
    told = first[:, shape[1] :]
    told = told.transpose(1, 0, 2, 3).reshape(told.shape[1], parts * blocks, cols)
    flags = told[-1][:, :: cols // seqs].T
    told = told[:-1].reshape(seqs, each, parts * blocks, cols).transpose(0, 2, 1, 3)
    return told.reshape(seqs, parts * blocks, width), flags


def told_summary(first_ref, s):
    parts, rows, blocks, width = first_ref.shape
    row = chunk_shape(parts, blocks, width)[1] + s
    return first_ref[:, row].reshape(parts * blocks, width)


def told_flags(first_ref, seqs, s):
    parts, rows, blocks, width = first_ref.shape
    flags = first_ref[:, rows - 1, :, s * (width // seqs) : s * (width // seqs) + 128]
    return flags.reshape(parts * blocks, 128).astype(F32)


def plan_kernel(sort_scale, told_ref, w_ref, proj_ref, steps_ref, plan_ref, low_ref, entropy_ref, count_ref):
    seqs = plan_ref.shape[0]
    plans, reals = [], []
    entropy = jnp.zeros((), F32)
    for s in range(seqs):
        summary = told_summary(told_ref, s)
        flags = told_flags(told_ref, seqs, s)
        real = flags.T > 0.5
        proj = dot(summary, w_ref[...]).astype(BF16)
        proj_ref[s] = proj
        plans.append(jnp.where(real, sort_scale * dot(proj, summary, 1, 1), NEG))
        reals.append(real)
    for step in range(2 * ITERS):
        axis = 1 - step % 2
        for s in range(seqs):
            peak = jnp.max(plans[s], axis=axis, keepdims=True)
            share = jnp.exp(plans[s] - peak)
            total = jnp.sum(share, axis=axis, keepdims=True)
            fall = peak + jnp.log(total)
            share = share * (1.0 / total)
            if axis == 0:
                fall = jnp.where(reals[s][:1], fall, 0.0)
                share = jnp.where(reals[s], share, 0.0)
            plans[s] = plans[s] - fall
            steps_ref[step, s] = share
    for s in range(seqs):
        flags = told_flags(told_ref, seqs, s)[:, :1]
        prob = jnp.exp(plans[s])
        plan_ref[s] = plans[s]
        low_ref[s] = prob.astype(BF16)
        entropy = entropy + jnp.sum(jnp.where(flags > 0.5, prob * plans[s], 0.0))
    entropy_ref[...] = jnp.full(entropy_ref.shape, entropy, F32)
    blocks = [jnp.sum(told_flags(told_ref, seqs, s), axis=0, keepdims=True) for s in range(seqs)]
    count_ref[...] = jnp.broadcast_to(sum(blocks), count_ref.shape)


def plan_back_kernel(
    sort_scale,
    count_ref,
    place_ref,
    heard_ref,
    told_ref,
    w_ref,
    proj_ref,
    steps_ref,
    plan_ref,
    split_ref,
    d_summary_ref,
    keep_ref,
    give_ref,
    buffer,
    whole_grad,
):
    place = place_ref[0, 0]
    seqs = plan_ref.shape[0]
    blocks = told_ref.shape[2]
    part = 1.0 / count_ref[:1]
    grads = []
    for s in range(seqs):
        flags = told_flags(told_ref, seqs, s)[:, :1]
        plan = plan_ref[s]
        prob = jnp.exp(plan)
        d_prob = heard_ref[s].astype(F32)
        grads.append(prob * d_prob - jnp.where(flags > 0.5, prob * plan + prob, 0.0) * part)
    for step in reversed(range(2 * ITERS)):
        for s in range(seqs):
            total = jnp.sum(grads[s], axis=1 - step % 2, keepdims=True)
            grads[s] = grads[s] - steps_ref[step, s] * total
    grad_sort = None
    for s in range(seqs):
        summary = told_summary(told_ref, s)
        flags = told_flags(told_ref, seqs, s)
        real = flags.T > 0.5
        d_logits = jnp.where(real, grads[s], 0.0)
        low = d_logits.astype(BF16)
        d_proj = (sort_scale * dot(low, summary)).astype(BF16)
        turned = low.astype(F32).T.astype(BF16)
        buffer[...] = sort_scale * dot(turned, proj_ref[s]) + dot(d_proj, w_ref[...], 1, 1)
        first = pl.multiple_of(place * blocks, blocks)
        d_summary_ref[s] = buffer[pl.ds(first, blocks), :]
        here = dot(summary, d_proj, 0, 0)
        grad_sort = here if grad_sort is None else grad_sort + here
    half = keep_ref.shape[0]
    whole_grad[...] = grad_sort
    keep_ref[...] = whole_grad[pl.ds(pl.multiple_of(split_ref[0] * half, half), half)].astype(BF16)
    give_ref[...] = whole_grad[
        pl.ds(pl.multiple_of((1 - split_ref[0]) * half, half), half)
    ].astype(BF16)


def spread_row(ref, t):
    parts, rows, blocks, width = ref.shape
    return ref[:, t].reshape(parts * blocks, width)


def mix_kernel(low_ref, spread_ref, mixed_ref):
    parts, rows, blocks, width = mixed_ref.shape
    for t in range(rows):
        mixed = dot(low_ref[0], spread_row(spread_ref, t)).astype(BF16)
        mixed_ref[:, t] = mixed.reshape(parts, blocks, width)


def mix(low, spread, index, width, after=()):
    shape = chunk_shape(spread.shape[0], spread.shape[2], width)
    specs = [nth(low, index), whole(spread)]
    return call(mix_kernel, [like(shape, BF16)], [low, spread], specs, after=after)[0]


def unmix_kernel(low_ref, *refs):
    seqs = low_ref.shape[0]
    spread_refs, d_mixed_refs = refs[:seqs], refs[seqs : 2 * seqs]
    d_spread_ref, d_prob_ref = refs[2 * seqs :]
    parts, rows, blocks, width = d_mixed_refs[0].shape
    for s in range(seqs):
        turned = low_ref[s].astype(F32).T.astype(BF16)
        d_prob = None
        for t in range(rows):
            grad = spread_row(d_mixed_refs[s], t)
            here = dot(grad, spread_row(spread_refs[s], t), 1, 1)
            d_prob = here if d_prob is None else d_prob + here
            back = dot(turned, grad).astype(BF16)
            d_spread_ref[:, s * rows + t] = back.reshape(parts, blocks, width)
        d_prob_ref[s] = d_prob.astype(BF16)


def unmix(low, spread, d_mixed, after=()):
    p, r, n, w = d_mixed[0].shape
    seqs = low.shape[0]
    return call(
        unmix_kernel,
        [like((p, seqs * r, n, w), BF16), like(low.shape, BF16)],
        [low, *spread, *d_mixed],
        after=after,
    )


def block_masks():
    lane = lax.broadcasted_iota(jnp.int32, (BLOCK, 2 * GROUP), 1)
    owner = (lane % GROUP) // BLOCK
    return [owner == b for b in range(GROUP // BLOCK)]


def narrow(full, masks, start):
    out = full[start : start + BLOCK]
    for b in range(1, len(masks)):
        out = jnp.where(masks[b], full[start + b * BLOCK : start + (b + 1) * BLOCK], out)
    return out


def widen(first, second, masks):
    zero = jnp.zeros_like(first)
    return jnp.concatenate(
        [jnp.where(m, first, zero) for m in masks] + [jnp.where(m, second, zero) for m in masks],
        axis=0,
    ).astype(BF16)


def two_heads_lanes(rows):
    lane = lax.broadcasted_iota(jnp.int32, rows.shape, 1)
    low = lane < rows.shape[1] // 2
    zero = jnp.zeros_like(rows)
    return jnp.concatenate([jnp.where(low, rows, zero), jnp.where(low, zero, rows)], axis=0)


def two_heads_rows(columns):
    row = lax.broadcasted_iota(jnp.int32, columns.shape, 0)
    low = row < columns.shape[0] // 2
    zero = jnp.zeros_like(columns)
    return jnp.concatenate([jnp.where(low, columns, zero), jnp.where(low, zero, columns)], axis=1)


def own_heads(full):
    half = full.shape[1] // 2
    row = lax.broadcasted_iota(jnp.int32, (full.shape[0], half), 0)
    return jnp.where(row < full.shape[0] // 2, full[:, :half], full[:, half:])


def turn(array):
    return array.astype(F32).T.astype(BF16)


def project_kernel(hidden_ref, wq_ref, wk_ref, wv_ref, q_ref, k_ref, v_ref, qt_ref, kt_ref, vt_ref):
    hidden = hidden_ref[0]
    for w_ref, flat_ref, turned_ref in (
        (wq_ref, q_ref, qt_ref),
        (wk_ref, k_ref, kt_ref),
        (wv_ref, v_ref, vt_ref),
    ):
        full = dot(hidden, w_ref[...])
        flat_ref[0] = full.astype(BF16)
        turned_ref[0] = full.T.astype(BF16)


def project(hidden, wq, wk, wv):
    seqs, span, width = hidden.shape
    flat = pl.BlockSpec((1, span, width), lambda s: (s, 0, 0))
    turned = pl.BlockSpec((1, width, span), lambda s: (s, 0, 0))
    return call(
        project_kernel,
        [like((seqs, span, width), BF16)] * 3 + [like((seqs, width, span), BF16)] * 3,
        [hidden, wq, wk, wv],
        [flat] + [whole(wq)] * 3,
        flops=6 * seqs * span * width * width,
        grid=(seqs,),
        out_specs=[flat] * 3 + [turned] * 3,
    )


def attend_kernel(
    att_scale,
    rows_ref,
    allowed_ref,
    wk_ref,
    wv_ref,
    k_ref,
    qt_ref,
    vt_ref,
    att_ref,
    mixed_ref,
    vs_ref,
    kst_ref,
    weights_ref,
    buffer,
    ks,
    vst,
):
    span, width = mixed_ref.shape
    for t in range(BLOCK):
        strew(buffer, t, load_row(rows_ref, t).astype(F32))
    mixed_ref[...] = lift(buffer).astype(BF16)
    mixed = mixed_ref[...]
    full = dot(mixed, wk_ref[...])
    ks[...] = full.astype(BF16)
    kst_ref[...] = full.T.astype(BF16)
    full = dot(mixed, wv_ref[...])
    vs_ref[...] = full.astype(BF16)
    vst[...] = full.T.astype(BF16)
    masks = block_masks()
    pairs = HEADS // 2

    def group(g, carry):
        rows = pl.ds(pl.multiple_of(g * GROUP, GROUP), GROUP)
        allowed = allowed_ref[0, :, rows]
        allowed = jnp.concatenate([allowed, allowed], axis=1) > 0.5
        for p in range(pairs):
            lanes = pl.ds(p * GROUP, GROUP)
            keys = jnp.concatenate([k_ref[0, rows, lanes], ks[rows, lanes]], axis=0)
            scores = dot(keys, two_heads_rows(qt_ref[0, lanes, rows]))
            near = jnp.where(allowed, narrow(scores, masks, 0) * att_scale, NEG)
            far = narrow(scores, masks, GROUP) * att_scale
            peak = jnp.maximum(
                jnp.max(near, axis=0, keepdims=True), jnp.max(far, axis=0, keepdims=True)
            )
            near = jnp.exp(near - peak)
            far = jnp.exp(far - peak)
            total = jnp.sum(near, axis=0, keepdims=True) + jnp.sum(far, axis=0, keepdims=True)
            part = 1.0 / total
            near = near * part
            far = far * part
            weights_ref[g * pairs + p, :BLOCK] = near
            weights_ref[g * pairs + p, BLOCK:] = far
            values = jnp.concatenate([vt_ref[0, lanes, rows], vst[lanes, rows]], axis=1)
            out = own_heads(dot(values, widen(near, far, masks)))
            att_ref[rows, lanes] = out.T.astype(BF16)
        return carry

    lax.fori_loop(0, span // GROUP, group, 0)


def attend(rows, allowed, wk, wv, k, qt, vt, index):
    seqs, span, width = k.shape
    units = span // GROUP * (HEADS // 2)
    flat = like((span, width), BF16)
    args = [rows, allowed, wk, wv, k, qt, vt]
    return call(
        lambda *refs: attend_kernel(1.0 / math.sqrt(width // HEADS), *refs),
        [flat] * 3 + [like((width, span), BF16), like((units, 2 * BLOCK, 2 * GROUP), F32)],
        args,
        [whole(rows), nth(allowed, index), whole(wk), whole(wv)]
        + [nth(a, index) for a in (k, qt, vt)],
        [row_buffer(span, width), pltpu.VMEM((span, width), BF16), pltpu.VMEM((width, span), BF16)],
        flops=8 * span * width * width,
    )


def attend_back_kernel(
    att_scale,
    d_att_ref,
    q_ref,
    v_ref,
    kt_ref,
    vs_ref,
    kst_ref,
    weights_ref,
    wk_ref,
    wv_ref,
    d_rows_ref,
    dq,
    dk,
    dv,
    dks,
    dvs,
    buffer,
    datt_t,
):
    span, width = vs_ref.shape
    datt_t[...] = turn(d_att_ref[0])
    masks = block_masks()
    pairs = HEADS // 2

    def group(g, carry):
        rows = pl.ds(pl.multiple_of(g * GROUP, GROUP), GROUP)
        for p in range(pairs):
            lanes = pl.ds(p * GROUP, GROUP)
            values = jnp.concatenate([v_ref[0, rows, lanes], vs_ref[rows, lanes]], axis=0)
            d_weights = dot(values, two_heads_rows(datt_t[lanes, rows]))
            near = weights_ref[g * pairs + p, :BLOCK]
            far = weights_ref[g * pairs + p, BLOCK:]
            d_near = near * narrow(d_weights, masks, 0)
            d_far = far * narrow(d_weights, masks, GROUP)
            total = jnp.sum(d_near, axis=0, keepdims=True) + jnp.sum(d_far, axis=0, keepdims=True)
            d_near = d_near - near * total
            d_far = d_far - far * total
            d_scores = widen(d_near, d_far, masks)
            keys = jnp.concatenate([kt_ref[0, lanes, rows], kst_ref[lanes, rows]], axis=1)
            dq[rows, lanes] = (own_heads(dot(keys, d_scores)).T * att_scale).astype(BF16)
            d_keys = (dot(d_scores, two_heads_lanes(q_ref[0, rows, lanes])) * att_scale).astype(BF16)
            dk[rows, lanes] = d_keys[:GROUP]
            dks[rows, lanes] = d_keys[GROUP:]
            d_values = dot(
                widen(near, far, masks), two_heads_lanes(d_att_ref[0, rows, lanes])
            ).astype(BF16)
            dv[rows, lanes] = d_values[:GROUP]
            dvs[rows, lanes] = d_values[GROUP:]
        return carry

    lax.fori_loop(0, span // GROUP, group, 0)
    lay(buffer, dot(dks[...], wk_ref[...], 1, 1) + dot(dvs[...], wv_ref[...], 1, 1))
    for t in range(BLOCK):
        store_row(d_rows_ref, t, pick(buffer, t, d_rows_ref.shape[2]).astype(BF16))


def attend_back(d_att, q, v, kt, kept, wk, wv, shape, index, after=()):
    seqs, span, width = q.shape
    args = [d_att, q, v, kt, *kept, wk, wv]
    flat = like((span, width), BF16)
    return call(
        lambda *refs: attend_back_kernel(1.0 / math.sqrt(width // HEADS), *refs),
        [like(shape, BF16)] + [flat] * 5,
        args,
        [nth(a, index) for a in args[:4]]
        + [whole(a) for a in args[4:]],
        [row_buffer(span, width), pltpu.VMEM((width, span), BF16)],
        flops=12 * span * width * width,
        after=after,
    )


def late_kernel(split_ref, hidden_ref, gwo_ref, *refs):
    keep_ref, give_ref, buffer = refs[-3:]
    seqs, span, width = hidden_ref.shape
    core, place = split_ref[0], split_ref[1]
    per = len(refs[:-3]) // seqs
    totals = [None, None, None]
    for s in range(seqs):
        mixed_ref, dq, dk, dv, dks, dvs = refs[s * per : (s + 1) * per]
        hidden_t = turn(hidden_ref[s])
        mixed_t = turn(mixed_ref[...])
        here = (
            dot(hidden_t, dq[...]),
            dot(hidden_t, dk[...]) + dot(mixed_t, dks[...]),
            dot(hidden_t, dv[...]) + dot(mixed_t, dvs[...]),
        )
        totals = [h if t is None else t + h for t, h in zip(totals, here)]
    for n in range(3):
        buffer[n] = totals[n]
    buffer[3] = gwo_ref[...].astype(F32)
    blocks, rows = keep_ref.shape[0], keep_ref.shape[1] // 4
    for side, ref in ((core, keep_ref), (1 - core, give_ref)):
        for j in range(blocks):
            part = pl.ds(pl.multiple_of((side * blocks + j) * rows, rows), rows)
            at = spot(j, place, side)
            for n in range(4):
                ref[at, n * rows : (n + 1) * rows] = buffer[n, part].astype(BF16)


def late(split, hidden, gwo, parts, after=()):
    seqs, span, width = hidden.shape
    args = [split, hidden, gwo, *[a for part in parts for a in part]]
    shape = like((16, 4 * width // 32, width), BF16)
    return call(
        late_kernel,
        [shape, shape],
        args,
        [SCALAR] + [whole(a) for a in args[1:]],
        [pltpu.VMEM((4, width, width), F32)],
        flops=10 * seqs * span * width * width,
        after=after,
    )


def end_blocks(split_ref, refs):
    each = refs[0].shape[0]
    for n, ref in enumerate(refs):
        core = split_ref[0] if n < 2 else 1 - split_ref[0]
        for r in range(each):
            index = core * 16 + spot(0, n % 2 * each + r, core)
            yield ref[r], index ^ (split_ref[1] % 16)


def late_end_kernel(split_ref, *refs):
    outs = refs[-4:]
    rows = refs[0].shape[1] // 4
    for block, index in end_blocks(split_ref, refs[:-4]):
        part = pl.ds(pl.multiple_of(index * rows, rows), rows)
        for n, out_ref in enumerate(outs):
            out_ref[part] = block[n * rows : (n + 1) * rows].astype(F32)


def late_end(split, parts, after=()):
    width = parts[0].shape[2]
    return call(
        late_end_kernel,
        [like((width, width), F32)] * 4,
        [split, *parts],
        [SCALAR] + [whole(p) for p in parts],
        after=after,
    )


def d_hidden_kernel(wq_ref, wk_ref, wv_ref, *refs):
    out_ref = refs[-1]
    for s in range(out_ref.shape[0]):
        dq, dk, dv = refs[3 * s : 3 * s + 3]
        out_ref[s] = (
            dot(dq[...], wq_ref[...], 1, 1)
            + dot(dk[...], wk_ref[...], 1, 1)
            + dot(dv[...], wv_ref[...], 1, 1)
        )


def d_hidden_of(wq, wk, wv, parts, after=()):
    args = [wq, wk, wv] + [a for part in parts for a in part]
    shape = (len(parts),) + parts[0][0].shape
    flops = 6 * shape[0] * shape[1] * shape[2] ** 2
    return call(d_hidden_kernel, [like(shape, F32)], args, flops=flops, after=after)[0]


def feed_kernel(
    seqs,
    split_ref,
    x_ref,
    cot_ref,
    gain_ref,
    wo_ref,
    win_ref,
    wout_ref,
    *refs,
):
    att_refs = refs[:seqs]
    (
        out_ref,
        keep_ref,
        give_ref,
        gwo_ref,
        d_resid_ref,
        d_att_ref,
        slope_ref,
        y1,
        unit,
        h2,
        h2t,
        d_h2,
        f_all,
        du_all,
        scales,
    ) = refs[seqs:]
    step = pl.program_id(0)
    span = x_ref.shape[0]
    tile = 512
    tiles = [pl.ds(r, tile) for r in range(0, span, tile)]

    def att_tile(rows):
        each = att_refs[0].shape[0]
        return att_refs[rows.start // each][pl.ds(rows.start % each, tile)]

    @pl.when(step == 0)
    def _():
        for rows in tiles:
            y = x_ref[rows].astype(F32) + dot(att_tile(rows), wo_ref[...])
            y1[rows] = y
            scale = lax.rsqrt(jnp.mean(y * y, axis=-1, keepdims=True) + EPS)
            n = y * scale
            unit[rows] = n
            scales[rows] = jnp.broadcast_to(scale, (tile, scales.shape[1]))
            low = (n * gain_ref[...]).astype(BF16)
            h2[rows] = low
            h2t[:, rows] = turn(low)
            d_h2[rows] = jnp.zeros((tile, d_h2.shape[1]), F32)

    root = math.sqrt(2.0 / math.pi)
    for rows in tiles:
        u = dot(h2[rows], win_ref[...])
        square = u * u
        bend = jnp.tanh(root * u * (1.0 + 0.044715 * square))
        half = 0.5 + 0.5 * bend
        f = (u * half).astype(BF16)
        slope = half + (0.5 * root) * u * (1.0 - bend * bend) * (1.0 + 0.134145 * square)
        du = (dot(cot_ref[rows], wout_ref[...], 1, 1) * slope).astype(BF16)
        y1[rows] = y1[rows] + dot(f, wout_ref[...])
        d_h2[rows] = d_h2[rows] + dot(du, win_ref[...], 1, 1)
        f_all[:, rows] = turn(f)
        du_all[rows] = du
    grads = (
        dot(f_all[...], cot_ref[...]).astype(BF16),
        dot(h2t[...], du_all[...]).astype(BF16),
    )
    blocks, block = keep_ref.shape[0], keep_ref.shape[1] // 2
    count = grads[0].shape[0] // block
    for first, ref in ((0, give_ref), (2, keep_ref)):

        @pl.when(step // 2 * 2 == first)
        def _():
            for j in range(count):
                core = split_ref[0] if first else 1 - split_ref[0]
                at = spot((step % 2) * count + j, split_ref[1], core)
                for n in range(2):
                    ref[at, n * block : (n + 1) * block] = grads[n][j * block : (j + 1) * block]


    @pl.when(step == pl.num_programs(0) - 1)
    def _():
        total = None
        grad = None
        for rows in tiles:
            out_ref[rows] = y1[rows].astype(BF16)
            up, n = d_h2[rows], unit[rows]
            here = jnp.sum(up * n, axis=0, keepdims=True)
            total = here if total is None else total + here
            d_n = up * gain_ref[...]
            d_y = scales[rows][:, :1] * (d_n - n * jnp.mean(d_n * n, axis=-1, keepdims=True))
            d_y = d_y + cot_ref[rows].astype(F32)
            low = d_y.astype(BF16)
            d_resid_ref[rows] = low
            d_att_ref[rows] = dot(low, wo_ref[...], 1, 1).astype(BF16)
            du_all[rows] = low
            f_all[:, rows] = turn(att_tile(rows))
        gwo_ref[...] = dot(f_all[...], du_all[...]).astype(BF16)
        slope_ref[...] = jnp.broadcast_to(total, slope_ref.shape)


def feed(split, x, att, cot, gain, wo, win, wout):
    span, width = x.shape
    hidden = win.shape[1]
    steps = hidden // width
    flat = lambda dtype: like((span, width), dtype)
    parts = like((16, 2 * hidden // 32, width), BF16)
    outs = [
        flat(BF16),
        parts,
        parts,
        like((width, width), BF16),
        flat(BF16),
        flat(BF16),
        like((8, width), F32),
    ]

    def chunk(c, split_ref):
        return ((1 - c // 2) ^ split_ref[0]) * 2 + c % 2

    return pl.pallas_call(
        lambda *refs: feed_kernel(len(att), *refs),
        grid_spec=pltpu.PrefetchScalarGridSpec(
            num_scalar_prefetch=1,
            grid=(steps,),
            in_specs=[whole(a) for a in (x, cot, gain, wo)]
            + [
                pl.BlockSpec((width, width), lambda c, r: (0, chunk(c, r))),
                pl.BlockSpec((width, width), lambda c, r: (chunk(c, r), 0)),
            ]
            + [whole(a) for a in att],
            out_specs=[whole(o) for o in outs],
            scratch_shapes=[
                pltpu.VMEM((span, width), F32),
                pltpu.VMEM((span, width), F32),
                pltpu.VMEM((span, width), BF16),
                pltpu.VMEM((width, span), BF16),
                pltpu.VMEM((span, width), F32),
                pltpu.VMEM((width, span), BF16),
                pltpu.VMEM((span, width), BF16),
                pltpu.VMEM((span, 128), F32),
            ],
        ),
        out_shape=outs,
        compiler_params=pltpu.CompilerParams(vmem_limit_bytes=VMEM_BYTES),
        cost_estimate=pl.CostEstimate(
            flops=int(COST * 12 * span * width * hidden),
            bytes_accessed=int(COST * (24 << 20)),
            transcendentals=0,
        ),
    )(split, x, cot, gain, wo, win, wout, *att)


def feed_end_kernel(split_ref, *refs):
    gout_ref, gin_ref = refs[-2:]
    width = gout_ref.shape[1]
    rows = refs[0].shape[1] // 2
    per = width // rows
    for block, index in end_blocks(split_ref, refs[:-2]):
        gout_ref[pl.ds(pl.multiple_of(index * rows, rows), rows)] = block[:rows].astype(F32)
        part = pl.ds(pl.multiple_of(index % per * rows, rows), rows)
        lanes = pl.ds(pl.multiple_of(index // per * width, width), width)
        gin_ref[part, lanes] = block[rows:].astype(F32)


def feed_end(split, parts):
    width = parts[0].shape[2]
    hidden = 16 * parts[0].shape[1]
    return call(
        feed_end_kernel,
        [like((hidden, width), F32), like((width, hidden), F32)],
        [split, *parts],
        [SCALAR] + [whole(p) for p in parts],
    )


def leave_kernel(
    x_ref,
    gain_ref,
    d_hidden_ref,
    rows_ref,
    d_summary_ref,
    d_resid_ref,
    slope_ref,
    entropy_ref,
    out_ref,
    small_ref,
    buffer,
    total,
):
    step = pl.program_id(0)
    d_summary = d_summary_ref[0] * (1.0 / BLOCK)
    for t in range(BLOCK):
        strew(buffer, t, load_row(rows_ref, t).astype(F32) + d_summary)
    x = x_ref[0].astype(F32)
    scale = lax.rsqrt(jnp.mean(x * x, axis=-1, keepdims=True) + EPS)
    n = x * scale
    up = d_hidden_ref[0] + lift(buffer)
    here = jnp.sum(up * n, axis=0, keepdims=True)

    @pl.when(step == 0)
    def _():
        total[...] = jnp.broadcast_to(here, total.shape)

    @pl.when(step > 0)
    def _():
        total[...] = total[...] + here

    d_n = up * gain_ref[...]
    d_x = scale * (d_n - n * jnp.mean(d_n * n, axis=-1, keepdims=True))
    out_ref[0] = (d_x + d_resid_ref[0].astype(F32)).astype(BF16)

    @pl.when(step == pl.num_programs(0) - 1)
    def _():
        row = lax.broadcasted_iota(jnp.int32, total.shape, 0)
        entropy = entropy_ref[...]
        entropy = jnp.concatenate([entropy] * (total.shape[1] // entropy.shape[1]), axis=1)
        rest = jnp.where(row == 1, slope_ref[...], entropy)
        all_rows = jnp.where(row == 0, total[...], rest)
        for part in range(small_ref.shape[0]):
            small_ref[part] = all_rows


def leave(inputs, gain, d_hidden, rows, d_summary, d_resid, slope, entropy, parts):
    seqs, span, width = inputs.shape
    p, r, n, w = rows.shape
    args = [inputs, gain, d_hidden, rows, d_summary, d_resid, slope, entropy]
    each = lambda a: pl.BlockSpec((1,) + a.shape[1:], lambda s: (s, 0, 0))
    outs = [like(inputs.shape, BF16), like((parts, 8, width), F32)]
    return call(
        leave_kernel,
        outs,
        args,
        [
            each(inputs),
            whole(gain),
            each(d_hidden),
            pl.BlockSpec((p, r // seqs, n, w), lambda s: (0, s, 0, 0)),
            each(d_summary),
            each(d_resid),
            whole(slope),
            whole(entropy),
        ],
        [row_buffer(span, width), pltpu.VMEM((8, width), F32)],
        grid=(seqs,),
        out_specs=[each(outs[0]), whole(outs[1])],
    )


def small_kernel(part, small_ref, count_ref, out_ref):
    total = small_ref[0]
    for k in range(1, small_ref.shape[0]):
        total = total + small_ref[k]
    row = lax.broadcasted_iota(jnp.int32, total.shape, 0)
    out_ref[...] = jnp.where(row == 2, total * (-part / count_ref[:1, :1]), total)


def sort_end_kernel(split_ref, half_ref, other_ref, out_ref):
    half = half_ref.shape[0]
    for core, ref in ((split_ref[0], half_ref), (1 - split_ref[0], other_ref)):
        out_ref[pl.ds(pl.multiple_of(core * half, half), half)] = ref[...].astype(F32)


def plan_plain(sort_scale, summary_all, real, w_sort):
    def plan_of(logits):
        plan = jnp.where(real, logits, NEG)
        for _ in range(ITERS):
            plan = plan - jax.nn.logsumexp(plan, axis=2, keepdims=True)
            fall = jax.nn.logsumexp(plan, axis=1, keepdims=True)
            plan = plan - jnp.where(real, fall, 0.0)
        return plan

    proj = lax.dot_general(
        summary_all, w_sort, (((2,), (0,)), ((), ())), preferred_element_type=F32
    ).astype(BF16)
    logits = sort_scale * jnp.einsum("sid,sjd->sij", proj, summary_all, preferred_element_type=F32)
    plan, back = jax.vjp(plan_of, logits)
    return proj, plan, back


def places():
    dp, seq = lax.axis_index("dp"), lax.axis_index("seq")
    core, x, y = dp % 2, (dp // 2) % 2, seq % 2
    line = (seq // 2) % 2 * 2 + (seq // 4) % 2
    return jnp.stack([core, core * 16 + x * 8 + y * 4 + line]).astype(jnp.int32)


def body(
    inputs,
    segment_ids,
    real_block,
    gain_attn,
    w_query,
    w_key,
    w_value,
    w_output,
    w_sort,
    gain_ffn,
    w_in,
    w_out,
    cotangent,
):
    seqs, span, width = inputs.shape
    blocks = span // BLOCK
    seq_size, dp_size = lax.axis_size("seq"), lax.axis_size("dp")
    count = blocks * seq_size
    small_plan = count == 128
    sort_scale = SORT_GAIN * BLOCK / math.sqrt(width)
    gain_one = gain_attn.astype(F32).reshape(1, width)
    gain_two = gain_ffn.astype(F32).reshape(1, width)
    place = lax.axis_index("seq")
    first_block = place * blocks
    place = place.astype(jnp.int32).reshape(1, 1)
    split = places()

    segments = segment_ids.reshape(seqs, blocks, BLOCK)
    allowed = (segments.transpose(0, 2, 1)[:, :, :, None] == segments[:, None]).astype(F32)
    allowed = allowed.reshape(seqs, BLOCK, span)


    hidden, *rows = enter(inputs, gain_one, real_block, seq_size)
    spread = [exchange(r) for r in rows]
    q, k, v, qt, kt, vt = project(hidden, w_query, w_key, w_value)

    if small_plan:
        proj, steps, plan, low, entropy, total_blocks = call(
            lambda *refs: plan_kernel(sort_scale, *refs),
            [
                like((seqs, count, width), BF16),
                like((2 * ITERS, seqs, count, count), F32),
                like((seqs, count, count), F32),
                like((seqs, count, count), BF16),
                like((8, 128), F32),
                like((8, 128), F32),
            ],
            [spread[0], w_sort],
            after=(q,),
        )
    else:
        summary_all, reals = told_of(spread[0], seqs, width)
        real = reals[:, None, :] == 1
        proj, plan, plan_back = plan_plain(sort_scale, summary_all, real, w_sort)
        prob = jnp.exp(plan)
        low = prob.astype(BF16)
        entropy = jnp.sum(jnp.where(reals[:, :, None] == 1, prob * plan, 0.0))
        total_blocks = jnp.full((8, 128), jnp.sum(reals.astype(F32)))
        entropy = jnp.full((8, 128), entropy)
    for bit in bits(dp_size):
        total_blocks = total_blocks + swap(total_blocks, "dp", bit)

    att, kept = [], []
    for s in range(seqs):
        part = mix(low, spread[s], s, width, [allowed, split, gain_two, total_blocks] if s else ())
        here, *rest = attend(exchange(part), allowed, w_key, w_value, k, qt, vt, s)
        att.append(here)
        kept.append(rest)

    flat = (seqs * span, width)
    output, keep, give, grad_output, d_resid, d_att, slope = feed(
        split,
        inputs.reshape(flat),
        att,
        cotangent.reshape(flat),
        gain_two,
        w_output,
        w_in,
        w_out,
    )
    d_resid = d_resid.reshape(inputs.shape)
    d_att = d_att.reshape(inputs.shape)
    more = {}
    stages = sum_stages(keep, give, more)
    summed = next(stages)
    grads, d_mixed = [], []
    chunks = chunk_shape(seq_size, blocks, width)
    for s in range(seqs):
        after = summed[:1] if s else ()
        sent, *here = attend_back(d_att, q, v, kt, kept[s][1:], w_key, w_value, chunks, s, after)
        grads.append(here)
        d_mixed.append(exchange(sent))
    parts = late(
        split, hidden, grad_output, [[kept[s][0], *grads[s]] for s in range(seqs)]
    )
    plane = next(stages)
    d_hidden = d_hidden_of(w_query, w_key, w_value, [g[:3] for g in grads])
    late_more = {}
    late_stages = sum_stages(*parts, late_more)
    d_rows, d_prob = unmix(low, spread, d_mixed, plane[:1])
    heard = sum_seq(d_prob)
    more["line"] = dict(passing=[d_rows])
    next(stages)
    _, d_rows = next(stages)
    d_rows = exchange(d_rows)
    next(late_stages)
    late2 = next(late_stages)
    more["half"] = dict(after=[late2[0]])
    *_, last = stages
    grad_out, grad_in = feed_end(split, last)

    if small_plan:
        args = [
            total_blocks,
            place,
            heard,
            spread[0],
            w_sort,
            proj,
            steps,
            plan,
        ]
        half = like((width // 2, width), BF16)
        outs = [like((seqs, blocks, width), F32), half, half]
        d_summary, sort_keep, sort_give = call(
            lambda *refs: plan_back_kernel(sort_scale, *refs),
            outs,
            args + [split],
            [whole(total_blocks), SCALAR] + [whole(a) for a in args[2:]] + [SCALAR],
            [pltpu.VMEM((count, width), F32), pltpu.VMEM((width, width), F32)],
            after=[late2[0], d_hidden],
        )
    else:
        d_prob = heard.astype(F32)
        d_plan = prob * d_prob - (
            jnp.where(reals[:, :, None] == 1, prob * plan + prob, 0.0) / total_blocks[0, 0]
        )
        (d_logits,) = plan_back(d_plan)
        d_logits = d_logits.astype(BF16)
        d_proj = sort_scale * jnp.einsum(
            "sij,sjd->sid", d_logits, summary_all, preferred_element_type=F32
        )
        d_proj = d_proj.astype(BF16)
        grad_sort = jnp.einsum("sid,sie->de", summary_all, d_proj, preferred_element_type=F32)
        d_summary = sort_scale * jnp.einsum(
            "sij,sid->sjd", d_logits, proj, preferred_element_type=F32
        ) + jnp.einsum("sie,de->sid", d_proj, w_sort, preferred_element_type=F32)
        d_summary = lax.dynamic_slice_in_dim(d_summary, first_block, blocks, 1)
        sides = grad_sort.astype(BF16).reshape(2, width // 2, width)
        sort_keep = lax.dynamic_index_in_dim(sides, split[0], 0, False)
        sort_give = lax.dynamic_index_in_dim(sides, 1 - split[0], 0, False)

    (sort_half,) = add_split([sort_keep, send(sort_give, CORE)], 1)
    late_more["second"] = dict(after=[sort_half])
    next(late_stages)
    (sort_half,) = add_split([sort_half, send(sort_half, X)], 1)
    late_more["line"] = dict(after=[sort_half])
    sort_other = send(sort_half, CORE)
    input_grad, small = leave(
        inputs,
        gain_one,
        d_hidden,
        d_rows,
        d_summary,
        d_resid,
        slope,
        entropy,
        dp_size * seq_size,
    )
    small = lax.all_to_all(small, ("dp", "seq"), 0, 0, tiled=True)
    *_, last = late_stages
    grad_query, grad_key, grad_value, grad_output = late_end(split, last)
    (grad_sort,) = call(
        sort_end_kernel,
        [like((width, width), F32)],
        [split, sort_half, sort_other],
        [SCALAR, whole(sort_half), whole(sort_other)],
    )
    (small,) = call(
        lambda *refs: small_kernel(1.0 / seq_size, *refs),
        [like((8, width), F32)],
        [small, total_blocks],
    )
    penalty = small[2, 0]
    return (
        output.reshape(inputs.shape),
        input_grad,
        penalty,
        small[0],
        grad_query,
        grad_key,
        grad_value,
        grad_output,
        grad_sort,
        small[1],
        grad_in,
        grad_out,
    )


def solution(mesh):
    placed = (
        P("dp", "seq", None),
        P("dp", "seq"),
        P("dp", "seq"),
        P(),
        P(),
        P(),
        P(),
        P(),
        P(),
        P(),
        P(),
        P(),
        P("dp", "seq", None),
    )
    return jax.shard_map(
        body,
        mesh=mesh,
        in_specs=placed,
        out_specs=(
            P("dp", "seq", None),
            P("dp", "seq", None),
            P(),
            P(),
            P(),
            P(),
            P(),
            P(),
            P(),
            P(),
            P(),
            P(),
        ),
        check_vma=False,
    )
```

```python
import math

import jax
import jax.numpy as jnp
from jax import lax
from jax.experimental import pallas as pl
from jax.experimental.pallas import tpu as pltpu
from jax.sharding import PartitionSpec as P

HEADS = 8
BLOCK = 32
ITERS = 8
GROUP = 128

EPS = 1e-06
NEG = -1000000000.0
SORT_GAIN = 2.5
F32 = jnp.float32
BF16 = jnp.bfloat16
VMEM_BYTES = 56 * 2**20
COST = 3.0


def bits(size):
    return [1 << k for k in range(size.bit_length() - 1)]


def swap(array, axis, bit):
    return lax.ppermute(array, axis, [(i, i ^ bit) for i in range(lax.axis_size(axis))])


def send(array, *to):
    seq = lax.axis_size("seq")
    pairs = []
    for i in range(lax.axis_size("dp") * seq):
        dp_bits, seq_bits = to[-(i // seq % 2)]
        pairs.append((i, i ^ (dp_bits * seq + seq_bits)))
    return lax.ppermute(array, ("dp", "seq"), pairs)


CORE = (1, 0)
X, Y = (2, 0), (0, 1)
LINE = ((0, 4), (0, 2), (0, 6))


def spot(index, place, core):
    at = (index ^ place) % 16
    turned = at % 4 + at // 4 % 2 * 8 + at // 8 * 4
    return jnp.where(core == 0, at, turned)


def add_kernel(count, *refs):
    outs = refs[count:]
    each = outs[0].shape[0]
    for n, out_ref in enumerate(outs):
        part = pl.ds(n * each, each)
        total = refs[0][part].astype(F32)
        for ref in refs[1:count]:
            total = total + ref[part].astype(F32)
        out_ref[...] = total.astype(out_ref.dtype)


def add_split(arrays, pieces, dtype=BF16, **more):
    shape = arrays[0].shape
    out = like((shape[0] // pieces,) + shape[1:], dtype)
    kernel = lambda *refs: add_kernel(len(arrays), *refs)
    return list(call(kernel, [out] * pieces, arrays, HELD, out_specs=HELD, **more))


def join_kernel(*refs):
    each = refs[0].shape[0]
    for n, ref in enumerate(refs[:-1]):
        refs[-1][n * each : (n + 1) * each] = ref[...]


def join(arrays, **more):
    shape = arrays[0].shape
    out = like((len(arrays) * shape[0],) + shape[1:], BF16)
    return list(call(join_kernel, [out], arrays, HELD, out_specs=HELD, **more))


def sum_stages(keep, give, more):
    own = add_split([keep, send(give, CORE)], 2)
    yield own
    own = add_split([own[0], send(own[1], X, Y)], 2)
    yield own
    own = add_split([own[0], send(own[1], Y, X)], 4, **more.get("second", {}))
    yield own
    got = [send(g, to) for g, to in zip(own[1:], LINE)]
    own = add_split([own[0]] + got, 1, **more.get("line", {}))
    for bit in bits(lax.axis_size("seq"))[3:]:
        own = add_split([own[0], send(own[0], (0, bit))], 1) + own[1:]
    yield own
    got = [send(own[0], to) for to in LINE]
    quarter, *passed = join(own[:1] + got, **more.get("join", {}))
    yield [quarter, *passed]
    (half,) = join([quarter, send(quarter, Y, X)], **more.get("half", {}))
    yield [half]
    halves = [half, send(half, X, Y)]
    yield halves
    yield halves + [send(h, CORE) for h in halves]


def exchange(chunks):
    return lax.all_to_all(chunks, "seq", 0, 0, tiled=True)


def add(left, right):
    return (left.astype(F32) + right.astype(F32)).astype(BF16)


def sum_seq(part):
    for bit in bits(lax.axis_size("seq")):
        part = add(part, swap(part, "seq", bit))
    return part


def dot(left, right, left_dim=1, right_dim=0):
    return lax.dot_general(
        left, right, (((left_dim,), (right_dim,)), ((), ())), preferred_element_type=F32
    )


def whole(array):
    return pl.BlockSpec(array.shape, lambda *_: (0,) * array.ndim)


def nth(array, index):
    return pl.BlockSpec((1,) + array.shape[1:], lambda *_: (index,) + (0,) * (array.ndim - 1))


def call(
    kernel,
    outs,
    args,
    specs=None,
    scratch=(),
    flops=0,
    out_specs=None,
    grid=(1,),
    after=(),
    passing=(),
):
    vmem = VMEM_BYTES
    if specs is HELD:
        specs, out_specs = [IN_VMEM] * len(args), [IN_VMEM] * len(outs)
        vmem = 16 * 2**20
    specs = specs or [whole(a) for a in args]
    moved = sum(math.prod(o.shape) * o.dtype.itemsize for o in outs)
    moved += sum(math.prod(a.shape) * a.dtype.itemsize for a in args)
    count, made = len(args), len(outs)
    extra = [*passing, *after]
    skip, pas = len(extra), len(passing)
    anywhere = pl.BlockSpec(memory_space=pl.ANY)
    return pl.pallas_call(
        lambda *refs: kernel(
            *refs[:count],
            *refs[count + skip : count + skip + made],
            *refs[count + skip + made + pas :],
        ),
        out_shape=list(outs) + [like(p.shape, p.dtype) for p in passing],
        grid=grid,
        in_specs=list(specs) + [anywhere] * skip,
        out_specs=list(out_specs or [whole(o) for o in outs]) + [anywhere] * pas,
        scratch_shapes=list(scratch),
        input_output_aliases={count + k: made + k for k in range(pas)},
        compiler_params=pltpu.CompilerParams(vmem_limit_bytes=vmem),
        cost_estimate=pl.CostEstimate(
            flops=int(flops * COST), bytes_accessed=int(moved * COST), transcendentals=0
        ),
    )(*args, *extra)


HELD = object()
IN_VMEM = pl.BlockSpec(memory_space=pltpu.VMEM)
SCALAR = pl.BlockSpec(memory_space=pltpu.SMEM)


def like(shape, dtype):
    return jax.ShapeDtypeStruct(shape, dtype)


def lay(buffer, value):
    for c in range(buffer.shape[0]):
        buffer[c] = value[:, c * 128 : (c + 1) * 128]


def lift(buffer):
    return jnp.concatenate([buffer[c] for c in range(buffer.shape[0])], axis=1)


def pick(buffer, t, count):
    return jnp.concatenate(
        [buffer[c, pl.ds(t, count, stride=BLOCK), :] for c in range(buffer.shape[0])], axis=1
    )


def strew(buffer, t, rows):
    for c in range(buffer.shape[0]):
        buffer[c, pl.ds(t, rows.shape[0], stride=BLOCK), :] = rows[:, c * 128 : (c + 1) * 128]


def chunk_shape(parts, blocks, width):
    row_parts = min(parts, BLOCK)
    return (parts, BLOCK // row_parts, blocks, width * row_parts // parts)


def chunk_places(shape, t):
    per = BLOCK // shape[1]
    cols = shape[0] // per
    return [(t // shape[1]) * cols + f for f in range(cols)], t % shape[1]


def store_row(ref, t, rows, shape=None):
    parts, place = chunk_places(shape or ref.shape, t)
    for f, part in enumerate(parts):
        ref[part, place] = rows[:, f * ref.shape[3] : (f + 1) * ref.shape[3]]


def load_row(ref, t):
    parts, place = chunk_places(ref.shape, t)
    return jnp.concatenate([ref[part, place] for part in parts], axis=1)


def row_buffer(span, width):
    return pltpu.VMEM((width // 128, span, 128), F32)


def enter_kernel(x_ref, gain_ref, flag_ref, hidden_ref, *refs):
    rows_refs, buffer = refs[:-1], refs[-1]
    seqs = len(rows_refs)
    parts, _, blocks, cols = rows_refs[0].shape
    width = hidden_ref.shape[2]
    each = width // cols
    shape = chunk_shape(parts, blocks, width)
    for s in range(seqs):
        x = x_ref[s].astype(F32)
        scale = lax.rsqrt(jnp.mean(x * x, axis=-1, keepdims=True) + EPS)
        hidden = (x * scale * gain_ref[...]).astype(BF16)
        hidden_ref[s] = hidden
        lay(buffer, hidden.astype(F32))
        total = None
        for t in range(BLOCK):
            rows = pick(buffer, t, blocks)
            store_row(rows_refs[s], t, rows.astype(BF16), shape)
            total = rows if total is None else total + rows
        low = (total * (1.0 / BLOCK)).astype(BF16)
        for part in range(parts):
            for f in range(each):
                rows_refs[0][part, shape[1] + s * each + f] = low[:, f * cols : (f + 1) * cols]
    for part in range(parts):
        rows_refs[0][part, shape[1] + seqs * each] = flag_ref[...]


def enter(inputs, gain, real, parts):
    seqs, span, width = inputs.shape
    blocks = span // BLOCK
    p, r, n, w = chunk_shape(parts, blocks, width)
    lane = jnp.arange(w)[None] * seqs // w
    flags = jnp.zeros((blocks, w), BF16)
    for s in range(seqs):
        flags = jnp.where(lane == s, real[s].astype(BF16)[:, None], flags)
    more = seqs * (width // w) + 1
    return call(
        enter_kernel,
        [like(inputs.shape, BF16)]
        + [like((p, r + (more if s == 0 else 0), n, w), BF16) for s in range(seqs)],
        [inputs, gain, flags],
        scratch=[row_buffer(span, width)],
    )


def told_of(first, seqs, width):
    parts, _, blocks, cols = first.shape
    shape = chunk_shape(parts, blocks, width)
    each = width // cols
    told = first[:, shape[1] :]
    told = told.transpose(1, 0, 2, 3).reshape(told.shape[1], parts * blocks, cols)
    flags = told[-1][:, :: cols // seqs].T
    told = told[:-1].reshape(seqs, each, parts * blocks, cols).transpose(0, 2, 1, 3)
    return told.reshape(seqs, parts * blocks, width), flags


def told_summary(first_ref, s):
    parts, rows, blocks, width = first_ref.shape
    row = chunk_shape(parts, blocks, width)[1] + s
    return first_ref[:, row].reshape(parts * blocks, width)


def told_flags(first_ref, seqs, s):
    parts, rows, blocks, width = first_ref.shape
    flags = first_ref[:, rows - 1, :, s * (width // seqs) : s * (width // seqs) + 128]
    return flags.reshape(parts * blocks, 128).astype(F32)


def plan_kernel(sort_scale, told_ref, w_ref, proj_ref, steps_ref, plan_ref, low_ref, entropy_ref, count_ref):
    seqs = plan_ref.shape[0]
    plans, reals = [], []
    entropy = jnp.zeros((), F32)
    for s in range(seqs):
        summary = told_summary(told_ref, s)
        flags = told_flags(told_ref, seqs, s)
        real = flags.T > 0.5
        proj = dot(summary, w_ref[...]).astype(BF16)
        proj_ref[s] = proj
        plans.append(jnp.where(real, sort_scale * dot(proj, summary, 1, 1), NEG))
        reals.append(real)
    for step in range(2 * ITERS):
        axis = 1 - step % 2
        for s in range(seqs):
            peak = jnp.max(plans[s], axis=axis, keepdims=True)
            share = jnp.exp(plans[s] - peak)
            total = jnp.sum(share, axis=axis, keepdims=True)
            fall = peak + jnp.log(total)
            share = share * (1.0 / total)
            if axis == 0:
                fall = jnp.where(reals[s][:1], fall, 0.0)
                share = jnp.where(reals[s], share, 0.0)
            plans[s] = plans[s] - fall
            steps_ref[step, s] = share
    for s in range(seqs):
        flags = told_flags(told_ref, seqs, s)[:, :1]
        prob = jnp.exp(plans[s])
        plan_ref[s] = plans[s]
        low_ref[s] = prob.astype(BF16)
        entropy = entropy + jnp.sum(jnp.where(flags > 0.5, prob * plans[s], 0.0))
    entropy_ref[...] = jnp.full(entropy_ref.shape, entropy, F32)
    blocks = [jnp.sum(told_flags(told_ref, seqs, s), axis=0, keepdims=True) for s in range(seqs)]
    count_ref[...] = jnp.broadcast_to(sum(blocks), count_ref.shape)


def plan_back_kernel(
    sort_scale,
    count_ref,
    place_ref,
    heard_ref,
    told_ref,
    w_ref,
    proj_ref,
    steps_ref,
    plan_ref,
    split_ref,
    d_summary_ref,
    keep_ref,
    give_ref,
    buffer,
    whole_grad,
):
    place = place_ref[0, 0]
    seqs = plan_ref.shape[0]
    blocks = told_ref.shape[2]
    part = 1.0 / count_ref[:1]
    grads = []
    for s in range(seqs):
        flags = told_flags(told_ref, seqs, s)[:, :1]
        plan = plan_ref[s]
        prob = jnp.exp(plan)
        d_prob = heard_ref[s].astype(F32)
        grads.append(prob * d_prob - jnp.where(flags > 0.5, prob * plan + prob, 0.0) * part)
    for step in reversed(range(2 * ITERS)):
        for s in range(seqs):
            total = jnp.sum(grads[s], axis=1 - step % 2, keepdims=True)
            grads[s] = grads[s] - steps_ref[step, s] * total
    grad_sort = None
    for s in range(seqs):
        summary = told_summary(told_ref, s)
        flags = told_flags(told_ref, seqs, s)
        real = flags.T > 0.5
        d_logits = jnp.where(real, grads[s], 0.0)
        low = d_logits.astype(BF16)
        d_proj = (sort_scale * dot(low, summary)).astype(BF16)
        turned = low.astype(F32).T.astype(BF16)
        buffer[...] = sort_scale * dot(turned, proj_ref[s]) + dot(d_proj, w_ref[...], 1, 1)
        first = pl.multiple_of(place * blocks, blocks)
        d_summary_ref[s] = buffer[pl.ds(first, blocks), :]
        here = dot(summary, d_proj, 0, 0)
        grad_sort = here if grad_sort is None else grad_sort + here
    half = keep_ref.shape[0]
    whole_grad[...] = grad_sort
    keep_ref[...] = whole_grad[pl.ds(pl.multiple_of(split_ref[0] * half, half), half)].astype(BF16)
    give_ref[...] = whole_grad[
        pl.ds(pl.multiple_of((1 - split_ref[0]) * half, half), half)
    ].astype(BF16)


def spread_row(ref, t):
    parts, rows, blocks, width = ref.shape
    return ref[:, t].reshape(parts * blocks, width)


def mix_kernel(low_ref, spread_ref, mixed_ref):
    parts, rows, blocks, width = mixed_ref.shape
    for t in range(rows):
        mixed = dot(low_ref[0], spread_row(spread_ref, t)).astype(BF16)
        mixed_ref[:, t] = mixed.reshape(parts, blocks, width)


def mix(low, spread, index, width, after=()):
    shape = chunk_shape(spread.shape[0], spread.shape[2], width)
    specs = [nth(low, index), whole(spread)]
    return call(mix_kernel, [like(shape, BF16)], [low, spread], specs, after=after)[0]


def unmix_kernel(low_ref, *refs):
    seqs = low_ref.shape[0]
    spread_refs, d_mixed_refs = refs[:seqs], refs[seqs : 2 * seqs]
    d_spread_ref, d_prob_ref = refs[2 * seqs :]
    parts, rows, blocks, width = d_mixed_refs[0].shape
    for s in range(seqs):
        turned = low_ref[s].astype(F32).T.astype(BF16)
        d_prob = None
        for t in range(rows):
            grad = spread_row(d_mixed_refs[s], t)
            here = dot(grad, spread_row(spread_refs[s], t), 1, 1)
            d_prob = here if d_prob is None else d_prob + here
            back = dot(turned, grad).astype(BF16)
            d_spread_ref[:, s * rows + t] = back.reshape(parts, blocks, width)
        d_prob_ref[s] = d_prob.astype(BF16)


def unmix(low, spread, d_mixed, after=()):
    p, r, n, w = d_mixed[0].shape
    seqs = low.shape[0]
    return call(
        unmix_kernel,
        [like((p, seqs * r, n, w), BF16), like(low.shape, BF16)],
        [low, *spread, *d_mixed],
        after=after,
    )


def block_masks():
    lane = lax.broadcasted_iota(jnp.int32, (BLOCK, 2 * GROUP), 1)
    owner = (lane % GROUP) // BLOCK
    return [owner == b for b in range(GROUP // BLOCK)]


def narrow(full, masks, start):
    out = full[start : start + BLOCK]
    for b in range(1, len(masks)):
        out = jnp.where(masks[b], full[start + b * BLOCK : start + (b + 1) * BLOCK], out)
    return out


def widen(first, second, masks):
    zero = jnp.zeros_like(first)
    return jnp.concatenate(
        [jnp.where(m, first, zero) for m in masks] + [jnp.where(m, second, zero) for m in masks],
        axis=0,
    ).astype(BF16)


def two_heads_lanes(rows):
    lane = lax.broadcasted_iota(jnp.int32, rows.shape, 1)
    low = lane < rows.shape[1] // 2
    zero = jnp.zeros_like(rows)
    return jnp.concatenate([jnp.where(low, rows, zero), jnp.where(low, zero, rows)], axis=0)


def two_heads_rows(columns):
    row = lax.broadcasted_iota(jnp.int32, columns.shape, 0)
    low = row < columns.shape[0] // 2
    zero = jnp.zeros_like(columns)
    return jnp.concatenate([jnp.where(low, columns, zero), jnp.where(low, zero, columns)], axis=1)


def own_heads(full):
    half = full.shape[1] // 2
    row = lax.broadcasted_iota(jnp.int32, (full.shape[0], half), 0)
    return jnp.where(row < full.shape[0] // 2, full[:, :half], full[:, half:])


def turn(array):
    return array.astype(F32).T.astype(BF16)


def project_kernel(hidden_ref, wq_ref, wk_ref, wv_ref, q_ref, k_ref, v_ref, qt_ref, kt_ref, vt_ref):
    hidden = hidden_ref[0]
    for w_ref, flat_ref, turned_ref in (
        (wq_ref, q_ref, qt_ref),
        (wk_ref, k_ref, kt_ref),
        (wv_ref, v_ref, vt_ref),
    ):
        full = dot(hidden, w_ref[...])
        flat_ref[0] = full.astype(BF16)
        turned_ref[0] = full.T.astype(BF16)


def project(hidden, wq, wk, wv):
    seqs, span, width = hidden.shape
    flat = pl.BlockSpec((1, span, width), lambda s: (s, 0, 0))
    turned = pl.BlockSpec((1, width, span), lambda s: (s, 0, 0))
    return call(
        project_kernel,
        [like((seqs, span, width), BF16)] * 3 + [like((seqs, width, span), BF16)] * 3,
        [hidden, wq, wk, wv],
        [flat] + [whole(wq)] * 3,
        flops=6 * seqs * span * width * width,
        grid=(seqs,),
        out_specs=[flat] * 3 + [turned] * 3,
    )


def attend_kernel(
    att_scale,
    rows_ref,
    allowed_ref,
    wk_ref,
    wv_ref,
    k_ref,
    qt_ref,
    vt_ref,
    att_ref,
    mixed_ref,
    vs_ref,
    kst_ref,
    weights_ref,
    buffer,
    ks,
    vst,
):
    span, width = mixed_ref.shape
    for t in range(BLOCK):
        strew(buffer, t, load_row(rows_ref, t).astype(F32))
    mixed_ref[...] = lift(buffer).astype(BF16)
    mixed = mixed_ref[...]
    full = dot(mixed, wk_ref[...])
    ks[...] = full.astype(BF16)
    kst_ref[...] = full.T.astype(BF16)
    full = dot(mixed, wv_ref[...])
    vs_ref[...] = full.astype(BF16)
    vst[...] = full.T.astype(BF16)
    masks = block_masks()
    pairs = HEADS // 2

    def group(g, carry):
        rows = pl.ds(pl.multiple_of(g * GROUP, GROUP), GROUP)
        allowed = allowed_ref[0, :, rows]
        allowed = jnp.concatenate([allowed, allowed], axis=1) > 0.5
        for p in range(pairs):
            lanes = pl.ds(p * GROUP, GROUP)
            keys = jnp.concatenate([k_ref[0, rows, lanes], ks[rows, lanes]], axis=0)
            scores = dot(keys, two_heads_rows(qt_ref[0, lanes, rows]))
            near = jnp.where(allowed, narrow(scores, masks, 0) * att_scale, NEG)
            far = narrow(scores, masks, GROUP) * att_scale
            peak = jnp.maximum(
                jnp.max(near, axis=0, keepdims=True), jnp.max(far, axis=0, keepdims=True)
            )
            near = jnp.exp(near - peak)
            far = jnp.exp(far - peak)
            total = jnp.sum(near, axis=0, keepdims=True) + jnp.sum(far, axis=0, keepdims=True)
            part = 1.0 / total
            near = near * part
            far = far * part
            weights_ref[g * pairs + p, :BLOCK] = near
            weights_ref[g * pairs + p, BLOCK:] = far
            values = jnp.concatenate([vt_ref[0, lanes, rows], vst[lanes, rows]], axis=1)
            out = own_heads(dot(values, widen(near, far, masks)))
            att_ref[rows, lanes] = out.T.astype(BF16)
        return carry

    lax.fori_loop(0, span // GROUP, group, 0)


def attend(rows, allowed, wk, wv, k, qt, vt, index):
    seqs, span, width = k.shape
    units = span // GROUP * (HEADS // 2)
    flat = like((span, width), BF16)
    args = [rows, allowed, wk, wv, k, qt, vt]
    return call(
        lambda *refs: attend_kernel(1.0 / math.sqrt(width // HEADS), *refs),
        [flat] * 3 + [like((width, span), BF16), like((units, 2 * BLOCK, 2 * GROUP), F32)],
        args,
        [whole(rows), nth(allowed, index), whole(wk), whole(wv)]
        + [nth(a, index) for a in (k, qt, vt)],
        [row_buffer(span, width), pltpu.VMEM((span, width), BF16), pltpu.VMEM((width, span), BF16)],
        flops=8 * span * width * width,
    )


def attend_back_kernel(
    att_scale,
    d_att_ref,
    q_ref,
    v_ref,
    kt_ref,
    vs_ref,
    kst_ref,
    weights_ref,
    wk_ref,
    wv_ref,
    d_rows_ref,
    dq,
    dk,
    dv,
    dks,
    dvs,
    buffer,
    datt_t,
):
    span, width = vs_ref.shape
    datt_t[...] = turn(d_att_ref[0])
    masks = block_masks()
    pairs = HEADS // 2

    def group(g, carry):
        rows = pl.ds(pl.multiple_of(g * GROUP, GROUP), GROUP)
        for p in range(pairs):
            lanes = pl.ds(p * GROUP, GROUP)
            values = jnp.concatenate([v_ref[0, rows, lanes], vs_ref[rows, lanes]], axis=0)
            d_weights = dot(values, two_heads_rows(datt_t[lanes, rows]))
            near = weights_ref[g * pairs + p, :BLOCK]
            far = weights_ref[g * pairs + p, BLOCK:]
            d_near = near * narrow(d_weights, masks, 0)
            d_far = far * narrow(d_weights, masks, GROUP)
            total = jnp.sum(d_near, axis=0, keepdims=True) + jnp.sum(d_far, axis=0, keepdims=True)
            d_near = d_near - near * total
            d_far = d_far - far * total
            d_scores = widen(d_near, d_far, masks)
            keys = jnp.concatenate([kt_ref[0, lanes, rows], kst_ref[lanes, rows]], axis=1)
            dq[rows, lanes] = (own_heads(dot(keys, d_scores)).T * att_scale).astype(BF16)
            d_keys = (dot(d_scores, two_heads_lanes(q_ref[0, rows, lanes])) * att_scale).astype(BF16)
            dk[rows, lanes] = d_keys[:GROUP]
            dks[rows, lanes] = d_keys[GROUP:]
            d_values = dot(
                widen(near, far, masks), two_heads_lanes(d_att_ref[0, rows, lanes])
            ).astype(BF16)
            dv[rows, lanes] = d_values[:GROUP]
            dvs[rows, lanes] = d_values[GROUP:]
        return carry

    lax.fori_loop(0, span // GROUP, group, 0)
    lay(buffer, dot(dks[...], wk_ref[...], 1, 1) + dot(dvs[...], wv_ref[...], 1, 1))
    for t in range(BLOCK):
        store_row(d_rows_ref, t, pick(buffer, t, d_rows_ref.shape[2]).astype(BF16))


def attend_back(d_att, q, v, kt, kept, wk, wv, shape, index, after=()):
    seqs, span, width = q.shape
    args = [d_att, q, v, kt, *kept, wk, wv]
    flat = like((span, width), BF16)
    return call(
        lambda *refs: attend_back_kernel(1.0 / math.sqrt(width // HEADS), *refs),
        [like(shape, BF16)] + [flat] * 5,
        args,
        [nth(a, index) for a in args[:4]]
        + [whole(a) for a in args[4:]],
        [row_buffer(span, width), pltpu.VMEM((width, span), BF16)],
        flops=12 * span * width * width,
        after=after,
    )


def late_kernel(split_ref, hidden_ref, gwo_ref, *refs):
    keep_ref, give_ref, buffer = refs[-3:]
    seqs, span, width = hidden_ref.shape
    core, place = split_ref[0], split_ref[1]
    per = len(refs[:-3]) // seqs
    totals = [None, None, None]
    for s in range(seqs):
        mixed_ref, dq, dk, dv, dks, dvs = refs[s * per : (s + 1) * per]
        hidden_t = turn(hidden_ref[s])
        mixed_t = turn(mixed_ref[...])
        here = (
            dot(hidden_t, dq[...]),
            dot(hidden_t, dk[...]) + dot(mixed_t, dks[...]),
            dot(hidden_t, dv[...]) + dot(mixed_t, dvs[...]),
        )
        totals = [h if t is None else t + h for t, h in zip(totals, here)]
    for n in range(3):
        buffer[n] = totals[n]
    buffer[3] = gwo_ref[...].astype(F32)
    blocks, rows = keep_ref.shape[0], keep_ref.shape[1] // 4
    for side, ref in ((core, keep_ref), (1 - core, give_ref)):
        for j in range(blocks):
            part = pl.ds(pl.multiple_of((side * blocks + j) * rows, rows), rows)
            at = spot(j, place, side)
            for n in range(4):
                ref[at, n * rows : (n + 1) * rows] = buffer[n, part].astype(BF16)


def late(split, hidden, gwo, parts, after=()):
    seqs, span, width = hidden.shape
    args = [split, hidden, gwo, *[a for part in parts for a in part]]
    shape = like((16, 4 * width // 32, width), BF16)
    return call(
        late_kernel,
        [shape, shape],
        args,
        [SCALAR] + [whole(a) for a in args[1:]],
        [pltpu.VMEM((4, width, width), F32)],
        flops=10 * seqs * span * width * width,
        after=after,
    )


def end_blocks(split_ref, refs):
    each = refs[0].shape[0]
    for n, ref in enumerate(refs):
        core = split_ref[0] if n < 2 else 1 - split_ref[0]
        for r in range(each):
            index = core * 16 + spot(0, n % 2 * each + r, core)
            yield ref[r], index ^ (split_ref[1] % 16)


def late_end_kernel(split_ref, *refs):
    outs = refs[-4:]
    rows = refs[0].shape[1] // 4
    for block, index in end_blocks(split_ref, refs[:-4]):
        part = pl.ds(pl.multiple_of(index * rows, rows), rows)
        for n, out_ref in enumerate(outs):
            out_ref[part] = block[n * rows : (n + 1) * rows].astype(F32)


def late_end(split, parts, after=()):
    width = parts[0].shape[2]
    return call(
        late_end_kernel,
        [like((width, width), F32)] * 4,
        [split, *parts],
        [SCALAR] + [whole(p) for p in parts],
        after=after,
    )


def d_hidden_kernel(wq_ref, wk_ref, wv_ref, *refs):
    out_ref = refs[-1]
    for s in range(out_ref.shape[0]):
        dq, dk, dv = refs[3 * s : 3 * s + 3]
        out_ref[s] = (
            dot(dq[...], wq_ref[...], 1, 1)
            + dot(dk[...], wk_ref[...], 1, 1)
            + dot(dv[...], wv_ref[...], 1, 1)
        )


def d_hidden_of(wq, wk, wv, parts, after=()):
    args = [wq, wk, wv] + [a for part in parts for a in part]
    shape = (len(parts),) + parts[0][0].shape
    flops = 6 * shape[0] * shape[1] * shape[2] ** 2
    return call(d_hidden_kernel, [like(shape, F32)], args, flops=flops, after=after)[0]


def feed_kernel(
    seqs,
    split_ref,
    x_ref,
    cot_ref,
    gain_ref,
    wo_ref,
    win_ref,
    wout_ref,
    *refs,
):
    att_refs = refs[:seqs]
    (
        out_ref,
        keep_ref,
        give_ref,
        gwo_ref,
        d_resid_ref,
        d_att_ref,
        slope_ref,
        y1,
        unit,
        h2,
        h2t,
        d_h2,
        f_all,
        du_all,
        scales,
    ) = refs[seqs:]
    step = pl.program_id(0)
    span = x_ref.shape[0]
    tile = 512
    tiles = [pl.ds(r, tile) for r in range(0, span, tile)]

    def att_tile(rows):
        each = att_refs[0].shape[0]
        return att_refs[rows.start // each][pl.ds(rows.start % each, tile)]

    @pl.when(step == 0)
    def _():
        for rows in tiles:
            y = x_ref[rows].astype(F32) + dot(att_tile(rows), wo_ref[...])
            y1[rows] = y
            scale = lax.rsqrt(jnp.mean(y * y, axis=-1, keepdims=True) + EPS)
            n = y * scale
            unit[rows] = n
            scales[rows] = jnp.broadcast_to(scale, (tile, scales.shape[1]))
            low = (n * gain_ref[...]).astype(BF16)
            h2[rows] = low
            h2t[:, rows] = turn(low)
            d_h2[rows] = jnp.zeros((tile, d_h2.shape[1]), F32)

    root = math.sqrt(2.0 / math.pi)
    for rows in tiles:
        u = dot(h2[rows], win_ref[...])
        square = u * u
        bend = jnp.tanh(root * u * (1.0 + 0.044715 * square))
        half = 0.5 + 0.5 * bend
        f = (u * half).astype(BF16)
        slope = half + (0.5 * root) * u * (1.0 - bend * bend) * (1.0 + 0.134145 * square)
        du = (dot(cot_ref[rows], wout_ref[...], 1, 1) * slope).astype(BF16)
        y1[rows] = y1[rows] + dot(f, wout_ref[...])
        d_h2[rows] = d_h2[rows] + dot(du, win_ref[...], 1, 1)
        f_all[:, rows] = turn(f)
        du_all[rows] = du
    grads = (
        dot(f_all[...], cot_ref[...]).astype(BF16),
        dot(h2t[...], du_all[...]).astype(BF16),
    )
    blocks, block = keep_ref.shape[0], keep_ref.shape[1] // 2
    count = grads[0].shape[0] // block
    for first, ref in ((0, give_ref), (2, keep_ref)):

        @pl.when(step // 2 * 2 == first)
        def _():
            for j in range(count):
                core = split_ref[0] if first else 1 - split_ref[0]
                at = spot((step % 2) * count + j, split_ref[1], core)
                for n in range(2):
                    ref[at, n * block : (n + 1) * block] = grads[n][j * block : (j + 1) * block]


    @pl.when(step == pl.num_programs(0) - 1)
    def _():
        total = None
        grad = None
        for rows in tiles:
            out_ref[rows] = y1[rows].astype(BF16)
            up, n = d_h2[rows], unit[rows]
            here = jnp.sum(up * n, axis=0, keepdims=True)
            total = here if total is None else total + here
            d_n = up * gain_ref[...]
            d_y = scales[rows][:, :1] * (d_n - n * jnp.mean(d_n * n, axis=-1, keepdims=True))
            d_y = d_y + cot_ref[rows].astype(F32)
            low = d_y.astype(BF16)
            d_resid_ref[rows] = low
            d_att_ref[rows] = dot(low, wo_ref[...], 1, 1).astype(BF16)
            du_all[rows] = low
            f_all[:, rows] = turn(att_tile(rows))
        gwo_ref[...] = dot(f_all[...], du_all[...]).astype(BF16)
        slope_ref[...] = jnp.broadcast_to(total, slope_ref.shape)


def feed(split, x, att, cot, gain, wo, win, wout):
    span, width = x.shape
    hidden = win.shape[1]
    steps = hidden // width
    flat = lambda dtype: like((span, width), dtype)
    parts = like((16, 2 * hidden // 32, width), BF16)
    outs = [
        flat(BF16),
        parts,
        parts,
        like((width, width), BF16),
        flat(BF16),
        flat(BF16),
        like((8, width), F32),
    ]

    def chunk(c, split_ref):
        return ((1 - c // 2) ^ split_ref[0]) * 2 + c % 2

    return pl.pallas_call(
        lambda *refs: feed_kernel(len(att), *refs),
        grid_spec=pltpu.PrefetchScalarGridSpec(
            num_scalar_prefetch=1,
            grid=(steps,),
            in_specs=[whole(a) for a in (x, cot, gain, wo)]
            + [
                pl.BlockSpec((width, width), lambda c, r: (0, chunk(c, r))),
                pl.BlockSpec((width, width), lambda c, r: (chunk(c, r), 0)),
            ]
            + [whole(a) for a in att],
            out_specs=[whole(o) for o in outs],
            scratch_shapes=[
                pltpu.VMEM((span, width), F32),
                pltpu.VMEM((span, width), F32),
                pltpu.VMEM((span, width), BF16),
                pltpu.VMEM((width, span), BF16),
                pltpu.VMEM((span, width), F32),
                pltpu.VMEM((width, span), BF16),
                pltpu.VMEM((span, width), BF16),
                pltpu.VMEM((span, 128), F32),
            ],
        ),
        out_shape=outs,
        compiler_params=pltpu.CompilerParams(vmem_limit_bytes=VMEM_BYTES),
        cost_estimate=pl.CostEstimate(
            flops=int(COST * 12 * span * width * hidden),
            bytes_accessed=int(COST * (24 << 20)),
            transcendentals=0,
        ),
    )(split, x, cot, gain, wo, win, wout, *att)


def feed_end_kernel(split_ref, *refs):
    gout_ref, gin_ref = refs[-2:]
    width = gout_ref.shape[1]
    rows = refs[0].shape[1] // 2
    per = width // rows
    for block, index in end_blocks(split_ref, refs[:-2]):
        gout_ref[pl.ds(pl.multiple_of(index * rows, rows), rows)] = block[:rows].astype(F32)
        part = pl.ds(pl.multiple_of(index % per * rows, rows), rows)
        lanes = pl.ds(pl.multiple_of(index // per * width, width), width)
        gin_ref[part, lanes] = block[rows:].astype(F32)


def feed_end(split, parts):
    width = parts[0].shape[2]
    hidden = 16 * parts[0].shape[1]
    return call(
        feed_end_kernel,
        [like((hidden, width), F32), like((width, hidden), F32)],
        [split, *parts],
        [SCALAR] + [whole(p) for p in parts],
    )


def leave_kernel(
    x_ref,
    gain_ref,
    d_hidden_ref,
    rows_ref,
    d_summary_ref,
    d_resid_ref,
    slope_ref,
    entropy_ref,
    out_ref,
    small_ref,
    buffer,
    total,
):
    step = pl.program_id(0)
    d_summary = d_summary_ref[0] * (1.0 / BLOCK)
    for t in range(BLOCK):
        strew(buffer, t, load_row(rows_ref, t).astype(F32) + d_summary)
    x = x_ref[0].astype(F32)
    scale = lax.rsqrt(jnp.mean(x * x, axis=-1, keepdims=True) + EPS)
    n = x * scale
    up = d_hidden_ref[0] + lift(buffer)
    here = jnp.sum(up * n, axis=0, keepdims=True)

    @pl.when(step == 0)
    def _():
        total[...] = jnp.broadcast_to(here, total.shape)

    @pl.when(step > 0)
    def _():
        total[...] = total[...] + here

    d_n = up * gain_ref[...]
    d_x = scale * (d_n - n * jnp.mean(d_n * n, axis=-1, keepdims=True))
    out_ref[0] = (d_x + d_resid_ref[0].astype(F32)).astype(BF16)

    @pl.when(step == pl.num_programs(0) - 1)
    def _():
        row = lax.broadcasted_iota(jnp.int32, total.shape, 0)
        entropy = entropy_ref[...]
        entropy = jnp.concatenate([entropy] * (total.shape[1] // entropy.shape[1]), axis=1)
        rest = jnp.where(row == 1, slope_ref[...], entropy)
        all_rows = jnp.where(row == 0, total[...], rest)
        for part in range(small_ref.shape[0]):
            small_ref[part] = all_rows


def leave(inputs, gain, d_hidden, rows, d_summary, d_resid, slope, entropy, parts):
    seqs, span, width = inputs.shape
    p, r, n, w = rows.shape
    args = [inputs, gain, d_hidden, rows, d_summary, d_resid, slope, entropy]
    each = lambda a: pl.BlockSpec((1,) + a.shape[1:], lambda s: (s, 0, 0))
    outs = [like(inputs.shape, BF16), like((parts, 8, width), F32)]
    return call(
        leave_kernel,
        outs,
        args,
        [
            each(inputs),
            whole(gain),
            each(d_hidden),
            pl.BlockSpec((p, r // seqs, n, w), lambda s: (0, s, 0, 0)),
            each(d_summary),
            each(d_resid),
            whole(slope),
            whole(entropy),
        ],
        [row_buffer(span, width), pltpu.VMEM((8, width), F32)],
        grid=(seqs,),
        out_specs=[each(outs[0]), whole(outs[1])],
    )


def small_kernel(part, small_ref, count_ref, out_ref):
    total = small_ref[0]
    for k in range(1, small_ref.shape[0]):
        total = total + small_ref[k]
    row = lax.broadcasted_iota(jnp.int32, total.shape, 0)
    out_ref[...] = jnp.where(row == 2, total * (-part / count_ref[:1, :1]), total)


def sort_end_kernel(split_ref, half_ref, other_ref, out_ref):
    half = half_ref.shape[0]
    for core, ref in ((split_ref[0], half_ref), (1 - split_ref[0], other_ref)):
        out_ref[pl.ds(pl.multiple_of(core * half, half), half)] = ref[...].astype(F32)


def plan_plain(sort_scale, summary_all, real, w_sort):
    def plan_of(logits):
        plan = jnp.where(real, logits, NEG)
        for _ in range(ITERS):
            plan = plan - jax.nn.logsumexp(plan, axis=2, keepdims=True)
            fall = jax.nn.logsumexp(plan, axis=1, keepdims=True)
            plan = plan - jnp.where(real, fall, 0.0)
        return plan

    proj = lax.dot_general(
        summary_all, w_sort, (((2,), (0,)), ((), ())), preferred_element_type=F32
    ).astype(BF16)
    logits = sort_scale * jnp.einsum("sid,sjd->sij", proj, summary_all, preferred_element_type=F32)
    plan, back = jax.vjp(plan_of, logits)
    return proj, plan, back


def places():
    dp, seq = lax.axis_index("dp"), lax.axis_index("seq")
    core, x, y = dp % 2, (dp // 2) % 2, seq % 2
    line = (seq // 2) % 2 * 2 + (seq // 4) % 2
    return jnp.stack([core, core * 16 + x * 8 + y * 4 + line]).astype(jnp.int32)


def body(
    inputs,
    segment_ids,
    real_block,
    gain_attn,
    w_query,
    w_key,
    w_value,
    w_output,
    w_sort,
    gain_ffn,
    w_in,
    w_out,
    cotangent,
):
    seqs, span, width = inputs.shape
    blocks = span // BLOCK
    seq_size, dp_size = lax.axis_size("seq"), lax.axis_size("dp")
    count = blocks * seq_size
    small_plan = count == 128
    sort_scale = SORT_GAIN * BLOCK / math.sqrt(width)
    gain_one = gain_attn.astype(F32).reshape(1, width)
    gain_two = gain_ffn.astype(F32).reshape(1, width)
    place = lax.axis_index("seq")
    first_block = place * blocks
    place = place.astype(jnp.int32).reshape(1, 1)
    split = places()

    segments = segment_ids.reshape(seqs, blocks, BLOCK)
    allowed = (segments.transpose(0, 2, 1)[:, :, :, None] == segments[:, None]).astype(F32)
    allowed = allowed.reshape(seqs, BLOCK, span)


    hidden, *rows = enter(inputs, gain_one, real_block, seq_size)
    spread = [exchange(r) for r in rows]
    q, k, v, qt, kt, vt = project(hidden, w_query, w_key, w_value)

    if small_plan:
        proj, steps, plan, low, entropy, total_blocks = call(
            lambda *refs: plan_kernel(sort_scale, *refs),
            [
                like((seqs, count, width), BF16),
                like((2 * ITERS, seqs, count, count), F32),
                like((seqs, count, count), F32),
                like((seqs, count, count), BF16),
                like((8, 128), F32),
                like((8, 128), F32),
            ],
            [spread[0], w_sort],
            after=(q,),
        )
    else:
        summary_all, reals = told_of(spread[0], seqs, width)
        real = reals[:, None, :] == 1
        proj, plan, plan_back = plan_plain(sort_scale, summary_all, real, w_sort)
        prob = jnp.exp(plan)
        low = prob.astype(BF16)
        entropy = jnp.sum(jnp.where(reals[:, :, None] == 1, prob * plan, 0.0))
        total_blocks = jnp.full((8, 128), jnp.sum(reals.astype(F32)))
        entropy = jnp.full((8, 128), entropy)
    for bit in bits(dp_size):
        total_blocks = total_blocks + swap(total_blocks, "dp", bit)

    att, kept = [], []
    for s in range(seqs):
        part = mix(low, spread[s], s, width, [allowed, split, gain_two, total_blocks] if s else ())
        here, *rest = attend(exchange(part), allowed, w_key, w_value, k, qt, vt, s)
        att.append(here)
        kept.append(rest)

    flat = (seqs * span, width)
    output, keep, give, grad_output, d_resid, d_att, slope = feed(
        split,
        inputs.reshape(flat),
        att,
        cotangent.reshape(flat),
        gain_two,
        w_output,
        w_in,
        w_out,
    )
    d_resid = d_resid.reshape(inputs.shape)
    d_att = d_att.reshape(inputs.shape)
    more = {}
    stages = sum_stages(keep, give, more)
    summed = next(stages)
    grads, d_mixed = [], []
    chunks = chunk_shape(seq_size, blocks, width)
    for s in range(seqs):
        after = summed[:1] if s else ()
        sent, *here = attend_back(d_att, q, v, kt, kept[s][1:], w_key, w_value, chunks, s, after)
        grads.append(here)
        d_mixed.append(exchange(sent))
    parts = late(
        split, hidden, grad_output, [[kept[s][0], *grads[s]] for s in range(seqs)]
    )
    plane = next(stages)
    d_hidden = d_hidden_of(w_query, w_key, w_value, [g[:3] for g in grads])
    late_more = {}
    late_stages = sum_stages(*parts, late_more)
    d_rows, d_prob = unmix(low, spread, d_mixed, plane[:1])
    heard = sum_seq(d_prob)
    more["line"] = dict(passing=[d_rows])
    next(stages)
    _, d_rows = next(stages)
    d_rows = exchange(d_rows)
    next(late_stages)
    late2 = next(late_stages)
    more["half"] = dict(after=[late2[0]])
    *_, last = stages
    grad_out, grad_in = feed_end(split, last)

    if small_plan:
        args = [
            total_blocks,
            place,
            heard,
            spread[0],
            w_sort,
            proj,
            steps,
            plan,
        ]
        half = like((width // 2, width), BF16)
        outs = [like((seqs, blocks, width), F32), half, half]
        d_summary, sort_keep, sort_give = call(
            lambda *refs: plan_back_kernel(sort_scale, *refs),
            outs,
            args + [split],
            [whole(total_blocks), SCALAR] + [whole(a) for a in args[2:]] + [SCALAR],
            [pltpu.VMEM((count, width), F32), pltpu.VMEM((width, width), F32)],
            after=[late2[0], d_hidden],
        )
    else:
        d_prob = heard.astype(F32)
        d_plan = prob * d_prob - (
            jnp.where(reals[:, :, None] == 1, prob * plan + prob, 0.0) / total_blocks[0, 0]
        )
        (d_logits,) = plan_back(d_plan)
        d_logits = d_logits.astype(BF16)
        d_proj = sort_scale * jnp.einsum(
            "sij,sjd->sid", d_logits, summary_all, preferred_element_type=F32
        )
        d_proj = d_proj.astype(BF16)
        grad_sort = jnp.einsum("sid,sie->de", summary_all, d_proj, preferred_element_type=F32)
        d_summary = sort_scale * jnp.einsum(
            "sij,sid->sjd", d_logits, proj, preferred_element_type=F32
        ) + jnp.einsum("sie,de->sid", d_proj, w_sort, preferred_element_type=F32)
        d_summary = lax.dynamic_slice_in_dim(d_summary, first_block, blocks, 1)
        sides = grad_sort.astype(BF16).reshape(2, width // 2, width)
        sort_keep = lax.dynamic_index_in_dim(sides, split[0], 0, False)
        sort_give = lax.dynamic_index_in_dim(sides, 1 - split[0], 0, False)

    (sort_half,) = add_split([sort_keep, send(sort_give, CORE)], 1)
    late_more["second"] = dict(after=[sort_half])
    next(late_stages)
    (sort_half,) = add_split([sort_half, send(sort_half, X)], 1)
    late_more["line"] = dict(after=[sort_half])
    sort_other = send(sort_half, CORE)
    input_grad, small = leave(
        inputs,
        gain_one,
        d_hidden,
        d_rows,
        d_summary,
        d_resid,
        slope,
        entropy,
        dp_size * seq_size,
    )
    small = lax.all_to_all(small, ("dp", "seq"), 0, 0, tiled=True)
    *_, last = late_stages
    grad_query, grad_key, grad_value, grad_output = late_end(split, last)
    (grad_sort,) = call(
        sort_end_kernel,
        [like((width, width), F32)],
        [split, sort_half, sort_other],
        [SCALAR, whole(sort_half), whole(sort_other)],
    )
    (small,) = call(
        lambda *refs: small_kernel(1.0 / seq_size, *refs),
        [like((8, width), F32)],
        [small, total_blocks],
    )
    penalty = small[2, 0]
    return (
        output.reshape(inputs.shape),
        input_grad,
        penalty,
        small[0],
        grad_query,
        grad_key,
        grad_value,
        grad_output,
        grad_sort,
        small[1],
        grad_in,
        grad_out,
    )


def solution(mesh):
    placed = (
        P("dp", "seq", None),
        P("dp", "seq"),
        P("dp", "seq"),
        P(),
        P(),
        P(),
        P(),
        P(),
        P(),
        P(),
        P(),
        P(),
        P("dp", "seq", None),
    )
    return jax.shard_map(
        body,
        mesh=mesh,
        in_specs=placed,
        out_specs=(
            P("dp", "seq", None),
            P("dp", "seq", None),
            P(),
            P(),
            P(),
            P(),
            P(),
            P(),
            P(),
            P(),
            P(),
            P(),
        ),
        check_vma=False,
    )
```
